32 devices in a mesh: wide: 8 (over z, x), narrow: 4 (over y, core).
Axes of the slice: x: 2, y: 2, z: 4, core: 2. Of those that a mesh axis runs over, the one named last changes fastest.
Arguments:
- word_states: bfloat16 [32, 64, 512], P(('wide', 'narrow')), may hold values from -6 to 6
- character_ids: int32 [32, 64, 16], P(('wide', 'narrow')), may hold values from 0 to 255
- word_lengths: int32 [32, 64], P(('wide', 'narrow')), may hold values from 1 to 16
- doc_lengths: int32 [32, 4], P(('wide', 'narrow')), may hold values from 1 to 32, 64 in all within a row
- embedding: bfloat16 [256, 256], P(('wide', 'narrow')), may hold values from -6 to 6
- char_qkv: bfloat16 [2, 256, 768], P(None, 'narrow', 'wide'), may hold values from -0.375 to 0.375
- char_out_w: bfloat16 [2, 256, 256], P(None, 'narrow', 'wide'), may hold values from -1 to 1
- char_up: bfloat16 [2, 256, 1024], P(None, 'narrow', 'wide'), may hold values from -0.375 to 0.375
- char_down: bfloat16 [2, 1024, 256], P(None, 'narrow', 'wide'), may hold values from -0.25 to 0.25
- char_proj: bfloat16 [2, 256, 512], P(None, 'narrow', 'wide'), may hold values from -1 to 1
- word_qkv: bfloat16 [2, 512, 1536], P(None, 'narrow', 'wide'), may hold values from -0.25 to 0.25
- word_out_w: bfloat16 [2, 512, 512], P(None, 'narrow', 'wide'), may hold values from -1 to 1
- word_up: bfloat16 [2, 512, 2048], P(None, 'narrow', 'wide'), may hold values from -0.25 to 0.25
- word_down: bfloat16 [2, 2048, 512], P(None, 'narrow', 'wide'), may hold values from -0.1875 to 0.1875
- char_gains: float32 [2, 2, 256], replicated, may hold values from 0.5 to 1.5
- char_shifts: float32 [2, 2, 256], replicated, may hold values from -1.5 to 1.5
- pool_query: float32 [2, 256], replicated, may hold values from -0.375 to 0.375
- word_gains: float32 [2, 2, 512], replicated, may hold values from 0.5 to 1.5
- word_shifts: float32 [2, 2, 512], replicated, may hold values from -1.5 to 1.5
- char_cot: bfloat16 [32, 64, 16, 256], P(('wide', 'narrow')), may hold values from -6 to 6
- word_cot: bfloat16 [32, 64, 512], P(('wide', 'narrow')), may hold values from -6 to 6
Outputs:
- char_out: bfloat16 [32, 64, 16, 256], P(('wide', 'narrow'))
- word_out: bfloat16 [32, 64, 512], P(('wide', 'narrow'))
- word_states_grad: float32 [32, 64, 512], P(('wide', 'narrow'))
- embedding_grad: float32 [256, 256], P(('wide', 'narrow'))
- char_qkv_grad: float32 [2, 256, 768], P(None, 'narrow', 'wide')
- char_out_w_grad: float32 [2, 256, 256], P(None, 'narrow', 'wide')
- char_up_grad: float32 [2, 256, 1024], P(None, 'narrow', 'wide')
- char_down_grad: float32 [2, 1024, 256], P(None, 'narrow', 'wide')
- char_proj_grad: float32 [2, 256, 512], P(None, 'narrow', 'wide')
- word_qkv_grad: float32 [2, 512, 1536], P(None, 'narrow', 'wide')
- word_out_w_grad: float32 [2, 512, 512], P(None, 'narrow', 'wide')
- word_up_grad: float32 [2, 512, 2048], P(None, 'narrow', 'wide')
- word_down_grad: float32 [2, 2048, 512], P(None, 'narrow', 'wide')
- char_gains_grad: float32 [2, 2, 256], replicated
- char_shifts_grad: float32 [2, 2, 256], replicated
- pool_query_grad: float32 [2, 256], replicated
- word_gains_grad: float32 [2, 2, 512], replicated
- word_shifts_grad: float32 [2, 2, 512], replicated
The draws below stay inside these ranges and needn't reach their ends.
Inputs may be any that keep to these rules, and one draw needn't show every extreme that they name: `doc_lengths`: each row's 4 document lengths sum to 64.
All inputs are finite; a program needn't handle non-finite values.
Results may differ from the reference program's by a relative error of at most 0.02.
The reference program's roundings to bfloat16 on the way count: a program that leaves them out, or rounds other values in their place, can miss the bound.
Values may be sent and summed in bfloat16 or wider, within the bound.
No kernel may reach another device: no remote copies, remote signals or barrier semaphores. Data moves between devices by JAX's collectives and lax.ppermute only.
A program may use at most 192 MiB of HBM per device.

```python
import math
import jax
import jax.numpy as jnp
import numpy as np
from jax import lax

CW = 256
CHARACTER_HEADS = 4
CF = 1024
WW = 512
WORD_HEADS = 8
WF = 2048
VOCAB = 256
SLOTS = 16
NDOC = 4
LAYERS = 2
WORDS = 64
ROWS = 32


def with_ends(entries, rng, smallest, high):
    extent = entries.shape
    index_at = [jax.random.randint(jax.random.fold_in(rng, axis), (), 0, extent[axis]) for axis in range(len(extent))]
    entries = entries.at[tuple(index_at)].set(smallest)
    longest = extent.index(max(extent))
    index_at[longest] = (index_at[longest] + 1) % extent[longest]
    return entries.at[tuple(index_at)].set(high)


def block_scale(key, extent, pieces, least, top_value):
    loudness, own = 1.0, jax.random.fold_in(key, 6)
    for dim, shards_of in pieces:
        draws = jnp.exp(jax.random.uniform(jax.random.fold_in(own, dim), (shards_of,), jnp.float32, least / len(pieces), top_value / len(pieces)))
        loudness = loudness * jnp.repeat(draws, extent[dim] // shards_of).reshape([-1 if axis == dim else 1 for axis in range(len(extent))])
    return loudness


def cumulative_ranks(number_of, slope):
    loads = [(1 << 20) // math.isqrt(grade ** slope) + 1 for grade in range(1, number_of + 1)]
    scale = 1 + sum(loads) // (1 << 30)
    return np.cumsum(np.array([max(1, weight // scale) for weight in loads]))


def skewed_ids(key, dims, amount, skew):
    table = cumulative_ranks(amount, skew)
    ticket = jax.random.randint(jax.random.fold_in(key, 1), dims, 0, int(table[amount - 1]))
    rank = jnp.searchsorted(jnp.asarray(table, jnp.int32), ticket, side="right")
    return jax.random.permutation(jax.random.fold_in(key, 2), amount)[rank].astype(jnp.int32)


def split_up(amount, total, most, skew):
    loads = [(1 << 20) // math.isqrt(rank ** skew) + 1 for rank in range(2, amount + 1)]
    spare, holding = total - most - (amount - 1), [1] * (amount - 1)
    while spare > 0:
        movable = [i for i in range(amount - 1) if holding[i] < most]
        whole, budget = sum([loads[i] for i in movable]), spare
        for i in movable:
            more = min(most - holding[i], max(1, budget * loads[i] // whole), spare)
            holding[i] = holding[i] + more
            spare = spare - more
    return np.array([most] + holding)


def ragged(key, count, total, limit, skew):
    if count == 2:
        one = jax.random.randint(key, (), max(1, total - limit), min(limit, total - 1) + 1)
        return jnp.stack([one, total - one])
    sizes = jnp.asarray(split_up(count, total, limit, skew), jnp.int32)
    couples = (count - 1) // 2
    giver, taker = sizes[1:1 + 2 * couples:2], sizes[2:2 + 2 * couples:2]
    slack = jnp.minimum(giver - 1, limit - taker)
    passed = jax.random.randint(jax.random.fold_in(key, 1), (couples,), 0, 1 << 20) % (slack + 1)
    sizes = sizes.at[1:1 + 2 * couples:2].set(giver - passed).at[2:2 + 2 * couples:2].set(taker + passed)
    return sizes[jax.random.permutation(jax.random.fold_in(key, 2), count)]


def bell_draw(stream_key, shape, width, most, pieces=(), held_as=jnp.bfloat16):
    values = jax.random.normal(stream_key, shape, jnp.float32) * width
    if len(pieces) > 0:
        values = block_scale(stream_key, shape, pieces, -0.22, 0.18) * values
    return jnp.clip(values, min=-most, max=most).astype(held_as)


def setup_inputs(seed: int = 0) -> dict:
    seeds = jax.random.split(jax.random.key(seed), 22)
    word_states = bell_draw(seeds[0], (ROWS, WORDS, WW), 1.0, 6.0, ((0, 32),))
    character_ids = with_ends(skewed_ids(seeds[1], (ROWS, WORDS, SLOTS), VOCAB, 2), jax.random.fold_in(seeds[1], 3), 0, VOCAB - 1).astype(jnp.int32)
    word_lengths = with_ends(jax.random.randint(seeds[2], (ROWS, WORDS), 1, SLOTS + 1), jax.random.fold_in(seeds[2], 1), 1, SLOTS).astype(jnp.int32)
    doc_lengths = jax.vmap(lambda own: ragged(own, NDOC, WORDS, WORDS // 2, 0))(jax.random.split(seeds[3], ROWS)).reshape((ROWS, NDOC)).astype(jnp.int32)
    embedding = bell_draw(seeds[4], (VOCAB, CW), 1.0, 6.0, ((0, 32),))
    char_qkv = bell_draw(seeds[5], (LAYERS, CW, 3 * CW), CW ** -0.5, 0.375, ((1, 4), (2, 8)))
    char_out_w = bell_draw(seeds[6], (LAYERS, CW, CW), (CW // 8) ** -0.5, 1.0, ((1, 4), (2, 8)))
    char_up = bell_draw(seeds[7], (LAYERS, CW, CF), CW ** -0.5, 0.375, ((1, 4), (2, 8)))
    char_down = bell_draw(seeds[8], (LAYERS, CF, CW), (CF // 2) ** -0.5, 0.25, ((1, 4), (2, 8)))
    char_proj = bell_draw(seeds[9], (LAYERS, CW, WW), (CW // 8) ** -0.5, 1.0, ((1, 4), (2, 8)))
    word_qkv = bell_draw(seeds[10], (LAYERS, WW, 3 * WW), WW ** -0.5, 0.25, ((1, 4), (2, 8)))
    word_out_w = bell_draw(seeds[11], (LAYERS, WW, WW), (WW // 16) ** -0.5, 1.0, ((1, 4), (2, 8)))
    word_up = bell_draw(seeds[12], (LAYERS, WW, WF), WW ** -0.5, 0.25, ((1, 4), (2, 8)))
    word_down = bell_draw(seeds[13], (LAYERS, WF, WW), (WF // 2) ** -0.5, 0.1875, ((1, 4), (2, 8)))
    char_gains = jnp.clip(1.0 + 0.1 * jax.random.normal(seeds[14], (LAYERS, 2, CW), jnp.float32), 0.5, 1.5)
    char_shifts = bell_draw(seeds[15], (LAYERS, 2, CW), 0.3, 1.5, (), jnp.float32)
    pool_query = bell_draw(seeds[16], (LAYERS, CW), CW ** -0.5, 0.375, (), jnp.float32)
    word_gains = jnp.clip(1.0 + 0.1 * jax.random.normal(seeds[17], (LAYERS, 2, WW), jnp.float32), 0.5, 1.5)
    word_shifts = bell_draw(seeds[18], (LAYERS, 2, WW), 0.3, 1.5, (), jnp.float32)
    char_cot = bell_draw(seeds[19], (ROWS, WORDS, SLOTS, CW), 1.0, 6.0, ((0, 32),))
    word_cot = bell_draw(seeds[20], (ROWS, WORDS, WW), 1.0, 6.0, ((0, 32),))
    return dict(word_states=word_states, character_ids=character_ids, word_lengths=word_lengths, doc_lengths=doc_lengths, embedding=embedding, char_qkv=char_qkv, char_out_w=char_out_w, char_up=char_up, char_down=char_down, char_proj=char_proj, word_qkv=word_qkv, word_out_w=word_out_w, word_up=word_up, word_down=word_down, char_gains=char_gains, char_shifts=char_shifts, pool_query=pool_query, word_gains=word_gains, word_shifts=word_shifts, char_cot=char_cot, word_cot=word_cot)


@jax.custom_vjp
def low(v):
    return lax.optimization_barrier(v.astype(jnp.bfloat16)).astype(jnp.float32)

@jax.custom_vjp
def low_back(v):
    return v

def low_keep(v):
    return (low(v), None)

def low_pass(kept, grad):
    return (grad,)

def back_keep(v):
    return (v, None)

def back_low(kept, grad):
    return (low(grad),)
low.defvjp(low_keep, low_pass)
low_back.defvjp(back_keep, back_low)
exact_precision = lax.Precision.HIGHEST
masked_score = -1e+30

def rounded_operands(value):
    return low_back(low(value))

def matrix_multiply(left, right):
    return jnp.dot(left, right, precision=exact_precision)

def layer_norm(states, gain, shift):
    centre = states - lax.optimization_barrier(jnp.mean(states, axis=-1, keepdims=True))
    spread = lax.optimization_barrier(jnp.mean(centre * centre, axis=-1, keepdims=True))
    return centre * lax.rsqrt(spread + 1e-05) * gain + shift

def gelu_value(states):
    return 0.5 * states * (1.0 + jnp.tanh(0.7978845608028654 * (states + 0.044715 * states * states * states)))

def softmax_last(scores):
    shifted = jnp.exp(scores - lax.optimization_barrier(jnp.max(scores, axis=-1, keepdims=True)))
    return shifted / lax.optimization_barrier(jnp.sum(shifted, axis=-1, keepdims=True))

def pool_words(states, pooling_query_vector, valid_key_mask):
    scores = jnp.einsum('wsd,d->ws', states, pooling_query_vector, precision=exact_precision)
    weights = softmax_last(jnp.where(valid_key_mask, scores, masked_score))
    return jnp.einsum('ws,wsd->wd', weights, states, precision=exact_precision)

def build_masks(lengths_row, docs_row):
    slot_index = jnp.arange(SLOTS, dtype=jnp.int32)
    valid_key_mask = slot_index[None, :] < lengths_row[:, None]
    bounds = jnp.cumsum(docs_row).astype(jnp.int32)
    places = jnp.arange(WORDS, dtype=jnp.int32)
    document = lax.optimization_barrier(jnp.sum((places[:, None] >= bounds[None, :]).astype(jnp.int32), axis=-1))
    allowed = (document[:, None] == document[None, :]) & (places[None, :] <= places[:, None])
    return (valid_key_mask, allowed)

def nested_layer(character_states, word_now, matrices, vectors, valid_key_mask, allowed):
    character_qkv_weight, c_out, c_up, c_down, c_proj, w_qkv, w_out, w_up, w_down = matrices
    c_gain, c_shift, pooling_query_vector, w_gain, w_shift = vectors
    words_count, slots_count, character_width = character_states.shape
    wwidth = word_now.shape[-1]
    normalized_input = low(layer_norm(character_states, c_gain[0], c_shift[0]))
    projected_output = rounded_operands(matrix_multiply(normalized_input, character_qkv_weight)).reshape(words_count, slots_count, 3, CHARACTER_HEADS, character_width // CHARACTER_HEADS)
    scores = jnp.einsum('wqhd,wkhd->whqk', projected_output[:, :, 0], projected_output[:, :, 1], precision=exact_precision) * (character_width // CHARACTER_HEADS) ** (-0.5)
    scores = low_back(jnp.where(valid_key_mask[:, None, None, :], scores, masked_score))
    attend_heads = low(softmax_last(scores))
    mixed_heads = rounded_operands(jnp.einsum('gebi,giev->gbev', attend_heads, projected_output[:, :, 2], precision=exact_precision)).reshape(words_count, slots_count, character_width)
    character_states = character_states + low_back(matrix_multiply(mixed_heads, c_out))
    normalized_input = low(layer_norm(character_states, c_gain[1], c_shift[1]))
    hidden = low_back(matrix_multiply(normalized_input, c_up))
    character_states = character_states + low_back(matrix_multiply(low(gelu_value(hidden)), c_down))
    pooled = pool_words(character_states, pooling_query_vector, valid_key_mask)
    word_now = word_now + low_back(matrix_multiply(low(pooled), c_proj))
    normalized_input = low(layer_norm(word_now, w_gain[0], w_shift[0]))
    projected_output = rounded_operands(matrix_multiply(normalized_input, w_qkv)).reshape(words_count, 3, WORD_HEADS, wwidth // WORD_HEADS)
    scores = jnp.einsum('qhd,khd->hqk', projected_output[:, 0], projected_output[:, 1], precision=exact_precision) * (wwidth // WORD_HEADS) ** (-0.5)
    scores = low_back(jnp.where(allowed[None], scores, masked_score))
    attend_heads = low(softmax_last(scores))
    mixed_heads = rounded_operands(jnp.einsum('hqk,khd->qhd', attend_heads, projected_output[:, 2], precision=exact_precision)).reshape(words_count, wwidth)
    word_now = word_now + low_back(matrix_multiply(mixed_heads, w_out))
    normalized_input = low(layer_norm(word_now, w_gain[1], w_shift[1]))
    hidden = low_back(matrix_multiply(normalized_input, w_up))
    word_now = word_now + low_back(matrix_multiply(low(gelu_value(hidden)), w_down))
    return (character_states, word_now)

def reference(word_states, character_ids, word_lengths, doc_lengths, embedding, char_qkv, char_out_w, char_up, char_down, char_proj, word_qkv, word_out_w, word_up, word_down, char_gains, char_shifts, pool_query, word_gains, word_shifts, char_cot, word_cot):
    values = tuple((item.astype(jnp.float32) for item in (word_states, embedding, char_qkv, char_out_w, char_up, char_down, char_proj, word_qkv, word_out_w, word_up, word_down, char_gains, char_shifts, pool_query, word_gains, word_shifts)))

    def forward(word_in, table, character_qkv_weight, c_out, c_up, c_down, c_proj, w_qkv, w_out, w_up, w_down, c_gain, c_shift, pool_vec, w_gain, w_shift):

        def one_row(item):
            ids_row, words_row, lengths_row, docs_row = item
            valid_key_mask, allowed = build_masks(lengths_row, docs_row)
            character_states = table[ids_row]
            word_now = words_row
            for layer_index in range(LAYERS):
                matrices = (character_qkv_weight[layer_index], c_out[layer_index], c_up[layer_index], c_down[layer_index], c_proj[layer_index], w_qkv[layer_index], w_out[layer_index], w_up[layer_index], w_down[layer_index])
                vectors = (c_gain[layer_index], c_shift[layer_index], pool_vec[layer_index], w_gain[layer_index], w_shift[layer_index])
                character_states, word_now = nested_layer(character_states, word_now, matrices, vectors, valid_key_mask, allowed)
            return (character_states, word_now)
        return lax.map(jax.checkpoint(one_row), (character_ids, word_in, word_lengths, doc_lengths))
    outputs, pullback = jax.vjp(forward, *values)
    grads = pullback((char_cot.astype(jnp.float32), word_cot.astype(jnp.float32)))
    return (outputs[0].astype(jnp.bfloat16), outputs[1].astype(jnp.bfloat16), grads[0], grads[1], grads[2], grads[3], grads[4], grads[5], grads[6], grads[7], grads[8], grads[9], grads[10], grads[11], grads[12], grads[13], grads[14], grads[15])
```

```python
from functools import partial

import jax
import jax.numpy as jnp
from jax import lax
from jax.experimental import pallas as pl
from jax.experimental.pallas import tpu as pltpu
from jax.sharding import PartitionSpec as P

F32 = jnp.float32
BF = jnp.bfloat16
SLOTS = 16
masked_score = -1e30
ROOT = 0.7978845608028654
CUBE = 0.044715
LANES = 128
C_QKV, C_OUT, C_UP, C_PROJ, C_DOWN, C_EMB = (0, 48), (48, 16), (64, 64), (128, 32), (160, 32), (224, 16)
C_PAIRED = (C_QKV, C_OUT, C_UP, C_PROJ)
C_ROWS = 224
W_QKV, W_OUT, W_UP, W_DOWN = (0, 192), (192, 64), (256, 256), (512, 64)
W_ROWS = 768
BLOCK = 256


def dot(left, right, l, r):
    return lax.dot_general(left, right, (((l,), (r,)), ((), ())), preferred_element_type=F32)


def nn(left, right):
    return dot(left, right, 1, 0)


def nt(left, right):
    return dot(left, right, 1, 1)


def tn(left, right):
    return dot(left, right, 0, 0)


def iota(shape, dim):
    return lax.broadcasted_iota(jnp.int32, shape, dim)


def norm_parts(states):
    centre = states - jnp.mean(states, axis=-1, keepdims=True)
    spread = jnp.mean(centre * centre, axis=-1, keepdims=True)
    root = lax.rsqrt(spread + 1e-05)
    return centre * root, root


def norm_back(grad, hat, root, gain):
    scaled = grad * gain
    inner = scaled - jnp.mean(scaled, axis=-1, keepdims=True)
    back = root * (inner - hat * jnp.mean(scaled * hat, axis=-1, keepdims=True))
    return back, jnp.sum(grad * hat, axis=0, keepdims=True), jnp.sum(grad, axis=0, keepdims=True)


def gelu_value(h):
    return 0.5 * h * (1.0 + jnp.tanh(ROOT * (h + CUBE * h * h * h)))


def gelu_both(h):
    square = h * h
    t = jnp.tanh(ROOT * (h + CUBE * square * h))
    half = 0.5 * (1.0 + t)
    slope = half + 0.5 * h * (1.0 - t * t) * (ROOT * (1.0 + 3.0 * CUBE * square))
    return h * half, slope


def softmax_rows(scores):
    shifted = jnp.exp(scores - jnp.max(scores, axis=-1, keepdims=True))
    return shifted / jnp.sum(shifted, axis=-1, keepdims=True)


def low_half(shape):
    return iota(shape, len(shape) - 1) % LANES < 64


def two_heads(x):
    low = low_half(x.shape)
    zero = jnp.zeros_like(x)
    return jnp.concatenate([jnp.where(low, x, zero), jnp.where(low, zero, x)], axis=0)


def join_heads(x):
    k = x.shape[0] // 2
    return jnp.where(low_half((k, LANES)), x[:k], x[k:])


def place(rw, ry, x_first):
    rx, rz = rw & 1, rw >> 1
    return ry * 8 + rx * 4 + rz if x_first else rx * 8 + ry * 4 + rz


def unplace(q, s, x_first):
    a, rz = s >> 2, s & 3
    rx, ry = (a, q) if x_first else (q, a)
    return rz * 2 + rx, ry


def pack_kernel(cq, co, cu, cd, cp, wq, wo, wu, wd, emb, c0, c1, w0, w1):
    def turned(x):
        return x.astype(F32).T

    for layer, c in enumerate((c0, c1)):
        for ref, (row, rows) in zip((cq, co, cu, cp), C_PAIRED):
            t = turned(ref[layer])
            c[row : row + rows, :] = jnp.concatenate([t[:rows], t[rows:]], axis=1).astype(BF)
        t = turned(cd[layer])
        for k in range(2):
            row = C_DOWN[0] + 32 * k
            c[row : row + 32, :] = t[:, k * LANES : (k + 1) * LANES].astype(BF)
    e = emb[...].astype(F32)
    c0[C_EMB[0] : C_EMB[0] + 16, :] = jnp.concatenate([e[:, :LANES], e[:, LANES:]], axis=0).astype(BF)
    for layer, w in enumerate((w0, w1)):
        for ref, (row, rows) in zip((wq, wo, wu), (W_QKV, W_OUT, W_UP)):
            w[row : row + rows, :] = turned(ref[layer]).astype(BF)
        t = turned(wd[layer])
        for k in range(4):
            row = W_DOWN[0] + 64 * k
            w[row : row + 64, :] = t[:, k * LANES : (k + 1) * LANES].astype(BF)


def whole(shape, dtype):
    return jax.ShapeDtypeStruct(shape, dtype)


def cost(flops, moved):
    return pl.CostEstimate(flops=int(flops), bytes_accessed=int(moved), transcendentals=0)


def pack(weights, embedding):
    return pl.pallas_call(
        pack_kernel,
        out_shape=(
            whole((C_ROWS + 16, LANES), BF),
            whole((C_ROWS, LANES), BF),
            whole((W_ROWS, LANES), BF),
            whole((W_ROWS, LANES), BF),
        ),
        cost_estimate=cost(0, 4e6),
    )(*weights, embedding)


def unpack_kernel(c0, c1, w0, w1, cq, co, cu, cd, cp, wq, wo, wu, wd, emb):
    for layer, c in enumerate((c0, c1)):
        for ref, (row, rows) in zip((cq, co, cu, cp), C_PAIRED):
            t = c[row : row + rows, :]
            ref[layer] = jnp.concatenate([t[:, :64], t[:, 64:]], axis=0).T
        t = [c[C_DOWN[0] + 32 * k : C_DOWN[0] + 32 * k + 32, :] for k in range(2)]
        cd[layer] = jnp.concatenate(t, axis=1).T
    e = c0[C_EMB[0] : C_EMB[0] + 16, :]
    emb[...] = jnp.concatenate([e[:8], e[8:]], axis=1)
    for layer, w in enumerate((w0, w1)):
        for ref, (row, rows) in zip((wq, wo, wu), (W_QKV, W_OUT, W_UP)):
            ref[layer] = w[row : row + rows, :].T
        t = [w[W_DOWN[0] + 64 * k : W_DOWN[0] + 64 * k + 64, :] for k in range(4)]
        wd[layer] = jnp.concatenate(t, axis=1).T


def unpack(blocks, weights, embedding):
    return pl.pallas_call(
        unpack_kernel,
        out_shape=tuple(whole(x.shape, F32) for x in (*weights, embedding)),
        cost_estimate=cost(0, 8e6),
    )(*blocks)


def fetch_char(x_first, me, parts, raw, mats, table, sems):
    copies = [
        pltpu.make_async_copy(part, raw.at[pl.ds(8 * k, 8)], sems.at[k]) for k, part in enumerate(parts)
    ]
    for copy in copies:
        copy.start()
    for copy in copies:
        copy.wait()
    mw, my, mc = me[0], me[1] >> 1, me[1] & 1
    for w in range(8):
        for y in range(2):
            at = place(w ^ mw, y ^ my, x_first)
            cores = (mc * 16 + at, (1 - mc) * 16 + at)
            for ref, (row, rows) in zip(mats[:4], C_PAIRED):
                zero, one = (raw[k, row : row + rows, :] for k in cores)
                first = w * 2 * rows
                columns = slice(y * LANES, (y + 1) * LANES)
                ref[first : first + rows, columns] = jnp.concatenate([zero[:, :64], one[:, :64]], axis=1)
                ref[first + rows : first + 2 * rows, columns] = jnp.concatenate(
                    [zero[:, 64:], one[:, 64:]], axis=1
                )
            for c, k in enumerate(cores):
                for t in range(2):
                    column = (2 * y + c) * 256 + t * LANES
                    row = C_DOWN[0] + 32 * t
                    mats[4][w * 32 : w * 32 + 32, column : column + LANES] = raw[k, row : row + 32, :]
    if table is not None:
        for k in range(32):
            table[k * 16 : k * 16 + 16, :] = raw[k, C_EMB[0] : C_EMB[0] + 16, :]


def char_positions(ids, me, x_first):
    device = ids >> 3
    rw = (device >> 2) ^ me[0]
    rn = (device & 3) ^ me[1]
    return ((rn & 1) * 16 + place(rw, rn >> 1, x_first)) * 16 + (ids & 7)


def valid_keys(lens, first):
    lane = iota((1, LANES), 1)
    length = jnp.zeros((1, LANES), jnp.int32)
    for k in range(8):
        length = jnp.where(lane // SLOTS == k, lens[0, first + k], length)
    return lane % SLOTS < length


def to_column(row):
    square = (LANES, LANES)
    return jnp.sum(jnp.where(iota(square, 0) == iota(square, 1), row, 0.0), axis=-1, keepdims=True)


def char_attend(q, keys, allowed):
    scores = nt(q, keys) * 0.125
    scores = jnp.where(allowed, scores, masked_score)
    return jnp.concatenate([softmax_rows(scores[:, :LANES]), softmax_rows(scores[:, LANES:])], axis=1)


def char_masks(lens, block):
    out = []
    same = iota((LANES, LANES), 0) // SLOTS == iota((LANES, LANES), 1) // SLOTS
    for half in range(2):
        valid = valid_keys(lens, block * 16 + half * 8)
        pair = same & valid
        out.append((jnp.concatenate([pair, pair], axis=1), to_column(jnp.where(valid, 1.0, 0.0))))
    return out


def pool_weights(states, query, valid):
    scores = jnp.sum(states * query, axis=-1, keepdims=True)
    scores = jnp.where(valid > 0.5, scores, masked_score).reshape(16, SLOTS, 1)
    shifted = jnp.exp(scores - jnp.max(scores, axis=1, keepdims=True))
    return shifted / jnp.sum(shifted, axis=1, keepdims=True)


def char_forward_kernel(first, x_first, *refs):
    me, lens, source, p0, p1, p2, p3, gain, shift, query = refs[:10]
    refs = refs[10:]
    if first:
        x_out, refs = refs[0], refs[1:]
    qkv_out, mixed_out, after_out, hidden_out, next_out, pooled_out, delta_out = refs[:7]
    raw, m_qkv, m_out, m_up, m_proj, m_down, table, sems = refs[7:]
    block = pl.program_id(0)

    @pl.when(block == 0)
    def _():
        fetch_char(
            x_first, me, (p0, p1, p2, p3), raw, (m_qkv, m_out, m_up, m_proj, m_down), table if first else None, sems
        )

    if first:
        parts = []
        for half in range(2):
            ids = source[pl.ds(block * 2 + half, 1), :]
            column = to_column(char_positions(ids, me, x_first).astype(F32)).astype(jnp.int32)
            lane = iota((LANES, 512), 1)
            left = jnp.where(lane == column, 1.0, 0.0).astype(BF)
            right = jnp.where(lane == column + 8, 1.0, 0.0).astype(BF)
            parts.append(jnp.concatenate([nn(left, table[...]), nn(right, table[...])], axis=1))
        x = jnp.concatenate(parts, axis=0)
        x_out[...] = x
    else:
        x = source[...]
    hat, _ = norm_parts(x)
    normed = (hat * gain[0:1] + shift[0:1]).astype(BF)
    qkv = nt(normed, m_qkv[...]).astype(BF)
    qkv_out[...] = qkv
    masks = char_masks(lens, block)
    halves = []
    for half in range(2):
        rows = slice(half * LANES, (half + 1) * LANES)
        pairs = []
        for pair in range(2):
            q, k, v = (qkv[rows, t * 256 + pair * LANES : t * 256 + (pair + 1) * LANES] for t in range(3))
            attend = char_attend(q, two_heads(k), masks[half][0])
            pairs.append(nn(attend.astype(BF), two_heads(v)))
        halves.append(jnp.concatenate(pairs, axis=1))
    mixed = jnp.concatenate(halves, axis=0).astype(BF)
    mixed_out[...] = mixed
    after = x + nt(mixed, m_out[...])
    after_out[...] = after
    hat, _ = norm_parts(after)
    normed = (hat * gain[1:2] + shift[1:2]).astype(BF)
    hidden = nt(normed, m_up[...])
    hidden_out[...] = hidden
    states = after + nt(gelu_value(hidden).astype(BF), m_down[...])
    next_out[...] = states
    valid = jnp.concatenate([masks[0][1], masks[1][1]], axis=0)
    weights = pool_weights(states, query[...], valid)
    pooled = jnp.sum(weights * states.reshape(16, SLOTS, 256), axis=1).astype(BF)
    pooled_out[...] = pooled
    delta_out[...] = nt(pooled, m_proj[...])


def char_scratch(first):
    rows = C_ROWS + (16 if first else 0)
    return [
        pltpu.VMEM((32, rows, LANES), BF),
        pltpu.VMEM((768, 256), BF),
        pltpu.VMEM((256, 256), BF),
        pltpu.VMEM((1024, 256), BF),
        pltpu.VMEM((512, 256), BF),
        pltpu.VMEM((256, 1024), BF),
    ]


def rows_spec(rows, columns):
    return pl.BlockSpec((rows, columns), lambda i: (i, 0))


def fixed_spec(shape):
    return pl.BlockSpec(shape, lambda i: (0,) * len(shape))


smem = pl.BlockSpec(memory_space=pltpu.SMEM)
anywhere = pl.BlockSpec(memory_space=pl.ANY)


def char_forward(first, x_first, me, lens, source, parts, gain, shift, query):
    rows = lens.shape[1] * SLOTS
    grid = rows // BLOCK
    shapes = [(768, BF), (256, BF), (256, F32), (1024, F32), (256, F32)]
    if first:
        shapes = [(256, F32)] + shapes
    out = [(rows, BLOCK, c, t) for c, t in shapes]
    out += [(rows // SLOTS, BLOCK // SLOTS, 256, BF), (rows // SLOTS, BLOCK // SLOTS, 512, F32)]
    return pl.pallas_call(
        partial(char_forward_kernel, first, x_first),
        grid=(grid,),
        in_specs=[smem, smem, fixed_spec(source.shape) if first else rows_spec(BLOCK, 256)]
        + [anywhere] * 4
        + [fixed_spec((2, 256)), fixed_spec((2, 256)), fixed_spec((1, 256))],
        out_specs=[rows_spec(b, c) for _, b, c, _ in out],
        out_shape=[whole((r, c), t) for r, _, c, t in out],
        scratch_shapes=char_scratch(first)
        + [pltpu.VMEM((512, LANES) if first else (16, LANES), BF), pltpu.SemaphoreType.DMA((4,))],
        compiler_params=pltpu.CompilerParams(vmem_limit_bytes=40 << 20),
        cost_estimate=cost(2e9, 14e6),
    )(me, lens, source, *parts, gain, shift, query)


def pool_back(states, query, valid, grad):
    weights = pool_weights(states, query, valid)
    cube = states.reshape(16, SLOTS, 256)
    wide = grad.reshape(16, 1, 256)
    by_weight = jnp.sum(cube * wide, axis=-1, keepdims=True)
    by_score = weights * (by_weight - jnp.sum(weights * by_weight, axis=1, keepdims=True))
    added = weights * wide + by_score * query.reshape(1, 1, 256)
    by_query = jnp.sum((by_score * cube).reshape(256, 256), axis=0, keepdims=True)
    return added.reshape(256, 256), by_query


def char_backward_kernel(first, x_first, *refs):
    me, lens = refs[:2]
    refs = refs[2:]
    if first:
        ids, refs = refs[0], refs[1:]
    (grad_in, word_grad, x_in, qkv_in, mixed_in, after_in, hidden_in, next_in, pooled_in) = refs[:9]
    p0, p1, p2, p3, gain, shift, query = refs[9:16]
    refs = refs[16:]
    if not first:
        grad_out, refs = refs[0], refs[1:]
    keep, send, vectors = refs[:3]
    raw, m_qkv, m_out, m_up, m_proj, m_down, a_qkv, a_out, a_up, a_proj, a_down, a_table, sems = refs[3:]
    block = pl.program_id(0)
    rows_held = C_ROWS + (16 if first else 0)

    @pl.when(block == 0)
    def _():
        fetch_char(x_first, me, (p0, p1, p2, p3), raw, (m_qkv, m_out, m_up, m_proj, m_down), None, sems)
        for ref in (a_qkv, a_out, a_up, a_proj, a_down, a_table, vectors):
            ref[...] = jnp.zeros(ref.shape, ref.dtype)

    masks = char_masks(lens, block)
    low_word = word_grad[...].astype(BF)
    a_proj[...] += tn(low_word, pooled_in[...])
    grad_pooled = nn(low_word, m_proj[...])
    valid = jnp.concatenate([masks[0][1], masks[1][1]], axis=0)
    added, by_query = pool_back(next_in[...], query[...], valid, grad_pooled)
    grad = grad_in[...].astype(F32) + added
    vectors[4:5, :] += by_query
    low = grad.astype(BF)
    act, slope = gelu_both(hidden_in[...])
    a_down[...] += tn(low, act.astype(BF))
    by_hidden = (slope * nn(low, m_down[...])).astype(BF)
    hat, root = norm_parts(after_in[...])
    normed = (hat * gain[1:2] + shift[1:2]).astype(BF)
    a_up[...] += tn(normed, by_hidden)
    back, by_gain, by_shift = norm_back(nn(by_hidden, m_up[...]), hat, root, gain[1:2])
    grad = grad + back
    vectors[1:2, :] += by_gain
    vectors[3:4, :] += by_shift
    low = grad.astype(BF)
    a_out[...] += tn(low, mixed_in[...])
    by_mixed = nn(low, m_out[...]).astype(BF)
    sides = []
    for half in range(2):
        rows = slice(half * LANES, (half + 1) * LANES)
        by_q, by_k, by_v = [], [], []
        for pair in range(2):
            q, k, v = (qkv_in[rows, t * 256 + pair * LANES : t * 256 + (pair + 1) * LANES] for t in range(3))
            keys = two_heads(k)
            attend = char_attend(q, keys, masks[half][0])
            g = by_mixed[rows, pair * LANES : (pair + 1) * LANES]
            by_attend = nt(g, two_heads(v))
            product = attend * by_attend
            inner = jnp.concatenate(
                [
                    jnp.broadcast_to(jnp.sum(product[:, h : h + LANES], axis=-1, keepdims=True), (LANES, LANES))
                    for h in (0, LANES)
                ],
                axis=1,
            )
            by_scores = (product - attend * inner).astype(BF)
            by_v.append(join_heads(tn(attend.astype(BF), g)))
            by_q.append(nn(by_scores, keys) * 0.125)
            by_k.append(join_heads(tn(by_scores, q)) * 0.125)
        sides.append(jnp.concatenate(by_q + by_k + by_v, axis=1))
    by_qkv = jnp.concatenate(sides, axis=0).astype(BF)
    hat, root = norm_parts(x_in[...])
    normed = (hat * gain[0:1] + shift[0:1]).astype(BF)
    a_qkv[...] += tn(normed, by_qkv)
    back, by_gain, by_shift = norm_back(nn(by_qkv, m_qkv[...]), hat, root, gain[0:1])
    grad = grad + back
    vectors[0:1, :] += by_gain
    vectors[2:3, :] += by_shift
    if first:
        for half in range(2):
            at = char_positions(ids[pl.ds(block * 2 + half, 1), :], me, x_first)
            row = iota((512, LANES), 0)
            part = grad[half * LANES : (half + 1) * LANES]
            high = part.astype(BF)
            rest = (part - high.astype(F32)).astype(BF)
            both = jnp.concatenate([high, rest], axis=0)
            for side in range(2):
                hot = jnp.where(row == at + 8 * side, 1.0, 0.0).astype(BF)
                hot = jnp.concatenate([hot, hot], axis=1)
                a_table[...] += nn(hot, both[:, side * LANES : (side + 1) * LANES])
    else:
        grad_out[...] = grad

    @pl.when(block == pl.num_programs(0) - 1)
    def _():
        mw, my, mc = me[0], me[1] >> 1, me[1] & 1
        for ref, turn in ((a_qkv, m_qkv), (a_up, m_up)):
            turn[...] = ref[...].T.astype(BF)
        for ref, to in ((a_out, m_out), (a_proj, m_proj), (a_down, m_down)):
            to[...] = ref[...].astype(BF)

        def put(at, row, rows, zero, one):
            keep[at, row : row + rows, :] = jnp.where(mc == 0, zero, one)
            send[at, row : row + rows, :] = jnp.where(mc == 0, one, zero)

        for w in range(8):
            for y in range(2):
                at = place(w ^ mw, y ^ my, x_first)
                for ref, (row, rows) in zip((m_qkv, m_out, m_up, m_proj), C_PAIRED):
                    columns = slice(y * LANES, (y + 1) * LANES)
                    top = ref[w * 2 * rows : w * 2 * rows + rows, columns]
                    bottom = ref[w * 2 * rows + rows : w * 2 * rows + 2 * rows, columns]
                    put(
                        at,
                        row,
                        rows,
                        jnp.concatenate([top[:, :64], bottom[:, :64]], axis=1),
                        jnp.concatenate([top[:, 64:], bottom[:, 64:]], axis=1),
                    )
                for t in range(2):
                    zero, one = (
                        m_down[w * 32 : w * 32 + 32, (2 * y + c) * 256 + t * LANES : (2 * y + c) * 256 + (t + 1) * LANES]
                        for c in range(2)
                    )
                    put(at, C_DOWN[0] + 32 * t, 32, zero, one)
        if first:
            for k in range(16):
                keep[k, C_EMB[0] : C_EMB[0] + 16, :] = a_table[k * 16 : k * 16 + 16, :].astype(BF)
                send[k, C_EMB[0] : C_EMB[0] + 16, :] = a_table[256 + k * 16 : 272 + k * 16, :].astype(BF)


def char_backward(first, x_first, me, lens, ids, grad, word_grad, saved, parts, gain, shift, query):
    x, qkv, mixed, after, hidden, states, pooled = saved
    rows = x.shape[0]
    grid = rows // BLOCK
    held = C_ROWS + (16 if first else 0)
    operands = [me, lens] + ([ids] if first else [])
    specs = [smem, smem] + ([fixed_spec(ids.shape)] if first else [])
    outs = [] if first else [whole((rows, 256), F32)]
    out_specs = [] if first else [rows_spec(BLOCK, 256)]
    return pl.pallas_call(
        partial(char_backward_kernel, first, x_first),
        grid=(grid,),
        in_specs=specs
        + [
            rows_spec(BLOCK, 256),
            rows_spec(BLOCK // SLOTS, 512),
            rows_spec(BLOCK, 256),
            rows_spec(BLOCK, 768),
            rows_spec(BLOCK, 256),
            rows_spec(BLOCK, 256),
            rows_spec(BLOCK, 1024),
            rows_spec(BLOCK, 256),
            rows_spec(BLOCK // SLOTS, 256),
        ]
        + [anywhere] * 4
        + [fixed_spec((2, 256)), fixed_spec((2, 256)), fixed_spec((1, 256))],
        out_specs=out_specs + [fixed_spec((16, held, LANES))] * 2 + [fixed_spec((8, 256))],
        out_shape=outs + [whole((16, held, LANES), BF)] * 2 + [whole((8, 256), F32)],
        scratch_shapes=char_scratch(first)
        + [
            pltpu.VMEM((256, 768), F32),
            pltpu.VMEM((256, 256), F32),
            pltpu.VMEM((256, 1024), F32),
            pltpu.VMEM((512, 256), F32),
            pltpu.VMEM((256, 1024), F32),
            pltpu.VMEM((512 if first else 8, LANES), F32),
            pltpu.SemaphoreType.DMA((4,)),
        ],
        compiler_params=pltpu.CompilerParams(vmem_limit_bytes=48 << 20),
        cost_estimate=cost(4e9, 24e6),
    )(*operands, grad, word_grad, x, qkv, mixed, after, hidden, states, pooled, *parts, gain, shift, query)


def fetch_word(x_first, me, parts, upper, down, sems):
    for k, part in enumerate(parts):
        rc, q = k >> 1, k & 1

        def one(s, _, part=part, rc=rc, q=q):
            rw, ry = unplace(q, s, x_first)
            w, n = rw ^ me[0], (ry * 2 + rc) ^ me[1]
            block = part.at[s]
            column = pl.ds(pl.multiple_of(n * LANES, LANES), LANES)
            for base, (row, rows) in ((0, W_QKV), (1536, W_OUT), (2048, W_UP)):
                to = pl.ds(pl.multiple_of(base + w * rows, 64), rows)
                pltpu.make_async_copy(block.at[pl.ds(row, rows)], upper.at[to, column], sems.at[0]).start()
            for t in range(4):
                column = pl.ds(pl.multiple_of(n * 512 + t * LANES, LANES), LANES)
                to = pl.ds(pl.multiple_of(w * 64, 64), 64)
                pltpu.make_async_copy(
                    block.at[pl.ds(W_DOWN[0] + 64 * t, 64)], down.at[to, column], sems.at[1]
                ).start()
            return 0

        lax.fori_loop(0, 8, one, 0)
    pltpu.make_async_copy(upper, upper, sems.at[0]).wait()
    pltpu.make_async_copy(down, down, sems.at[1]).wait()


def word_allowed(docs, words):
    shape = (words, 2 * words)
    i, j = iota(shape, 0), iota(shape, 1) % words
    end = 0
    of_i, of_j = jnp.zeros(shape, jnp.int32), jnp.zeros(shape, jnp.int32)
    for k in range(docs.shape[1]):
        end = end + docs[0, k]
        of_i = of_i + (i >= end).astype(jnp.int32)
        of_j = of_j + (j >= end).astype(jnp.int32)
    return (of_i == of_j) & (j <= i)


def by_half(x, reduce, fill):
    low = low_half(x.shape)
    left = reduce(jnp.where(low, x, fill), axis=-1, keepdims=True)
    right = reduce(jnp.where(low, fill, x), axis=-1, keepdims=True)
    return jnp.where(low, left, right)


def word_attend(q, keys, allowed):
    scores = jnp.where(allowed, nt(q, keys) * 0.125, masked_score)
    shifted = jnp.exp(scores - by_half(scores, jnp.max, 2 * masked_score))
    return shifted / by_half(shifted, jnp.sum, 0.0)


def word_forward_body(w1, upper, down, gain, shift, allowed):
    hat, root = norm_parts(w1)
    normed = (hat * gain[0:1] + shift[0:1]).astype(BF)
    qkv = nt(normed, upper[0:1536, :]).astype(BF)
    mixed = []
    for pair in range(4):
        q, k, v = (qkv[:, t * 512 + pair * LANES : t * 512 + (pair + 1) * LANES] for t in range(3))
        attend = word_attend(q, two_heads(k), allowed)
        mixed.append(nn(attend.astype(BF), two_heads(v)))
    mixed = jnp.concatenate(mixed, axis=1).astype(BF)
    w2 = w1 + nt(mixed, upper[1536:2048, :])
    hat, root = norm_parts(w2)
    normed = (hat * gain[1:2] + shift[1:2]).astype(BF)
    hidden = nt(normed, upper[2048:4096, :])
    w3 = w2 + nt(gelu_value(hidden).astype(BF), down[...])
    return qkv, mixed, w2, hidden, w3


def word_backward_body(x_first, me, grad, w1, qkv, mixed, w2, hidden, upper, down, gain, shift, allowed, keep, send, vectors):
    mw, my, mc = me[0], me[1] >> 1, me[1] & 1
    words = grad.shape[0]

    def put(w, row, rows, blocks):
        for y in range(2):
            at = place(w ^ mw, y ^ my, x_first)
            zero, one = blocks(2 * y), blocks(2 * y + 1)
            keep[at, row : row + rows, :] = jnp.where(mc == 0, zero, one)
            send[at, row : row + rows, :] = jnp.where(mc == 0, one, zero)

    low = grad.astype(BF)
    act, slope = gelu_both(hidden)
    act = act.astype(BF)
    for pair in range(4):
        part = tn(low[:, pair * LANES : (pair + 1) * LANES], act).astype(BF)
        for k in range(2):
            for t in range(4):
                put(
                    2 * pair + k,
                    W_DOWN[0] + 64 * t,
                    64,
                    lambda n: part[k * 64 : k * 64 + 64, n * 512 + t * LANES : n * 512 + (t + 1) * LANES],
                )
    by_hidden = (slope * nn(low, down[...])).astype(BF)
    hat, root = norm_parts(w2)
    normed = (hat * gain[1:2] + shift[1:2]).astype(BF)
    for w in range(8):
        part = tn(by_hidden[:, w * 256 : (w + 1) * 256], normed).astype(BF)
        put(w, W_UP[0], 256, lambda n: part[:, n * LANES : (n + 1) * LANES])
    back, by_gain, by_shift = norm_back(nn(by_hidden, upper[2048:4096, :]), hat, root, gain[1:2])
    grad = grad + back
    vectors[1:2, :] = by_gain
    vectors[3:4, :] = by_shift
    low = grad.astype(BF)
    for pair in range(4):
        part = tn(low[:, pair * LANES : (pair + 1) * LANES], mixed).astype(BF)
        for k in range(2):
            put(
                2 * pair + k,
                W_OUT[0],
                64,
                lambda n: part[k * 64 : k * 64 + 64, n * LANES : (n + 1) * LANES],
            )
    by_mixed = nn(low, upper[1536:2048, :]).astype(BF)
    by_q, by_k, by_v = [], [], []
    for pair in range(4):
        q, k, v = (qkv[:, t * 512 + pair * LANES : t * 512 + (pair + 1) * LANES] for t in range(3))
        keys = two_heads(k)
        attend = word_attend(q, keys, allowed)
        g = by_mixed[:, pair * LANES : (pair + 1) * LANES]
        by_attend = nt(g, two_heads(v))
        product = attend * by_attend
        by_scores = (product - attend * by_half(product, jnp.sum, 0.0)).astype(BF)
        by_v.append(join_heads(tn(attend.astype(BF), g)))
        by_q.append(nn(by_scores, keys) * 0.125)
        by_k.append(join_heads(tn(by_scores, q)) * 0.125)
    by_qkv = jnp.concatenate(by_q + by_k + by_v, axis=1).astype(BF)
    hat, root = norm_parts(w1)
    normed = (hat * gain[0:1] + shift[0:1]).astype(BF)
    for pair in range(4):
        part = tn(by_qkv[:, pair * 384 : (pair + 1) * 384], normed).astype(BF)
        for k in range(2):
            put(
                2 * pair + k,
                W_QKV[0],
                192,
                lambda n: part[k * 192 : (k + 1) * 192, n * LANES : (n + 1) * LANES],
            )
    back, by_gain, by_shift = norm_back(nn(by_qkv, upper[0:1536, :]), hat, root, gain[0:1])
    vectors[0:1, :] = by_gain
    vectors[2:3, :] = by_shift
    vectors[4:8, :] = jnp.zeros((4, vectors.shape[1]), F32)
    return grad + back


def word_first_kernel(x_first, me, docs, w_in, delta, p0, p1, p2, p3, gain, shift, *refs):
    w1_out, qkv_out, mixed_out, w2_out, hidden_out, w3_out, upper, down, sems = refs
    fetch_word(x_first, me, (p0, p1, p2, p3), upper, down, sems)
    w1 = w_in[...].astype(F32) + delta[...]
    w1_out[...] = w1
    qkv, mixed, w2, hidden, w3 = word_forward_body(
        w1, upper, down, gain[...], shift[...], word_allowed(docs, w1.shape[0])
    )
    qkv_out[...] = qkv
    mixed_out[...] = mixed
    w2_out[...] = w2
    hidden_out[...] = hidden
    w3_out[...] = w3


word_scratch = [pltpu.VMEM((4096, 512), BF), pltpu.VMEM((512, 2048), BF), pltpu.SemaphoreType.DMA((2,))]
vmem = pl.BlockSpec(memory_space=pltpu.VMEM)


def word_first(x_first, me, docs, w_in, delta, parts, gain, shift):
    words = w_in.shape[0]
    shapes = [(512, F32), (1536, BF), (512, BF), (512, F32), (2048, F32), (512, F32)]
    return pl.pallas_call(
        partial(word_first_kernel, x_first),
        in_specs=[smem, smem, vmem, vmem] + [anywhere] * 4 + [vmem, vmem],
        out_specs=[vmem] * len(shapes),
        out_shape=[whole((words, c), t) for c, t in shapes],
        scratch_shapes=word_scratch,
        compiler_params=pltpu.CompilerParams(vmem_limit_bytes=32 << 20),
        cost_estimate=cost(1e9, 9e6),
    )(me, docs, w_in, delta, *parts, gain, shift)


def word_last_kernel(x_first, me, docs, w_in, delta, cot, p0, p1, p2, p3, gain, shift, *refs):
    w3_out, grad_out, keep, send, vectors, upper, down, sems = refs
    fetch_word(x_first, me, (p0, p1, p2, p3), upper, down, sems)
    w1 = w_in[...] + delta[...]
    allowed = word_allowed(docs, w1.shape[0])
    gain, shift = gain[...], shift[...]
    qkv, mixed, w2, hidden, w3 = word_forward_body(w1, upper, down, gain, shift, allowed)
    w3_out[...] = w3.astype(BF)
    grad_out[...] = word_backward_body(
        x_first, me, cot[...].astype(F32), w1, qkv, mixed, w2, hidden, upper, down, gain, shift, allowed, keep, send, vectors
    )


def word_last(x_first, me, docs, w_in, delta, cot, parts, gain, shift):
    words = w_in.shape[0]
    return pl.pallas_call(
        partial(word_last_kernel, x_first),
        in_specs=[smem, smem, vmem, vmem, vmem] + [anywhere] * 4 + [vmem, vmem],
        out_specs=[vmem] * 5,
        out_shape=[whole((words, 512), BF), whole((words, 512), F32)]
        + [whole((16, W_ROWS, LANES), BF)] * 2
        + [whole((8, 512), F32)],
        scratch_shapes=word_scratch,
        compiler_params=pltpu.CompilerParams(vmem_limit_bytes=48 << 20),
        cost_estimate=cost(3e9, 16e6),
    )(me, docs, w_in, delta, cot, *parts, gain, shift)


def word_back_kernel(x_first, me, docs, cot, w1, qkv, mixed, w2, hidden, p0, p1, p2, p3, gain, shift, *refs):
    grad_out, keep, send, vectors, upper, down, sems = refs
    fetch_word(x_first, me, (p0, p1, p2, p3), upper, down, sems)
    grad_out[...] = word_backward_body(
        x_first,
        me,
        cot[...],
        w1[...],
        qkv[...],
        mixed[...],
        w2[...],
        hidden[...],
        upper,
        down,
        gain[...],
        shift[...],
        word_allowed(docs, w1.shape[0]),
        keep,
        send,
        vectors,
    )


def word_back(x_first, me, docs, grad, saved, parts, gain, shift):
    words = grad.shape[0]
    return pl.pallas_call(
        partial(word_back_kernel, x_first),
        in_specs=[smem, smem] + [vmem] * 6 + [anywhere] * 4 + [vmem, vmem],
        out_specs=[vmem] * 4,
        out_shape=[whole((words, 512), F32)] + [whole((16, W_ROWS, LANES), BF)] * 2 + [whole((8, 512), F32)],
        scratch_shapes=word_scratch,
        compiler_params=pltpu.CompilerParams(vmem_limit_bytes=48 << 20),
        cost_estimate=cost(2e9, 16e6),
    )(me, docs, grad, *saved, *parts, gain, shift)


def swap(x, axis, flip):
    return lax.ppermute(x, axis, [(k, k ^ flip) for k in range(lax.axis_size(axis))])


def over_x(x):
    return swap(x, "wide", 1)


def over_y(x):
    return swap(x, "narrow", 2)


def over_core(x):
    return swap(x, "narrow", 1)


def gather(block, x_first):
    z = jnp.stack([block] + [swap(block, "wide", 2 * k) for k in (1, 2, 3)])
    one, two = (over_x, over_y) if x_first else (over_y, over_x)
    first = jnp.concatenate([z, one(z)], axis=0)
    second = two(first)
    return first, second, over_core(first), over_core(second)


def add(*terms):
    total = terms[0].astype(F32)
    for term in terms[1:]:
        total = total + term.astype(F32)
    return total


def scatter(keep, send, x_first):
    one, two = (over_x, over_y) if x_first else (over_y, over_x)
    got = over_core(send)
    ours, theirs = (add(keep[k : k + 8], got[k : k + 8]).astype(BF) for k in (0, 8))
    got = two(theirs)
    ours, theirs = (add(ours[k : k + 4], got[k : k + 4]).astype(BF) for k in (0, 4))
    got = one(theirs)
    parts = [add(ours[k], got[k]).astype(BF) for k in range(4)]
    return add(parts[0], *[swap(parts[k], "wide", 2 * k) for k in (1, 2, 3)])


def total(x):
    x = x + over_core(x)
    x = x + over_y(x)
    x = x + over_x(x)
    x = x + swap(x, "wide", 2)
    return x + swap(x, "wide", 4)


def cut(matrices, table):
    qkv, out, up, down, proj, *words = matrices

    def split(m):
        r, c = m.shape
        return m.T.reshape(8, c // 8, 4, r // 4).transpose(0, 2, 1, 3)

    def paired(m):
        b = split(m)
        c = b.shape[2]
        return b.reshape(8, 4, 2, c // 2, 64).transpose(0, 1, 3, 2, 4).reshape(8, 4, c // 2, LANES)

    def tiled(m):
        b = split(m)
        c, r = b.shape[2:]
        return b.reshape(8, 4, c, r // LANES, LANES).transpose(0, 1, 3, 2, 4).reshape(8, 4, -1, LANES)

    char = [paired(qkv), paired(out), paired(up), paired(proj), tiled(down)]
    if table is not None:
        char.append(table.reshape(8, 4, 8, 2, LANES).transpose(0, 1, 3, 2, 4).reshape(8, 4, 16, LANES))
    word = [tiled(m) for m in words]
    return [ordered(jnp.concatenate(x, axis=2)) for x in (char, word)]


def ordered(blocks):
    b = blocks.reshape(4, 2, 2, 2, *blocks.shape[2:]).transpose(3, 2, 1, 0, 4, 5)
    return b.reshape(32, *blocks.shape[2:])


def uncut(blocks, is_char, with_table):
    b = blocks.reshape(2, 2, 2, 4, *blocks.shape[1:]).transpose(3, 2, 1, 0, 4, 5)
    b = b.reshape(8, 4, *blocks.shape[1:])

    def joined(x):
        c, r = x.shape[2:]
        return x.transpose(0, 2, 1, 3).reshape(8 * c, 4 * r).T

    def paired(x):
        c = x.shape[2]
        return joined(x.reshape(8, 4, c, 2, 64).transpose(0, 1, 3, 2, 4).reshape(8, 4, 2 * c, 64))

    def tiled(x, tiles):
        c = x.shape[2] // tiles
        return joined(x.reshape(8, 4, tiles, c, LANES).transpose(0, 1, 3, 2, 4).reshape(8, 4, c, tiles * LANES))

    def rows(span, count=None):
        return b[:, :, span[0] : span[0] + (count or span[1])]

    if not is_char:
        return [tiled(rows(W_QKV), 1), tiled(rows(W_OUT), 1), tiled(rows(W_UP), 1), tiled(rows(W_DOWN, 256), 4)], None
    table = None
    if with_table:
        table = rows(C_EMB).reshape(32, 2, 8, LANES).transpose(0, 2, 1, 3).reshape(256, 256)
    qkv, out, up, proj = (paired(rows(span)) for span in C_PAIRED)
    return [qkv, out, up, tiled(rows(C_DOWN, 64), 2), proj], table


def on_device(direct, *arguments):
    (word_states, character_ids, word_lengths, doc_lengths, embedding) = arguments[:5]
    weights = arguments[5:14]
    char_gains, char_shifts, pool_query, word_gains, word_shifts, char_cot, word_cot = arguments[14:]
    words_count, slots_count = character_ids.shape[1:]
    width = char_cot.shape[3]
    both = ("wide", "narrow")
    firsts = (True, False)
    if direct:
        me = jnp.stack([lax.axis_index("wide"), lax.axis_index("narrow")]).astype(jnp.int32)
        blocks = pack(weights, embedding)
        chars = [gather(blocks[k], firsts[k]) for k in range(2)]
        words = [gather(blocks[2 + k], firsts[k]) for k in range(2)]
    else:
        firsts = (True, True)
        me = jnp.zeros((2,), jnp.int32)
        table = lax.all_gather(embedding, both, axis=0, tiled=True)
        full = [
            lax.all_gather(lax.all_gather(m, "narrow", axis=1, tiled=True), "wide", axis=2, tiled=True) for m in weights
        ]
        chars, words = [], []
        for layer in range(2):
            char, word = cut([m[layer] for m in full], table if layer == 0 else None)
            chars.append([char[8 * k : 8 * k + 8] for k in range(4)])
            words.append([word[8 * k : 8 * k + 8] for k in range(4)])
    ids = character_ids.reshape(-1, LANES)
    source = ids
    char_saved, deltas = [], []
    for layer in range(2):
        out = char_forward(
            layer == 0,
            firsts[layer],
            me,
            word_lengths,
            source,
            chars[layer],
            char_gains[layer],
            char_shifts[layer],
            pool_query[layer : layer + 1],
        )
        if layer == 1:
            out = [source] + list(out)
        *saved, delta = out
        char_saved.append(saved)
        deltas.append(delta)
        source = saved[5]
    *word_saved, w3 = word_first(
        firsts[0], me, doc_lengths, word_states[0], deltas[0], words[0], word_gains[0], word_shifts[0]
    )
    word_out, grad_word, *word_grads_1 = word_last(
        firsts[1], me, doc_lengths, w3, deltas[1], word_cot[0], words[1], word_gains[1], word_shifts[1]
    )
    word_at = [None, grad_word]
    grad_word, *word_grads_0 = word_back(
        firsts[0], me, doc_lengths, grad_word, word_saved, words[0], word_gains[0], word_shifts[0]
    )
    word_at[0] = grad_word
    grad, *char_grads_1 = char_backward(
        False,
        firsts[1],
        me,
        word_lengths,
        None,
        char_cot[0].reshape(-1, width),
        word_at[1],
        char_saved[1],
        chars[1],
        char_gains[1],
        char_shifts[1],
        pool_query[1:2],
    )
    char_grads_0 = char_backward(
        True,
        firsts[0],
        me,
        word_lengths,
        ids,
        grad,
        word_at[0],
        char_saved[0],
        chars[0],
        char_gains[0],
        char_shifts[0],
        pool_query[0:1],
    )
    vectors = jnp.concatenate(
        [x.reshape(-1, LANES) for x in (word_grads_0[2], word_grads_1[2], char_grads_0[2], char_grads_1[2])], axis=0
    )
    pieces = ((char_grads_0, firsts[0]), (char_grads_1, firsts[1]), (word_grads_0, firsts[0]), (word_grads_1, firsts[1]))
    if direct:
        vectors = total(vectors)
        summed = [scatter(g[0], g[1], first) for g, first in pieces]
        *matrix_grads, embedding_grad = unpack(summed, weights, embedding)
    else:
        vectors = lax.psum(vectors, both)
        full = [uncut(jnp.concatenate(g[:2]), k < 2, k == 0) for k, (g, _) in enumerate(pieces)]
        matrix_grads = [
            lax.psum_scatter(
                lax.psum_scatter(jnp.stack([a, b]), "wide", scatter_dimension=2, tiled=True),
                "narrow",
                scatter_dimension=1,
                tiled=True,
            ).astype(F32)
            for a, b in zip(full[0][0] + full[2][0], full[1][0] + full[3][0])
        ]
        embedding_grad = lax.psum_scatter(full[0][1].astype(F32), both, scatter_dimension=0, tiled=True)
    word_vectors = vectors[:64].reshape(2, 8, 512)
    char_vectors = vectors[64:].reshape(2, 8, 256)
    return (
        source.astype(BF).reshape(1, words_count, slots_count, width),
        word_out[None],
        grad_word[None],
        embedding_grad,
        *matrix_grads,
        char_vectors[:, 0:2],
        char_vectors[:, 2:4],
        char_vectors[:, 4],
        word_vectors[:, 0:2],
        word_vectors[:, 2:4],
    )


def solution(mesh):
    rows = ("wide", "narrow")
    matrix = P(None, "narrow", "wide")
    by_rows = P(rows)
    return jax.shard_map(
        partial(on_device, mesh.shape["wide"] == 8 and mesh.shape["narrow"] == 4),
        mesh=mesh,
        in_specs=(by_rows,) * 5 + (matrix,) * 9 + (P(),) * 5 + (by_rows,) * 2,
        out_specs=(by_rows,) * 4 + (matrix,) * 9 + (P(),) * 5,
        check_vma=False,
    )
```

```python
from functools import partial

import jax
import jax.numpy as jnp
from jax import lax
from jax.experimental import pallas as pl
from jax.experimental.pallas import tpu as pltpu
from jax.sharding import PartitionSpec as P

F32 = jnp.float32
BF = jnp.bfloat16
SLOTS = 16
masked_score = -1e30
ROOT = 0.7978845608028654
CUBE = 0.044715
LANES = 128
C_QKV, C_OUT, C_UP, C_PROJ, C_DOWN, C_EMB = (0, 48), (48, 16), (64, 64), (128, 32), (160, 32), (224, 16)
C_PAIRED = (C_QKV, C_OUT, C_UP, C_PROJ)
C_ROWS = 224
W_QKV, W_OUT, W_UP, W_DOWN = (0, 192), (192, 64), (256, 256), (512, 64)
W_ROWS = 768
BLOCK = 256
VMEM = 56 << 20


def dot(left, right, l, r):
    return lax.dot_general(left, right, (((l,), (r,)), ((), ())), preferred_element_type=F32)


def nn(left, right):
    return dot(left, right, 1, 0)


def nt(left, right):
    return dot(left, right, 1, 1)


def tn(left, right):
    return dot(left, right, 0, 0)


def iota(shape, dim):
    return lax.broadcasted_iota(jnp.int32, shape, dim)


def norm_parts(states):
    centre = states - jnp.mean(states, axis=-1, keepdims=True)
    spread = jnp.mean(centre * centre, axis=-1, keepdims=True)
    root = lax.rsqrt(spread + 1e-05)
    return centre * root, root


def norm_back(grad, hat, root, gain):
    scaled = grad * gain
    inner = scaled - jnp.mean(scaled, axis=-1, keepdims=True)
    back = root * (inner - hat * jnp.mean(scaled * hat, axis=-1, keepdims=True))
    return back, jnp.sum(grad * hat, axis=0, keepdims=True), jnp.sum(grad, axis=0, keepdims=True)


def gelu_value(h):
    return 0.5 * h * (1.0 + jnp.tanh(ROOT * (h + CUBE * h * h * h)))


def gelu_both(h):
    square = h * h
    t = jnp.tanh(ROOT * (h + CUBE * square * h))
    half = 0.5 * (1.0 + t)
    slope = half + 0.5 * h * (1.0 - t * t) * (ROOT * (1.0 + 3.0 * CUBE * square))
    return h * half, slope


def softmax_rows(scores):
    shifted = jnp.exp(scores - jnp.max(scores, axis=-1, keepdims=True))
    return shifted / jnp.sum(shifted, axis=-1, keepdims=True)


def low_half(shape):
    return iota(shape, len(shape) - 1) % LANES < 64


def two_heads(x):
    low = low_half(x.shape)
    zero = jnp.zeros_like(x)
    return jnp.concatenate([jnp.where(low, x, zero), jnp.where(low, zero, x)], axis=0)


def join_heads(x):
    k = x.shape[0] // 2
    return jnp.where(low_half((k, LANES)), x[:k], x[k:])


def place(rw, ry, x_first):
    rx, rz = rw & 1, rw >> 1
    return ry * 8 + rx * 4 + rz if x_first else rx * 8 + ry * 4 + rz


def unplace(q, s, x_first):
    a, rz = s >> 2, s & 3
    rx, ry = (a, q) if x_first else (q, a)
    return rz * 2 + rx, ry


def pack_kernel(me, cq, co, cu, cd, cp, wq, wo, wu, wd, emb, c0, c1, mine, theirs):
    def turned(x):
        return x.astype(F32).T

    for layer, c in enumerate((c0, c1)):
        for t, (row, rows) in zip((turned(cq[layer]), co[layer], turned(cu[layer]), turned(cp[layer])), C_PAIRED):
            t = t.astype(F32)
            c[row : row + rows, :] = jnp.concatenate([t[:rows, :64], t[rows:, :64]], axis=1).astype(BF)
        for k in range(2):
            row = C_DOWN[0] + 32 * k
            c[row : row + 32, :] = cd[layer, :, k * LANES : (k + 1) * LANES]
    e = emb[...].astype(F32)
    c0[C_EMB[0] : C_EMB[0] + 16, :] = jnp.concatenate([e[:, :LANES], e[:, LANES:]], axis=0).astype(BF)
    for layer, w in ((me[2], mine), (1 - me[2], theirs)):
        w[W_QKV[0] : W_QKV[0] + 192, :] = wq[layer]
        w[W_OUT[0] : W_OUT[0] + 64, :] = wo[layer]
        w[W_UP[0] : W_UP[0] + 256, :] = turned(wu[layer]).astype(BF)
        for k in range(4):
            row = W_DOWN[0] + 64 * k
            w[row : row + 64, :] = wd[layer, :, k * LANES : (k + 1) * LANES]


def whole(shape, dtype):
    return jax.ShapeDtypeStruct(shape, dtype)


def cost(flops, moved):
    return pl.CostEstimate(flops=int(flops), bytes_accessed=int(moved), transcendentals=0)


smem = pl.BlockSpec(memory_space=pltpu.SMEM)
vmem = pl.BlockSpec(memory_space=pltpu.VMEM)
anywhere = pl.BlockSpec(memory_space=pl.ANY)
TURNED = (1, 3, 5, 6, 8)


def pack(me, weights, embedding):
    weights = [m.swapaxes(1, 2) if k in TURNED else m for k, m in enumerate(weights)]
    return pl.pallas_call(
        pack_kernel,
        in_specs=[smem] + [vmem] * 10,
        out_shape=(
            whole((C_ROWS + 16, LANES), BF),
            whole((C_ROWS, LANES), BF),
            whole((W_ROWS, LANES), BF),
            whole((W_ROWS, LANES), BF),
        ),
        cost_estimate=cost(0, 4e6),
    )(me, *weights, embedding)


def split_vector(x):
    high = x.astype(BF)
    return jnp.concatenate([high, (x - high.astype(F32)).astype(BF)], axis=0)


def whole_vector(x):
    return x[:96].astype(F32) + x[96:192].astype(F32)


def unpack_kernel(me, *refs):
    first, second, own_word, other_word, own_out, other_out = refs[:5], refs[5:9], *refs[9:13]
    cq, co, cu, cd, cp, wq, wo, wu, wd, emb, cg, cs, pq, wg, ws, word_out = refs[13:]
    layer_now = me[2]
    word_out[...] = jnp.where(layer_now == 1, own_out[...], other_out[...])
    c0 = (first[0][0].astype(F32) + first[2][0].astype(F32)) + (first[3][0].astype(F32) + first[4][0].astype(F32))
    c1 = (second[0][...].astype(F32) + second[1][...].astype(F32)) + (
        second[2][...].astype(F32) + second[3][...].astype(F32)
    )
    v = (whole_vector(first[1][1]) + whole_vector(first[2][1])) + (
        whole_vector(first[3][1]) + whole_vector(first[4][1])
    )
    for layer, c in enumerate((c0, c1)):
        for k, ref, (row, rows) in zip((0, 1, 2, 4), (cq, co, cu, cp), C_PAIRED):
            t = c[row : row + rows, :]
            t = jnp.concatenate([t[:, :64], t[:, 64:]], axis=0)
            ref[layer] = t if k in TURNED else t.T
        for k in range(2):
            row = C_DOWN[0] + 32 * k
            cd[layer, :, k * LANES : (k + 1) * LANES] = c[row : row + 32, :]
        for t in range(4):
            row = 32 * layer + 8 * t
            wg[layer, :, t * LANES : (t + 1) * LANES] = v[row : row + 2]
            ws[layer, :, t * LANES : (t + 1) * LANES] = v[row + 2 : row + 4]
        for t in range(2):
            row = 64 + 16 * layer + 8 * t
            cg[layer, :, t * LANES : (t + 1) * LANES] = v[row : row + 2]
            cs[layer, :, t * LANES : (t + 1) * LANES] = v[row + 2 : row + 4]
            pq[layer : layer + 1, t * LANES : (t + 1) * LANES] = v[row + 4 : row + 5]
    e = c0[C_EMB[0] : C_EMB[0] + 16, :]
    emb[...] = jnp.concatenate([e[:8], e[8:]], axis=1)
    for layer, w in ((layer_now, own_word), (1 - layer_now, other_word)):
        wq[layer] = w[0, W_QKV[0] : W_QKV[0] + 192, :].astype(F32)
        wo[layer] = w[0, W_OUT[0] : W_OUT[0] + 64, :].astype(F32)
        wu[layer] = w[0, W_UP[0] : W_UP[0] + 256, :].astype(F32).T
        for k in range(4):
            row = W_DOWN[0] + 64 * k
            wd[layer, :, k * LANES : (k + 1) * LANES] = w[0, row : row + 64, :].astype(F32)


def unpack(me, blocks, weights, embedding, vectors):
    shapes = [m.shape for m in weights]
    shapes = [(a, c, b) if k in TURNED else (a, b, c) for k, (a, b, c) in enumerate(shapes)]
    shapes += [embedding.shape] + [v.shape for v in vectors]
    out = pl.pallas_call(
        unpack_kernel,
        in_specs=[smem] + [vmem] * len(blocks),
        out_shape=tuple(whole(x, F32) for x in shapes) + (whole(blocks[-1].shape, BF),),
        cost_estimate=cost(0, 8e6),
    )(me, *blocks)
    return [x.swapaxes(1, 2) if k in TURNED else x for k, x in enumerate(out)]


def fold_kernel(count, keep, got, own, ours, *theirs):
    half = count // 2 if len(theirs) == 1 else 1
    for k in range(half):
        ours[k] = (keep[k].astype(F32) + got[k].astype(F32)).astype(BF)
    vector = split_vector(whole_vector(own[0]) + whole_vector(got[count]))
    rest = jnp.zeros((own.shape[1] - vector.shape[0], LANES), BF)
    if len(theirs) == 1:
        for k in range(half):
            theirs[0][k] = (keep[half + k].astype(F32) + got[half + k].astype(F32)).astype(BF)
    else:
        for k, ref in enumerate(theirs):
            ref[0] = (keep[1 + k].astype(F32) + got[1 + k].astype(F32)).astype(BF)
    for ref in theirs:
        ref[half, 0:192, :] = vector
        ref[half, 192:, :] = rest


def fold(keep, got, own, last):
    count, rows = keep.shape[:2]
    if last:
        shapes = [1, 2, 2, 2]
    else:
        shapes = [count // 2, count // 2 + 1]
    at = own.shape[0] - 1
    return pl.pallas_call(
        partial(fold_kernel, count),
        grid=(1,),
        in_specs=[
            pl.BlockSpec(keep.shape, lambda i: (0, 0, 0)),
            pl.BlockSpec(got.shape, lambda i: (0, 0, 0)),
            pl.BlockSpec((1, rows, LANES), lambda i: (at, 0, 0)),
        ],
        out_specs=[pl.BlockSpec((k, rows, LANES), lambda i: (0, 0, 0)) for k in shapes],
        out_shape=[whole((k, rows, LANES), BF) for k in shapes],
        cost_estimate=cost(0, 2e6),
    )(keep, got, own)


def fetch_char(x_first, me, parts, raw, mats, table, sems):
    copies = [
        pltpu.make_async_copy(part, raw.at[pl.ds(8 * k, 8)], sems.at[k]) for k, part in enumerate(parts)
    ]
    for copy in copies:
        copy.start()
    for copy in copies:
        copy.wait()
    mw, my, mc = me[0], me[1] >> 1, me[1] & 1
    for w in range(8):
        for y in range(2):
            at = place(w ^ mw, y ^ my, x_first)
            cores = (mc * 16 + at, (1 - mc) * 16 + at)
            for ref, (row, rows) in zip(mats[:4], C_PAIRED):
                zero, one = (raw[k, row : row + rows, :] for k in cores)
                first = w * 2 * rows
                columns = slice(y * LANES, (y + 1) * LANES)
                ref[first : first + rows, columns] = jnp.concatenate([zero[:, :64], one[:, :64]], axis=1)
                ref[first + rows : first + 2 * rows, columns] = jnp.concatenate(
                    [zero[:, 64:], one[:, 64:]], axis=1
                )
            for c, k in enumerate(cores):
                for t in range(2):
                    column = (2 * y + c) * 256 + t * LANES
                    row = C_DOWN[0] + 32 * t
                    mats[4][w * 32 : w * 32 + 32, column : column + LANES] = raw[k, row : row + 32, :]
    if table is not None:
        for k in range(32):
            table[k * 16 : k * 16 + 16, :] = raw[k, C_EMB[0] : C_EMB[0] + 16, :]


def char_positions(ids, me, x_first):
    device = ids >> 3
    rw = (device >> 2) ^ me[0]
    rn = (device & 3) ^ me[1]
    return ((rn & 1) * 16 + place(rw, rn >> 1, x_first)) * 16 + (ids & 7)


def valid_keys(lens, first):
    lane = iota((1, LANES), 1)
    length = jnp.zeros((1, LANES), jnp.int32)
    for k in range(8):
        length = jnp.where(lane // SLOTS == k, lens[0, first + k], length)
    return lane % SLOTS < length


def to_column(row):
    square = (LANES, LANES)
    return jnp.sum(jnp.where(iota(square, 0) == iota(square, 1), row, 0.0), axis=-1, keepdims=True)


def char_attend(q, keys, allowed):
    scores = nt(q, keys) * 0.125
    scores = jnp.where(allowed, scores, masked_score)
    return jnp.concatenate([softmax_rows(scores[:, :LANES]), softmax_rows(scores[:, LANES:])], axis=1)


def char_masks(lens, block):
    out = []
    same = iota((LANES, LANES), 0) // SLOTS == iota((LANES, LANES), 1) // SLOTS
    for half in range(2):
        valid = valid_keys(lens, block * 16 + half * 8)
        pair = same & valid
        out.append((jnp.concatenate([pair, pair], axis=1), to_column(jnp.where(valid, 1.0, 0.0))))
    return out


def pool_weights(states, query, valid):
    scores = jnp.sum(states * query, axis=-1, keepdims=True)
    scores = jnp.where(valid > 0.5, scores, masked_score).reshape(16, SLOTS, 1)
    shifted = jnp.exp(scores - jnp.max(scores, axis=1, keepdims=True))
    return shifted / jnp.sum(shifted, axis=1, keepdims=True)


def of_layer(first, gain, shift, query):
    layer = 0 if first else 1
    return gain[layer], shift[layer], query[layer : layer + 1, :]


def char_forward_kernel(first, x_first, *refs):
    me, lens, source, p0, p1, p2, p3, gain, shift, query = refs[:10]
    refs = refs[10:]
    if first:
        x_out, refs = refs[0], refs[1:]
    qkv_out, mixed_out, after_out, hidden_out, next_out, pooled_out, delta_out = refs[:7]
    refs = refs[7:]
    if not first:
        low_out, refs = refs[0], refs[1:]
    raw, m_qkv, m_out, m_up, m_proj, m_down, table, sems = refs
    block = pl.program_id(0)
    gain, shift, query = of_layer(first, gain, shift, query)

    @pl.when(block == 0)
    def _():
        fetch_char(
            x_first, me, (p0, p1, p2, p3), raw, (m_qkv, m_out, m_up, m_proj, m_down), table if first else None, sems
        )

    if first:
        parts = []
        for half in range(2):
            ids = source[pl.ds(block * 2 + half, 1), :]
            column = to_column(char_positions(ids, me, x_first).astype(F32)).astype(jnp.int32)
            lane = iota((LANES, 512), 1)
            left = jnp.where(lane == column, 1.0, 0.0).astype(BF)
            right = jnp.where(lane == column + 8, 1.0, 0.0).astype(BF)
            parts.append(jnp.concatenate([nn(left, table[...]), nn(right, table[...])], axis=1))
        x = jnp.concatenate(parts, axis=0)
        x_out[...] = x
    else:
        x = source[...]
    hat, _ = norm_parts(x)
    normed = (hat * gain[0:1] + shift[0:1]).astype(BF)
    qkv = nt(normed, m_qkv[...]).astype(BF)
    qkv_out[...] = qkv
    masks = char_masks(lens, block)
    halves = []
    for half in range(2):
        rows = slice(half * LANES, (half + 1) * LANES)
        pairs = []
        for pair in range(2):
            q, k, v = (qkv[rows, t * 256 + pair * LANES : t * 256 + (pair + 1) * LANES] for t in range(3))
            attend = char_attend(q, two_heads(k), masks[half][0])
            pairs.append(nn(attend.astype(BF), two_heads(v)))
        halves.append(jnp.concatenate(pairs, axis=1))
    mixed = jnp.concatenate(halves, axis=0).astype(BF)
    mixed_out[...] = mixed
    after = x + nt(mixed, m_out[...])
    after_out[...] = after
    hat, _ = norm_parts(after)
    normed = (hat * gain[1:2] + shift[1:2]).astype(BF)
    hidden = nt(normed, m_up[...])
    hidden_out[...] = hidden
    states = after + nt(gelu_value(hidden).astype(BF), m_down[...])
    next_out[...] = states
    if not first:
        low_out[...] = states.astype(BF)
    valid = jnp.concatenate([masks[0][1], masks[1][1]], axis=0)
    weights = pool_weights(states, query, valid)
    pooled = jnp.sum(weights * states.reshape(16, SLOTS, 256), axis=1).astype(BF)
    pooled_out[...] = pooled
    delta_out[...] = nt(pooled, m_proj[...])


def char_scratch(first):
    rows = C_ROWS + (16 if first else 0)
    return [
        pltpu.VMEM((32, rows, LANES), BF),
        pltpu.VMEM((768, 256), BF),
        pltpu.VMEM((256, 256), BF),
        pltpu.VMEM((1024, 256), BF),
        pltpu.VMEM((512, 256), BF),
        pltpu.VMEM((256, 1024), BF),
    ]


def rows_spec(rows, columns):
    return pl.BlockSpec((rows, columns), lambda i: (i, 0))


def fixed_spec(shape):
    return pl.BlockSpec(shape, lambda i: (0,) * len(shape))


def char_forward(first, x_first, me, lens, source, parts, gain, shift, query):
    rows = lens.shape[1] * SLOTS
    grid = rows // BLOCK
    shapes = [(768, BF), (256, BF), (256, F32), (1024, F32), (256, F32)]
    if first:
        shapes = [(256, F32)] + shapes
    out = [(rows, BLOCK, c, t) for c, t in shapes]
    out += [(rows // SLOTS, BLOCK // SLOTS, 256, BF), (rows // SLOTS, BLOCK // SLOTS, 512, F32)]
    if not first:
        out += [(rows, BLOCK, 256, BF)]
    return pl.pallas_call(
        partial(char_forward_kernel, first, x_first),
        grid=(grid,),
        in_specs=[smem, smem, fixed_spec(source.shape) if first else rows_spec(BLOCK, 256)]
        + [anywhere] * 4
        + [fixed_spec((2, 2, 256)), fixed_spec((2, 2, 256)), fixed_spec((2, 256))],
        out_specs=[rows_spec(b, c) for _, b, c, _ in out],
        out_shape=[whole((r, c), t) for r, _, c, t in out],
        scratch_shapes=char_scratch(first)
        + [pltpu.VMEM((512, LANES) if first else (16, LANES), BF), pltpu.SemaphoreType.DMA((4,))],
        compiler_params=pltpu.CompilerParams(vmem_limit_bytes=VMEM),
        cost_estimate=cost(2e9, 14e6),
    )(me, lens, source, *parts, gain, shift, query)


def pool_back(states, query, valid, grad):
    weights = pool_weights(states, query, valid)
    cube = states.reshape(16, SLOTS, 256)
    wide = grad.reshape(16, 1, 256)
    by_weight = jnp.sum(cube * wide, axis=-1, keepdims=True)
    by_score = weights * (by_weight - jnp.sum(weights * by_weight, axis=1, keepdims=True))
    added = weights * wide + by_score * query.reshape(1, 1, 256)
    by_query = jnp.sum((by_score * cube).reshape(256, 256), axis=0, keepdims=True)
    return added.reshape(256, 256), by_query


def char_backward_kernel(first, x_first, *refs):
    me, lens = refs[:2]
    refs = refs[2:]
    if first:
        ids, refs = refs[0], refs[1:]
    (grad_in, word_own, word_other, x_in, qkv_in, mixed_in, after_in, hidden_in, next_in, pooled_in) = refs[:10]
    p0, p1, p2, p3, gain, shift, query = refs[10:17]
    refs = refs[17:]
    gain, shift, query = of_layer(first, gain, shift, query)
    if first:
        word_0, word_1, char_1, word_out, keep, send, vectors = refs[:7]
        refs = refs[7:]
    else:
        grad_out, keep, send, vectors = refs[:4]
        refs = refs[4:]
    raw, m_qkv, m_out, m_up, m_proj, m_down, a_qkv, a_out, a_up, a_proj, a_down, a_table, sems = refs
    block = pl.program_id(0)

    @pl.when(block == 0)
    def _():
        fetch_char(x_first, me, (p0, p1, p2, p3), raw, (m_qkv, m_out, m_up, m_proj, m_down), None, sems)
        for ref in (a_qkv, a_out, a_up, a_proj, a_down, a_table, vectors):
            ref[...] = jnp.zeros(ref.shape, ref.dtype)

    masks = char_masks(lens, block)
    word_grad = jnp.where(me[2] == (0 if first else 1), word_own[...], word_other[...])
    if first:
        word_out[...] = word_grad
    low_word = word_grad.astype(BF)
    a_proj[...] += tn(low_word, pooled_in[...])
    grad_pooled = nn(low_word, m_proj[...])
    valid = jnp.concatenate([masks[0][1], masks[1][1]], axis=0)
    added, by_query = pool_back(next_in[...], query, valid, grad_pooled)
    grad = grad_in[...].astype(F32) + added
    vectors[4:5, :] += by_query
    low = grad.astype(BF)
    act, slope = gelu_both(hidden_in[...])
    a_down[...] += tn(low, act.astype(BF))
    by_hidden = (slope * nn(low, m_down[...])).astype(BF)
    hat, root = norm_parts(after_in[...])
    normed = (hat * gain[1:2] + shift[1:2]).astype(BF)
    a_up[...] += tn(normed, by_hidden)
    back, by_gain, by_shift = norm_back(nn(by_hidden, m_up[...]), hat, root, gain[1:2])
    grad = grad + back
    vectors[1:2, :] += by_gain
    vectors[3:4, :] += by_shift
    low = grad.astype(BF)
    a_out[...] += tn(low, mixed_in[...])
    by_mixed = nn(low, m_out[...]).astype(BF)
    sides = []
    for half in range(2):
        rows = slice(half * LANES, (half + 1) * LANES)
        by_q, by_k, by_v = [], [], []
        for pair in range(2):
            q, k, v = (qkv_in[rows, t * 256 + pair * LANES : t * 256 + (pair + 1) * LANES] for t in range(3))
            keys = two_heads(k)
            attend = char_attend(q, keys, masks[half][0])
            g = by_mixed[rows, pair * LANES : (pair + 1) * LANES]
            by_attend = nt(g, two_heads(v))
            product = attend * by_attend
            inner = jnp.concatenate(
                [
                    jnp.broadcast_to(jnp.sum(product[:, h : h + LANES], axis=-1, keepdims=True), (LANES, LANES))
                    for h in (0, LANES)
                ],
                axis=1,
            )
            by_scores = (product - attend * inner).astype(BF)
            by_v.append(join_heads(tn(attend.astype(BF), g)))
            by_q.append(nn(by_scores, keys) * 0.125)
            by_k.append(join_heads(tn(by_scores, q)) * 0.125)
        sides.append(jnp.concatenate(by_q + by_k + by_v, axis=1))
    by_qkv = jnp.concatenate(sides, axis=0).astype(BF)
    hat, root = norm_parts(x_in[...])
    normed = (hat * gain[0:1] + shift[0:1]).astype(BF)
    a_qkv[...] += tn(normed, by_qkv)
    back, by_gain, by_shift = norm_back(nn(by_qkv, m_qkv[...]), hat, root, gain[0:1])
    grad = grad + back
    vectors[0:1, :] += by_gain
    vectors[2:3, :] += by_shift
    if first:
        for half in range(2):
            at = char_positions(ids[pl.ds(block * 2 + half, 1), :], me, x_first)
            row = iota((512, LANES), 0)
            part = grad[half * LANES : (half + 1) * LANES]
            high = part.astype(BF)
            rest = (part - high.astype(F32)).astype(BF)
            both = jnp.concatenate([high, rest], axis=0)
            for side in range(2):
                hot = jnp.where(row == at + 8 * side, 1.0, 0.0).astype(BF)
                hot = jnp.concatenate([hot, hot], axis=1)
                a_table[...] += nn(hot, both[:, side * LANES : (side + 1) * LANES])
    else:
        grad_out[...] = grad

    @pl.when(block == pl.num_programs(0) - 1)
    def _():
        mw, my, mc = me[0], me[1] >> 1, me[1] & 1
        for ref, turn in ((a_qkv, m_qkv), (a_up, m_up)):
            turn[...] = ref[...].T.astype(BF)
        for ref, to in ((a_out, m_out), (a_proj, m_proj), (a_down, m_down)):
            to[...] = ref[...].astype(BF)

        def put(at, row, rows, zero, one):
            keep[at, row : row + rows, :] = jnp.where(mc == 0, zero, one)
            send[at, row : row + rows, :] = jnp.where(mc == 0, one, zero)

        for w in range(8):
            for y in range(2):
                at = place(w ^ mw, y ^ my, x_first)
                for ref, (row, rows) in zip((m_qkv, m_out, m_up, m_proj), C_PAIRED):
                    columns = slice(y * LANES, (y + 1) * LANES)
                    top = ref[w * 2 * rows : w * 2 * rows + rows, columns]
                    bottom = ref[w * 2 * rows + rows : w * 2 * rows + 2 * rows, columns]
                    put(
                        at,
                        row,
                        rows,
                        jnp.concatenate([top[:, :64], bottom[:, :64]], axis=1),
                        jnp.concatenate([top[:, 64:], bottom[:, 64:]], axis=1),
                    )
                for t in range(2):
                    zero, one = (
                        m_down[w * 32 : w * 32 + 32, (2 * y + c) * 256 + t * LANES : (2 * y + c) * 256 + (t + 1) * LANES]
                        for c in range(2)
                    )
                    put(at, C_DOWN[0] + 32 * t, 32, zero, one)
        if first:
            for k in range(16):
                keep[k, C_EMB[0] : C_EMB[0] + 16, :] = a_table[k * 16 : k * 16 + 16, :].astype(BF)
                send[k, C_EMB[0] : C_EMB[0] + 16, :] = a_table[256 + k * 16 : 272 + k * 16, :].astype(BF)
            tiles = [
                ref[:, t * LANES : (t + 1) * LANES]
                for ref in (word_0, word_1, vectors, char_1)
                for t in range(ref.shape[1] // LANES)
            ]
            send[16, 0:192, :] = split_vector(jnp.concatenate(tiles, axis=0))
            send[16, 192:, :] = jnp.zeros((48, LANES), BF)


def char_backward(first, x_first, me, lens, ids, grad, words, at, saved, parts, gain, shift, query, others):
    x, qkv, mixed, after, hidden, states, pooled = saved
    rows = x.shape[0]
    grid = rows // BLOCK
    held = C_ROWS + (16 if first else 0)
    operands = [me, lens] + ([ids] if first else [])
    specs = [smem, smem] + ([fixed_spec(ids.shape)] if first else [])
    if first:
        outs, out_specs = [whole((rows // SLOTS, 512), F32)], [rows_spec(BLOCK // SLOTS, 512)]
    else:
        outs, out_specs = [whole((rows, 256), F32)], [rows_spec(BLOCK, 256)]
    sends = 17 if first else 16
    half = BLOCK // SLOTS
    return pl.pallas_call(
        partial(char_backward_kernel, first, x_first),
        grid=(grid,),
        in_specs=specs
        + [
            rows_spec(BLOCK, 256),
            *[pl.BlockSpec((half, 512), lambda i, k=k: (k * grid + i, 0)) for k in at],
            rows_spec(BLOCK, 256),
            rows_spec(BLOCK, 768),
            rows_spec(BLOCK, 256),
            rows_spec(BLOCK, 256),
            rows_spec(BLOCK, 1024),
            rows_spec(BLOCK, 256),
            rows_spec(BLOCK // SLOTS, 256),
        ]
        + [anywhere] * 4
        + [fixed_spec((2, 2, 256)), fixed_spec((2, 2, 256)), fixed_spec((2, 256))]
        + [fixed_spec(x.shape) for x in others],
        out_specs=out_specs
        + [fixed_spec((16, held, LANES)), fixed_spec((sends, held, LANES))]
        + [fixed_spec((8, 256))],
        out_shape=outs
        + [whole((16, held, LANES), BF), whole((sends, held, LANES), BF)]
        + [whole((8, 256), F32)],
        scratch_shapes=char_scratch(first)
        + [
            pltpu.VMEM((256, 768), F32),
            pltpu.VMEM((256, 256), F32),
            pltpu.VMEM((256, 1024), F32),
            pltpu.VMEM((512, 256), F32),
            pltpu.VMEM((256, 1024), F32),
            pltpu.VMEM((512 if first else 8, LANES), F32),
            pltpu.SemaphoreType.DMA((4,)),
        ],
        compiler_params=pltpu.CompilerParams(vmem_limit_bytes=VMEM),
        cost_estimate=cost(4e9, 24e6),
    )(*operands, grad, *words, x, qkv, mixed, after, hidden, states, pooled, *parts, gain, shift, query, *others)


def fetch_word(firsts, me, parts, upper, down, sems):
    pieces = (
        ((0, 192, 0, 192, 0), (192, 64, 1536, 64, 0), (256, 128, 2048, 256, 0)),
        ((0, 128, 2048, 256, 128),),
    )
    for part in range(2):
        for k in range(4):
            rc, q = k >> 1, k & 1

            def one(s, _, ref=parts[4 * part + k], part=part, rc=rc, q=q):
                rw, ry = unplace(q, s, firsts[part])
                w, n = rw ^ me[0], (ry * 2 + rc) ^ me[1]
                block = ref.at[s]
                column = pl.ds(pl.multiple_of(n * LANES, LANES), LANES)
                for row, rows, base, stride, shift in pieces[part]:
                    to = pl.ds(pl.multiple_of(base + w * stride + shift, 64), rows)
                    pltpu.make_async_copy(block.at[pl.ds(row, rows)], upper.at[to, column], sems.at[0]).start()
                if part == 1:
                    for t in range(4):
                        column = pl.ds(pl.multiple_of(n * 512 + t * LANES, LANES), LANES)
                        to = pl.ds(pl.multiple_of(w * 64, 64), 64)
                        pltpu.make_async_copy(
                            block.at[pl.ds(128 + 64 * t, 64)], down.at[to, column], sems.at[1]
                        ).start()
                return 0

            lax.fori_loop(0, 8, one, 0)
    pltpu.make_async_copy(upper, upper, sems.at[0]).wait()
    pltpu.make_async_copy(down, down, sems.at[1]).wait()


def word_allowed(docs, words):
    shape = (words, 2 * words)
    i, j = iota(shape, 0), iota(shape, 1) % words
    end = 0
    of_i, of_j = jnp.zeros(shape, jnp.int32), jnp.zeros(shape, jnp.int32)
    for k in range(docs.shape[1]):
        end = end + docs[0, k]
        of_i = of_i + (i >= end).astype(jnp.int32)
        of_j = of_j + (j >= end).astype(jnp.int32)
    return (of_i == of_j) & (j <= i)


def by_half(x, reduce, fill):
    low = low_half(x.shape)
    left = reduce(jnp.where(low, x, fill), axis=-1, keepdims=True)
    right = reduce(jnp.where(low, fill, x), axis=-1, keepdims=True)
    return jnp.where(low, left, right)


def word_attend(q, keys, allowed):
    scores = jnp.where(allowed, nt(q, keys) * 0.125, masked_score)
    shifted = jnp.exp(scores - by_half(scores, jnp.max, 2 * masked_score))
    return shifted / by_half(shifted, jnp.sum, 0.0)


def word_forward_body(w1, upper, down, gain, shift, allowed):
    hat, root = norm_parts(w1)
    normed = (hat * gain[0:1] + shift[0:1]).astype(BF)
    qkv = nt(normed, upper[0:1536, :]).astype(BF)
    rows = w1.shape[0] // len(allowed)
    mixed = []
    for r, pairs in enumerate(allowed):
        heads = []
        for pair in range(4):
            q, k, v = word_heads(qkv, r * rows, rows, pair)
            attend = word_attend(q, two_heads(k), pairs)
            heads.append(nn(attend.astype(BF), two_heads(v)))
        mixed.append(jnp.concatenate(heads, axis=1))
    mixed = jnp.concatenate(mixed, axis=0).astype(BF)
    w2 = w1 + nt(mixed, upper[1536:2048, :])
    hat, root = norm_parts(w2)
    normed = (hat * gain[1:2] + shift[1:2]).astype(BF)
    hidden = nt(normed, upper[2048:4096, :])
    w3 = w2 + nt(gelu_value(hidden).astype(BF), down[...])
    return qkv, mixed, w2, hidden, w3


def word_heads(qkv, row, rows, pair):
    return (qkv[row : row + rows, t * 512 + pair * LANES : t * 512 + (pair + 1) * LANES] for t in range(3))


def word_backward_body(firsts, me, grad, w1, qkv, mixed, w2, hidden, upper, down, gain, shift, allowed, keep, send, vectors):
    mw, my, mc = me[0], me[1] >> 1, me[1] & 1

    def put(w, row, rows, blocks):
        for y in range(2):
            at = place(w ^ mw, y ^ my, firsts[row // 384])
            zero, one = blocks(2 * y), blocks(2 * y + 1)
            keep[at, row : row + rows, :] = jnp.where(mc == 0, zero, one)
            send[at, row : row + rows, :] = jnp.where(mc == 0, one, zero)

    low = grad.astype(BF)
    act, slope = gelu_both(hidden)
    act = act.astype(BF)
    for pair in range(4):
        part = tn(low[:, pair * LANES : (pair + 1) * LANES], act).astype(BF)
        for k in range(2):
            for t in range(4):
                put(
                    2 * pair + k,
                    W_DOWN[0] + 64 * t,
                    64,
                    lambda n: part[k * 64 : k * 64 + 64, n * 512 + t * LANES : n * 512 + (t + 1) * LANES],
                )
    by_hidden = (slope * nn(low, down[...])).astype(BF)
    hat, root = norm_parts(w2)
    normed = (hat * gain[1:2] + shift[1:2]).astype(BF)
    for w in range(8):
        part = tn(by_hidden[:, w * 256 : (w + 1) * 256], normed).astype(BF)
        for k in range(2):
            put(
                w,
                W_UP[0] + 128 * k,
                128,
                lambda n: part[k * 128 : k * 128 + 128, n * LANES : (n + 1) * LANES],
            )
    back, by_gain, by_shift = norm_back(nn(by_hidden, upper[2048:4096, :]), hat, root, gain[1:2])
    grad = grad + back
    vectors[1:2, :] = by_gain
    vectors[3:4, :] = by_shift
    low = grad.astype(BF)
    for pair in range(4):
        part = tn(low[:, pair * LANES : (pair + 1) * LANES], mixed).astype(BF)
        for k in range(2):
            put(
                2 * pair + k,
                W_OUT[0],
                64,
                lambda n: part[k * 64 : k * 64 + 64, n * LANES : (n + 1) * LANES],
            )
    by_mixed = nn(low, upper[1536:2048, :]).astype(BF)
    rows = w1.shape[0] // len(allowed)
    sides = []
    for r, pairs in enumerate(allowed):
        by_q, by_k, by_v = [], [], []
        for pair in range(4):
            q, k, v = word_heads(qkv, r * rows, rows, pair)
            keys = two_heads(k)
            attend = word_attend(q, keys, pairs)
            g = by_mixed[r * rows : (r + 1) * rows, pair * LANES : (pair + 1) * LANES]
            by_attend = nt(g, two_heads(v))
            product = attend * by_attend
            by_scores = (product - attend * by_half(product, jnp.sum, 0.0)).astype(BF)
            by_v.append(join_heads(tn(attend.astype(BF), g)))
            by_q.append(nn(by_scores, keys) * 0.125)
            by_k.append(join_heads(tn(by_scores, q)) * 0.125)
        sides.append(jnp.concatenate(by_q + by_k + by_v, axis=1))
    by_qkv = jnp.concatenate(sides, axis=0).astype(BF)
    hat, root = norm_parts(w1)
    normed = (hat * gain[0:1] + shift[0:1]).astype(BF)
    for pair in range(4):
        part = tn(by_qkv[:, pair * 384 : (pair + 1) * 384], normed).astype(BF)
        for k in range(2):
            put(
                2 * pair + k,
                W_QKV[0],
                192,
                lambda n: part[k * 192 : (k + 1) * 192, n * LANES : (n + 1) * LANES],
            )
    back, by_gain, by_shift = norm_back(nn(by_qkv, upper[0:1536, :]), hat, root, gain[0:1])
    vectors[0:1, :] = by_gain
    vectors[2:3, :] = by_shift
    return grad + back


def joined(refs):
    return jnp.concatenate([ref[...] for ref in refs], axis=0) if len(refs) > 1 else refs[0][...]


def swapped(x, count):
    half = x.shape[0] // 2
    return jnp.concatenate([x[half:], x[:half]], axis=0) if count == 2 else x


word_scratch = [pltpu.VMEM((4096, 512), BF), pltpu.VMEM((512, 2048), BF), pltpu.SemaphoreType.DMA((4,))]
grad_scratch = [pltpu.VMEM((16, W_ROWS, LANES), BF)] * 2


def word_call(kernel, count, firsts, tables, operands, outs, scratch, flops, alias=None):
    return pl.pallas_call(
        partial(kernel, count, firsts),
        in_specs=[smem] * len(tables) + [anywhere if x.ndim == 3 and x.shape[0] > 2 else vmem for x in operands],
        out_specs=[anywhere if len(shape) == 3 else vmem for shape, _ in outs],
        out_shape=[whole(shape, dtype) for shape, dtype in outs],
        scratch_shapes=scratch,
        input_output_aliases=alias or {},
        compiler_params=pltpu.CompilerParams(vmem_limit_bytes=VMEM),
        cost_estimate=cost(flops, 16e6),
    )(*tables, *operands)


def word_first_kernel(count, firsts, me, *refs):
    docs, states, deltas, parts = refs[:count], refs[count : 2 * count], refs[2 * count : 3 * count], refs[3 * count :]
    gain, shift, w1_out, qkv_out, mixed_out, w2_out, hidden_out, w3_out, upper, down, sems = parts[8:]

    @pl.when(me[2] == 0)
    def _():
        fetch_word(firsts, me, parts[:8], upper, down, sems)
        w1 = jnp.concatenate([a[0].astype(F32) + b[...] for a, b in zip(states, deltas)], axis=0)
        w1_out[...] = w1
        allowed = [word_allowed(d, w1.shape[0] // count) for d in docs]
        qkv, mixed, w2, hidden, w3 = word_forward_body(w1, upper, down, gain[0], shift[0], allowed)
        qkv_out[...] = qkv
        mixed_out[...] = mixed
        w2_out[...] = w2
        hidden_out[...] = hidden
        w3_out[...] = w3

    @pl.when(me[2] != 0)
    def _():
        w3_out[...] = jnp.zeros(w3_out.shape, F32)


def word_first(firsts, me, docs, states, deltas, parts, gain, shift):
    count = len(docs)
    words = count * deltas[0].shape[0]
    shapes = [(512, F32), (1536, BF), (512, BF), (512, F32), (2048, F32), (512, F32)]
    return word_call(
        word_first_kernel,
        count,
        firsts,
        [me, *docs],
        [*states, *deltas, *parts, gain, shift],
        [((words, c), t) for c, t in shapes],
        word_scratch,
        1e9,
    )


def send_out(pairs, sems):
    copies = [pltpu.make_async_copy(a, b, sems.at[2 + k]) for k, (a, b) in enumerate(pairs)]
    for copy in copies:
        copy.start()
    for copy in copies:
        copy.wait()


def word_last_kernel(count, firsts, me, *refs):
    docs, w_in, deltas, cots, parts = refs[:count], refs[count], refs[count + 1 : 2 * count + 1], *[None] * 2
    cots = refs[2 * count + 1 : 3 * count + 1]
    parts = refs[3 * count + 1 :]
    gain, shift, out_own, out_other, grad_out, keep, send, vectors = parts[8:16]
    upper, down, sems, keep_here, send_here = parts[16:]
    vectors[...] = jnp.zeros(vectors.shape, F32)

    @pl.when(me[2] == 1)
    def _():
        fetch_word(firsts, me, parts[:8], upper, down, sems)
        w1 = swapped(w_in[...], count) + joined(deltas)
        rows = w1.shape[0] // count
        allowed = [word_allowed(d, rows) for d in docs]
        gains, shifts = gain[1], shift[1]
        qkv, mixed, w2, hidden, w3 = word_forward_body(w1, upper, down, gains, shifts, allowed)
        out_own[...] = w3[:rows].astype(BF)
        out_other[...] = w3[(count - 1) * rows :].astype(BF)
        grad = jnp.concatenate([c[1].astype(F32) for c in cots], axis=0)
        grad_out[...] = word_backward_body(
            firsts, me, grad, w1, qkv, mixed, w2, hidden, upper, down, gains, shifts, allowed, keep_here, send_here, vectors
        )
        send_out([(send_here, send), (keep_here, keep)], sems)

    @pl.when(me[2] != 1)
    def _():
        for ref in (out_own, out_other, grad_out):
            ref[...] = jnp.zeros(ref.shape, ref.dtype)


def word_last(firsts, me, docs, w_in, deltas, cots, parts, gain, shift):
    count = len(docs)
    words = w_in.shape[0]
    row = words // count
    return word_call(
        word_last_kernel,
        count,
        firsts,
        [me, *docs],
        [w_in, *deltas, *cots, *parts, gain, shift],
        [((row, 512), BF)] * 2
        + [((words, 512), F32)]
        + [((16, W_ROWS, LANES), BF)] * 2
        + [((8, 512), F32)],
        word_scratch + grad_scratch,
        3e9,
    )


def word_back_kernel(count, firsts, me, *refs):
    docs, (grad_in, w1, qkv, mixed, w2, hidden), parts = refs[:count], refs[count : count + 6], refs[count + 6 :]
    gain, shift = parts[8:10]
    grad_own, grad_other, keep, send, vectors, upper, down, sems, keep_here, send_here = parts[-10:]
    vectors[...] = jnp.zeros(vectors.shape, F32)

    @pl.when(me[2] == 0)
    def _():
        fetch_word(firsts, me, parts[:8], upper, down, sems)
        rows = w1.shape[0] // count
        grad = word_backward_body(
            firsts,
            me,
            swapped(grad_in[...], count),
            w1[...],
            qkv[...],
            mixed[...],
            w2[...],
            hidden[...],
            upper,
            down,
            gain[0],
            shift[0],
            [word_allowed(d, rows) for d in docs],
            keep_here,
            send_here,
            vectors,
        )
        grad_own[...] = grad[:rows]
        grad_other[...] = grad[(count - 1) * rows :]
        send_out([(send_here, send), (keep_here, keep)], sems)

    @pl.when(me[2] != 0)
    def _():
        for ref in (grad_own, grad_other):
            ref[...] = jnp.zeros(ref.shape, F32)


def word_back(firsts, me, docs, grad, saved, parts, gain, shift, held):
    count = len(docs)
    row = grad.shape[0] // count
    tables = [me, *docs]
    operands = [grad, *saved, *parts, gain, shift, *held]
    first = len(tables) + len(operands) - 2
    return word_call(
        word_back_kernel,
        count,
        firsts,
        tables,
        operands,
        [((row, 512), F32)] * 2 + [((16, W_ROWS, LANES), BF)] * 2 + [((8, 512), F32)],
        word_scratch + grad_scratch,
        2e9,
        {first: 2, first + 1: 3} if held else None,
    )


def swap(x, axis, flip):
    return lax.ppermute(x, axis, [(k, k ^ flip) for k in range(lax.axis_size(axis))])


def over_x(x):
    return swap(x, "wide", 1)


def over_y(x):
    return swap(x, "narrow", 2)


def over_core(x):
    return swap(x, "narrow", 1)


def over_pair(x):
    return swap(x, "wide", 2)


def after(x, *others):
    return lax.optimization_barrier((x, *others))[0]


def add(*terms):
    total = terms[0].astype(F32)
    for term in terms[1:]:
        total = total + term.astype(F32)
    return total.astype(BF)


def gather_z(block):
    return jnp.stack([block] + [swap(block, "wide", 2 * k) for k in (1, 2, 3)])


def gather_one(z, x_first):
    return jnp.concatenate([z, (over_x if x_first else over_y)(z)], axis=0)


def gather_two(first, x_first):
    return first, (over_y if x_first else over_x)(first)


def gather_core(parts):
    return (*parts, *[over_core(part) for part in parts])


def two(x, x_first):
    return (over_y if x_first else over_x)(x)


def one(x, x_first):
    return (over_x if x_first else over_y)(x)


def cut(matrices, table):
    qkv, out, up, down, proj, *words = matrices

    def split(m):
        r, c = m.shape
        return m.T.reshape(8, c // 8, 4, r // 4).transpose(0, 2, 1, 3)

    def paired(m):
        b = split(m)
        c = b.shape[2]
        return b.reshape(8, 4, 2, c // 2, 64).transpose(0, 1, 3, 2, 4).reshape(8, 4, c // 2, LANES)

    def tiled(m):
        b = split(m)
        c, r = b.shape[2:]
        return b.reshape(8, 4, c, r // LANES, LANES).transpose(0, 1, 3, 2, 4).reshape(8, 4, -1, LANES)

    char = [paired(qkv), paired(out), paired(up), paired(proj), tiled(down)]
    if table is not None:
        char.append(table.reshape(8, 4, 8, 2, LANES).transpose(0, 1, 3, 2, 4).reshape(8, 4, 16, LANES))
    word = [tiled(m) for m in words]
    return [ordered(jnp.concatenate(x, axis=2)) for x in (char, word)]


def ordered(blocks):
    b = blocks.reshape(4, 2, 2, 2, *blocks.shape[2:]).transpose(3, 2, 1, 0, 4, 5)
    return b.reshape(32, *blocks.shape[2:])


def uncut(blocks, is_char, with_table):
    b = blocks.reshape(2, 2, 2, 4, *blocks.shape[1:]).transpose(3, 2, 1, 0, 4, 5)
    b = b.reshape(8, 4, *blocks.shape[1:])

    def joined(x):
        c, r = x.shape[2:]
        return x.transpose(0, 2, 1, 3).reshape(8 * c, 4 * r).T

    def paired(x):
        c = x.shape[2]
        return joined(x.reshape(8, 4, c, 2, 64).transpose(0, 1, 3, 2, 4).reshape(8, 4, 2 * c, 64))

    def tiled(x, tiles):
        c = x.shape[2] // tiles
        return joined(x.reshape(8, 4, tiles, c, LANES).transpose(0, 1, 3, 2, 4).reshape(8, 4, c, tiles * LANES))

    def rows(span, count=None):
        return b[:, :, span[0] : span[0] + (count or span[1])]

    if not is_char:
        return [tiled(rows(W_QKV), 1), tiled(rows(W_OUT), 1), tiled(rows(W_UP), 1), tiled(rows(W_DOWN, 256), 4)], None
    table = None
    if with_table:
        table = rows(C_EMB).reshape(32, 2, 8, LANES).transpose(0, 2, 1, 3).reshape(256, 256)
    qkv, out, up, proj = (paired(rows(span)) for span in C_PAIRED)
    return [qkv, out, up, tiled(rows(C_DOWN, 64), 2), proj], table


def direct_program(
    word_states, character_ids, word_lengths, doc_lengths, embedding, weights, vectors, char_cot, word_cot
):
    char_gains, char_shifts, pool_query, word_gains, word_shifts = vectors
    width = char_cot.shape[3]
    wide = lax.axis_index("wide")
    me = jnp.stack([wide, lax.axis_index("narrow"), (wide >> 1) & 1]).astype(jnp.int32)
    firsts = (True, False)
    c0, c1, mine, theirs = pack(me, weights, embedding)
    pair = jnp.stack([word_states[0], word_cot[0]])
    z0 = gather_z(c0)
    c1, theirs, pair = lax.optimization_barrier((c1, theirs, pair, z0))[:3]
    z1 = gather_z(c1)
    word = jnp.stack([mine, over_pair(theirs)])
    other_pair = over_pair(pair)
    other_docs = over_pair(doc_lengths)
    chars = [gather_core(gather_two(gather_one(z, f), f)) for z, f in zip((z0, z1), firsts)]
    far = swap(word, "wide", 4)
    halves = [jnp.concatenate([word[:, k : k + 384], far[:, k : k + 384]], axis=0) for k in (0, 384)]
    halves = [gather_two(gather_one(h, f), f) for h, f in zip(halves, firsts)]
    word_parts = [*gather_core(halves[0]), *gather_core(halves[1])]
    ids = character_ids.reshape(-1, LANES)
    vectors_char = (char_gains, char_shifts, pool_query)
    vectors_word = (word_gains, word_shifts)
    *saved_0, delta_0 = char_forward(True, firsts[0], me, word_lengths, ids, chars[0], *vectors_char)
    states = saved_0[5]
    *saved_1, delta_1, char_out = char_forward(False, firsts[1], me, word_lengths, states, chars[1], *vectors_char)
    saved_1 = [states] + saved_1
    docs = [doc_lengths, other_docs]
    pairs = [pair, other_pair]
    *word_saved, w3 = word_first(
        firsts, me, docs, pairs, [delta_0, over_pair(delta_0)], word_parts, *vectors_word
    )
    out_own, out_other, grad_1, *held, word_vec_1 = word_last(
        firsts, me, docs, over_pair(w3), [delta_1, over_pair(delta_1)], pairs, word_parts, *vectors_word
    )
    got_1 = over_pair(grad_1)
    grad_own, grad_other, keep, send, word_vec_0 = word_back(
        firsts, me, docs, got_1, word_saved, word_parts, *vectors_word, held
    )
    out_other = over_pair(out_other)
    got_0 = over_pair(grad_other)
    got = over_core(send)
    grad, keep_1, send_1, char_vec_1 = char_backward(
        False,
        firsts[1],
        me,
        word_lengths,
        None,
        char_cot[0].reshape(-1, width),
        (grad_1, got_1),
        (0, 1),
        saved_1,
        chars[1],
        *vectors_char,
        (),
    )
    word_grad, keep_0, send_0, _ = char_backward(
        True,
        firsts[0],
        me,
        word_lengths,
        ids,
        grad,
        (grad_own, got_0),
        (0, 0),
        saved_0,
        chars[0],
        *vectors_char,
        (word_vec_0, word_vec_1, char_vec_1),
    )
    pieces = []
    for h, f in enumerate(firsts):
        span = slice(384 * h, 384 * h + 384)
        ours, away = (add(keep[k : k + 8, span], got[k : k + 8, span]) for k in (0, 8))
        away = two(away, f)
        ours, away = (add(ours[k : k + 4], away[k : k + 4]) for k in (0, 4))
        pieces.append((ours, one(away, f)))
    ours, away = (
        jnp.concatenate([add(a[k : k + 2], b[k : k + 2]) for a, b in pieces], axis=1) for k in (0, 2)
    )
    away = swap(away, "wide", 4)
    ours, away = (add(ours[k : k + 1], away[k : k + 1]) for k in (0, 1))
    away = over_pair(away)
    f = firsts[1]
    got = over_core(send_1)
    own_1, away_1 = (add(keep_1[k : k + 8], got[k : k + 8]) for k in (0, 8))
    away_1 = two(away_1, f)
    own_1, away_1 = (add(own_1[k : k + 4], away_1[k : k + 4]) for k in (0, 4))
    away_1 = one(away_1, f)
    second = [add(own_1[k], away_1[k]) for k in range(4)]
    second = [second[0]] + [swap(second[k], "wide", 2 * k) for k in (1, 2, 3)]
    f = firsts[0]
    own_0, away_0 = fold(keep_0, over_core(send_0), send_0, False)
    own_0, away_0 = fold(own_0, two(away_0, f), away_0, False)
    own_0, *away_0 = fold(own_0, one(away_0, f), away_0, True)
    first = [own_0, away_0[0]] + [swap(away_0[k - 1], "wide", 2 * k) for k in (1, 2, 3)]
    out = unpack(me, [*first, *second, ours, away, out_own, out_other], weights, embedding, vectors)
    return (char_out, out[-1], word_grad, out[9], *out[:9], *out[10:15])


def plain_program(
    word_states, character_ids, word_lengths, doc_lengths, embedding, weights, vectors, char_cot, word_cot
):
    char_gains, char_shifts, pool_query, word_gains, word_shifts = vectors
    width = char_cot.shape[3]
    both = ("wide", "narrow")
    firsts = (True, True)
    at = [jnp.array([0, 0, layer], jnp.int32) for layer in range(2)]
    table = lax.all_gather(embedding, both, axis=0, tiled=True)
    full = [lax.all_gather(lax.all_gather(m, "narrow", axis=1, tiled=True), "wide", axis=2, tiled=True) for m in weights]
    chars, words = [], []
    for layer in range(2):
        char, word = cut([m[layer] for m in full], table if layer == 0 else None)
        chars.append([char[8 * k : 8 * k + 8] for k in range(4)])
        words.append([word[8 * k : 8 * k + 8, h : h + 384] for h in (0, 384) for k in range(4)])
    ids = character_ids.reshape(-1, LANES)
    vectors_char = (char_gains, char_shifts, pool_query)
    vectors_word = (word_gains, word_shifts)
    *saved_0, delta_0 = char_forward(True, True, at[0], word_lengths, ids, chars[0], *vectors_char)
    states = saved_0[5]
    *saved_1, delta_1, char_out = char_forward(False, True, at[0], word_lengths, states, chars[1], *vectors_char)
    saved_1 = [states] + saved_1
    docs = [doc_lengths]
    pair = [jnp.stack([word_states[0], word_cot[0]])]
    *word_saved, w3 = word_first(firsts, at[0], docs, pair, [delta_0], words[0], *vectors_word)
    word_out, _, grad_1, keep_3, send_3, word_vec_1 = word_last(
        firsts, at[1], docs, w3, [delta_1], pair, words[1], *vectors_word
    )
    grad_0, _, keep_2, send_2, word_vec_0 = word_back(
        firsts, at[0], docs, grad_1, word_saved, words[0], *vectors_word, ()
    )
    grad, keep_1, send_1, char_vec_1 = char_backward(
        False,
        True,
        at[0],
        word_lengths,
        None,
        char_cot[0].reshape(-1, width),
        (grad_1, grad_1),
        (0, 0),
        saved_1,
        chars[1],
        *vectors_char,
        (),
    )
    word_grad, keep_0, send_0, _ = char_backward(
        True,
        True,
        at[0],
        word_lengths,
        ids,
        grad,
        (grad_0, grad_0),
        (0, 0),
        saved_0,
        chars[0],
        *vectors_char,
        (word_vec_0, word_vec_1, char_vec_1),
    )
    summed = lax.psum(whole_vector(send_0[16]), both)
    blocks = ((keep_0, send_0[:16]), (keep_1, send_1), (keep_2, send_2), (keep_3, send_3))
    full = [uncut(jnp.concatenate(g), k < 2, k == 0) for k, g in enumerate(blocks)]
    matrix_grads = [
        lax.psum_scatter(
            lax.psum_scatter(jnp.stack([a, b]), "wide", scatter_dimension=2, tiled=True),
            "narrow",
            scatter_dimension=1,
            tiled=True,
        ).astype(F32)
        for a, b in zip(full[0][0] + full[2][0], full[1][0] + full[3][0])
    ]
    embedding_grad = lax.psum_scatter(full[0][1].astype(F32), both, scatter_dimension=0, tiled=True)
    word_vectors = summed[:64].reshape(2, 4, 8, LANES).transpose(0, 2, 1, 3).reshape(2, 8, 512)
    char_vectors = summed[64:].reshape(2, 2, 8, LANES).transpose(0, 2, 1, 3).reshape(2, 8, 256)
    return (
        char_out,
        word_out,
        word_grad,
        embedding_grad,
        *matrix_grads,
        char_vectors[:, 0:2],
        char_vectors[:, 2:4],
        char_vectors[:, 4],
        word_vectors[:, 0:2],
        word_vectors[:, 2:4],
    )


def on_device(direct, *arguments):
    char_cot, word_cot = arguments[19:]
    program = direct_program if direct else plain_program
    char_out, word_out, word_grad, *rest = program(
        *arguments[:5], arguments[5:14], arguments[14:19], char_cot, word_cot
    )
    return (char_out.reshape(char_cot.shape), word_out[None], word_grad[None], *rest)


def solution(mesh):
    rows = ("wide", "narrow")
    matrix = P(None, "narrow", "wide")
    by_rows = P(rows)
    return jax.shard_map(
        partial(on_device, mesh.shape["wide"] == 8 and mesh.shape["narrow"] == 4),
        mesh=mesh,
        in_specs=(by_rows,) * 5 + (matrix,) * 9 + (P(),) * 5 + (by_rows,) * 2,
        out_specs=(by_rows,) * 4 + (matrix,) * 9 + (P(),) * 5,
        check_vma=False,
    )
```

```python
from functools import partial

import jax
import jax.numpy as jnp
from jax import lax
from jax.experimental import pallas as pl
from jax.experimental.pallas import tpu as pltpu
from jax.sharding import PartitionSpec as P

F32 = jnp.float32
BF = jnp.bfloat16
SLOTS = 16
masked_score = -1e30
ROOT = 0.7978845608028654
CUBE = 0.044715
LANES = 128
C_QKV, C_OUT, C_UP, C_PROJ, C_DOWN, C_EMB = (0, 48), (48, 16), (64, 64), (128, 32), (160, 32), (224, 16)
C_PAIRED = (C_QKV, C_OUT, C_UP, C_PROJ)
C_ROWS = 224
HELD_0 = C_ROWS + 16
W_QKV, W_OUT, W_UP, W_DOWN = (0, 192), (192, 64), (256, 256), (512, 64)
W_ROWS = 768
CHUNK = 512
VMEM, SMALL = 24 << 20, 12 << 20
COST_FORWARD, COST_FEED, COST_MIX = 2e9, 2e9, 2e9
A_SPAN, F_SPAN = (0, 64), (64, 160)
E_ROWS = 16


def dot(left, right, l, r):
    return lax.dot_general(left, right, (((l,), (r,)), ((), ())), preferred_element_type=F32)


def nn(left, right):
    return dot(left, right, 1, 0)


def nt(left, right):
    return dot(left, right, 1, 1)


def tn(left, right):
    return dot(left, right, 0, 0)


def iota(shape, dim):
    return lax.broadcasted_iota(jnp.int32, shape, dim)


def norm_parts(states):
    centre = states - jnp.mean(states, axis=-1, keepdims=True)
    spread = jnp.mean(centre * centre, axis=-1, keepdims=True)
    root = lax.rsqrt(spread + 1e-05)
    return centre * root, root


def norm_back(grad, hat, root, gain):
    scaled = grad * gain
    inner = scaled - jnp.mean(scaled, axis=-1, keepdims=True)
    back = root * (inner - hat * jnp.mean(scaled * hat, axis=-1, keepdims=True))
    return back, jnp.sum(grad * hat, axis=0, keepdims=True), jnp.sum(grad, axis=0, keepdims=True)


def gelu_value(h):
    return 0.5 * h * (1.0 + jnp.tanh(ROOT * (h + CUBE * h * h * h)))


def gelu_both(h):
    square = h * h
    t = jnp.tanh(ROOT * (h + CUBE * square * h))
    half = 0.5 * (1.0 + t)
    slope = half + 0.5 * h * (1.0 - t * t) * (ROOT * (1.0 + 3.0 * CUBE * square))
    return h * half, slope


def softmax_rows(scores):
    shifted = jnp.exp(scores - jnp.max(scores, axis=-1, keepdims=True))
    return shifted / jnp.sum(shifted, axis=-1, keepdims=True)


def low_half(shape):
    return iota(shape, len(shape) - 1) % LANES < 64


def two_heads(x):
    low = low_half(x.shape)
    zero = jnp.zeros_like(x)
    return jnp.concatenate([jnp.where(low, x, zero), jnp.where(low, zero, x)], axis=0)


def join_heads(x):
    k = x.shape[0] // 2
    return jnp.where(low_half((k, LANES)), x[:k], x[k:])


def place(rw, ry, x_first):
    rx, rz = rw & 1, rw >> 1
    return ry * 8 + rx * 4 + rz if x_first else rx * 8 + ry * 4 + rz


def unplace(q, s, x_first):
    a, rz = s >> 2, s & 3
    rx, ry = (a, q) if x_first else (q, a)
    return rz * 2 + rx, ry


def pack_kernel(me, cq, co, cu, cd, cp, wq, wo, wu, wd, emb, c01, mine, theirs):
    def turned(x):
        return x.astype(F32).T

    for layer in range(2):
        base = layer * HELD_0
        for t, (row, rows) in zip((turned(cq[layer]), co[layer], turned(cu[layer]), turned(cp[layer])), C_PAIRED):
            t = t.astype(F32)
            c01[base + row : base + row + rows, :] = jnp.concatenate([t[:rows], t[rows:]], axis=1).astype(BF)
        for k in range(2):
            row = base + C_DOWN[0] + 32 * k
            c01[row : row + 32, :] = cd[layer, :, k * LANES : (k + 1) * LANES]
    e = emb[...].astype(F32)
    c01[C_EMB[0] : C_EMB[0] + 16, :] = jnp.concatenate([e[:, :LANES], e[:, LANES:]], axis=0).astype(BF)
    for layer, w in ((me[2], mine), (1 - me[2], theirs)):
        w[W_QKV[0] : W_QKV[0] + 192, :] = wq[layer]
        w[W_OUT[0] : W_OUT[0] + 64, :] = wo[layer]
        w[W_UP[0] : W_UP[0] + 256, :] = turned(wu[layer]).astype(BF)
        for k in range(4):
            row = W_DOWN[0] + 64 * k
            w[row : row + 64, :] = wd[layer, :, k * LANES : (k + 1) * LANES]


def whole(shape, dtype):
    return jax.ShapeDtypeStruct(shape, dtype)


def cost(flops, moved):
    return pl.CostEstimate(flops=int(flops), bytes_accessed=int(moved), transcendentals=0)


smem = pl.BlockSpec(memory_space=pltpu.SMEM)
vmem = pl.BlockSpec(memory_space=pltpu.VMEM)
anywhere = pl.BlockSpec(memory_space=pl.ANY)
TURNED = (1, 3, 5, 6, 8)


def pack(me, weights, embedding):
    weights = [m.swapaxes(1, 2) if k in TURNED else m for k, m in enumerate(weights)]
    return pl.pallas_call(
        pack_kernel,
        in_specs=[smem] + [vmem] * 10,
        out_shape=(
            whole((HELD_0 + C_ROWS, LANES), BF),
            whole((W_ROWS, LANES), BF),
            whole((W_ROWS, LANES), BF),
        ),
        compiler_params=pltpu.CompilerParams(vmem_limit_bytes=SMALL),
        cost_estimate=cost(0, 4e6),
    )(me, *weights, embedding)


def split_vector(x):
    high = x.astype(BF)
    return jnp.concatenate([high, (x - high.astype(F32)).astype(BF)], axis=0)


def whole_vector(x):
    return x[:64].astype(F32) + x[64:].astype(F32)


def unpack_kernel(me, *refs):
    first, second, own_word, other_word, own_out, other_out = refs[:5], refs[5:9], *refs[9:13]
    cq, co, cu, cd, cp, wq, wo, wu, wd, emb, cg, cs, pq, wg, ws, word_out = refs[13:]
    layer_now = me[2]
    word_out[...] = jnp.where(layer_now == 1, own_out[...], other_out[...])
    c0 = [first[k][0 : C_ROWS + 16, :].astype(F32) for k in (0, 2, 3, 4)]
    c0 = (c0[0] + c0[1]) + (c0[2] + c0[3])
    c1 = (second[0][...].astype(F32) + second[1][...].astype(F32)) + (
        second[2][...].astype(F32) + second[3][...].astype(F32)
    )
    v = [whole_vector(ref[C_ROWS + 16 :, :]) for ref in first[1:5]]
    v = (v[0] + v[1]) + (v[2] + v[3])
    for layer, c in enumerate((c0, c1)):
        for k, ref, (row, rows) in zip((0, 1, 2, 4), (cq, co, cu, cp), C_PAIRED):
            t = c[row : row + rows, :]
            t = jnp.concatenate([t[:, :64], t[:, 64:]], axis=0)
            ref[layer] = t if k in TURNED else t.T
        for k in range(2):
            row = C_DOWN[0] + 32 * k
            cd[layer, :, k * LANES : (k + 1) * LANES] = c[row : row + 32, :]
        for t in range(4):
            row = 8 * t + 4 * layer
            wg[layer, :, t * LANES : (t + 1) * LANES] = v[row : row + 2]
            ws[layer, :, t * LANES : (t + 1) * LANES] = v[row + 2 : row + 4]
        for t in range(2):
            row = 32 + 16 * t + 8 * layer
            cg[layer, :, t * LANES : (t + 1) * LANES] = v[row : row + 2]
            cs[layer, :, t * LANES : (t + 1) * LANES] = v[row + 2 : row + 4]
            pq[layer : layer + 1, t * LANES : (t + 1) * LANES] = v[row + 4 : row + 5]
    e = c0[C_EMB[0] : C_EMB[0] + 16, :]
    emb[...] = jnp.concatenate([e[:8], e[8:]], axis=1)
    for layer, w in ((layer_now, own_word), (1 - layer_now, other_word)):
        wq[layer] = w[0, W_QKV[0] : W_QKV[0] + 192, :].astype(F32)
        wo[layer] = w[0, W_OUT[0] : W_OUT[0] + 64, :].astype(F32)
        wu[layer] = w[0, W_UP[0] : W_UP[0] + 256, :].astype(F32).T
        for k in range(4):
            row = W_DOWN[0] + 64 * k
            wd[layer, :, k * LANES : (k + 1) * LANES] = w[0, row : row + 64, :].astype(F32)


def unpack(me, blocks, weights, embedding, vectors):
    shapes = [m.shape for m in weights]
    shapes = [(a, c, b) if k in TURNED else (a, b, c) for k, (a, b, c) in enumerate(shapes)]
    shapes += [embedding.shape] + [v.shape for v in vectors]
    out = pl.pallas_call(
        unpack_kernel,
        in_specs=[smem] + [vmem] * len(blocks),
        out_shape=tuple(whole(x, F32) for x in shapes) + (whole(blocks[-1].shape, BF),),
        cost_estimate=cost(0, 8e6),
    )(me, *blocks)
    return [x.swapaxes(1, 2) if k in TURNED else x for k, x in enumerate(out)]


def fold_one_kernel(keep_f, got_f, keep_a, got_a, sent_a, ours, *away):
    vector = [jnp.concatenate([ref[16], ref[17, 0:48, :]], axis=0) for ref in (sent_a, got_a)]
    vector = split_vector(whole_vector(vector[0]) + whole_vector(vector[1]))
    for part, ref in enumerate((ours, *away)):
        for k in range(4):
            at, row = 4 * part + k, k * HELD_0
            ref[row : row + 64, :] = (keep_a[at, 0:64, :].astype(F32) + got_a[at, 0:64, :].astype(F32)).astype(BF)
            ref[row + 64 : row + 224, :] = (keep_f[at].astype(F32) + got_f[at].astype(F32)).astype(BF)
            ref[row + 224 : row + 240, :] = (
                keep_a[at, 64:80, :].astype(F32) + got_a[at, 64:80, :].astype(F32)
            ).astype(BF)
        if part > 0:
            ref[4 * HELD_0 :, :] = vector


def fold_one(*operands):
    return pl.pallas_call(
        fold_one_kernel,
        out_shape=[whole((4 * HELD_0, LANES), BF)] + [whole((4 * HELD_0 + 128, LANES), BF)] * 3,
        compiler_params=pltpu.CompilerParams(vmem_limit_bytes=SMALL),
        cost_estimate=cost(0, 4e6),
    )(*operands)


def fold_two_kernel(ours, sent, over_x, over_y, over_xy, own, *away):
    vector = [whole_vector(ref[4 * HELD_0 :, :]) for ref in (sent, over_x, over_y, over_xy)]
    vector = split_vector((vector[0] + vector[1]) + (vector[2] + vector[3]))
    for k, ref in enumerate((own, *away)):
        row = k * HELD_0
        near = [r[row : row + HELD_0, :].astype(F32) for r in (ours, over_x, over_y, over_xy)]
        ref[0:HELD_0, :] = ((near[0] + near[1]) + (near[2] + near[3])).astype(BF)
        if k > 0:
            ref[HELD_0:, :] = vector


def fold_two(*operands):
    return pl.pallas_call(
        fold_two_kernel,
        out_shape=[whole((HELD_0, LANES), BF)] + [whole((HELD_0 + 128, LANES), BF)] * 3,
        compiler_params=pltpu.CompilerParams(vmem_limit_bytes=SMALL),
        cost_estimate=cost(0, 4e6),
    )(*operands)


def fold_cores_kernel(keep, got, *out):
    for part, ref in enumerate(out):
        for k in range(4):
            ref[k] = (keep[4 * part + k].astype(F32) + got[4 * part + k].astype(F32)).astype(BF)


def fold_cores(keep, got):
    return pl.pallas_call(
        fold_cores_kernel,
        out_shape=[whole((4, *keep.shape[1:]), BF)] * 4,
        compiler_params=pltpu.CompilerParams(vmem_limit_bytes=SMALL),
        cost_estimate=cost(0, 4e6),
    )(keep, got)


def fold_chips_kernel(ours, over_x, over_y, over_xy, *out):
    for k, ref in enumerate(out):
        near = ours[k].astype(F32) + over_x[k].astype(F32)
        ref[...] = (near + (over_y[k].astype(F32) + over_xy[k].astype(F32))).astype(BF)


def fold_chips(*operands):
    return pl.pallas_call(
        fold_chips_kernel,
        out_shape=[whole(operands[0].shape[1:], BF)] * 4,
        compiler_params=pltpu.CompilerParams(vmem_limit_bytes=SMALL),
        cost_estimate=cost(0, 2e6),
    )(*operands)


def assemble(x_first, me, span, raw, mats):
    mw, my, mc = me[0], me[1] >> 1, me[1] & 1
    for w in range(8):
        for y in range(2):
            at = place(w ^ mw, y ^ my, x_first)
            cores = (mc * 16 + at, (1 - mc) * 16 + at)
            for ref, (row, rows) in zip(mats[:4], C_PAIRED):
                if ref is None:
                    continue
                row = row - span
                zero, one = (raw[k, row : row + rows, :] for k in cores)
                first = w * 2 * rows
                columns = slice(y * LANES, (y + 1) * LANES)
                ref[first : first + rows, columns] = jnp.concatenate([zero[:, :64], one[:, :64]], axis=1)
                ref[first + rows : first + 2 * rows, columns] = jnp.concatenate(
                    [zero[:, 64:], one[:, 64:]], axis=1
                )
            if mats[4] is None:
                continue
            for c, k in enumerate(cores):
                for t in range(2):
                    column = (2 * y + c) * 256 + t * LANES
                    row = C_DOWN[0] + 32 * t - span
                    mats[4][w * 32 : w * 32 + 32, column : column + LANES] = raw[k, row : row + 32, :]

def put_char(x_first, me, keep, send, span, mats):
    mw, my, mc = me[0], me[1] >> 1, me[1] & 1

    def put(at, row, rows, zero, one):
        row = row - span
        keep[at, row : row + rows, :] = jnp.where(mc == 0, zero, one)
        send[at, row : row + rows, :] = jnp.where(mc == 0, one, zero)

    for w in range(8):
        for y in range(2):
            at = place(w ^ mw, y ^ my, x_first)
            for ref, (row, rows) in zip(mats[:4], C_PAIRED):
                if ref is None:
                    continue
                columns = slice(y * LANES, (y + 1) * LANES)
                top = ref[w * 2 * rows : w * 2 * rows + rows, columns]
                bottom = ref[w * 2 * rows + rows : w * 2 * rows + 2 * rows, columns]
                put(
                    at,
                    row,
                    rows,
                    jnp.concatenate([top[:, :64], bottom[:, :64]], axis=1),
                    jnp.concatenate([top[:, 64:], bottom[:, 64:]], axis=1),
                )
            if mats[4] is None:
                continue
            for t in range(2):
                zero, one = (
                    mats[4][w * 32 : w * 32 + 32, (2 * y + c) * 256 + t * LANES : (2 * y + c) * 256 + (t + 1) * LANES]
                    for c in range(2)
                )
                put(at, C_DOWN[0] + 32 * t, 32, zero, one)


def char_positions(ids, me, x_first):
    device = ids >> 3
    rw = (device >> 2) ^ me[0]
    rn = (device & 3) ^ me[1]
    return ((rn & 1) * 16 + place(rw, rn >> 1, x_first)) * 16 + (ids & 7)


def valid_keys(lens, first):
    lane = iota((1, LANES), 1)
    length = jnp.zeros((1, LANES), jnp.int32)
    for k in range(8):
        length = jnp.where(lane // SLOTS == k, lens[0, first + k], length)
    return lane % SLOTS < length


def to_column(row):
    square = (LANES, LANES)
    return jnp.sum(jnp.where(iota(square, 0) == iota(square, 1), row, 0.0), axis=-1, keepdims=True)


def char_masks(lens, first):
    same = iota((LANES, LANES), 0) // SLOTS == iota((LANES, LANES), 1) // SLOTS
    valid = valid_keys(lens, first)
    return to_column(jnp.where(valid, 1.0, 0.0)), same & valid, same


def char_attend(q, keys, allowed):
    scores = jnp.where(allowed, nt(q, keys) * 0.125, masked_score)
    return jnp.concatenate([softmax_rows(scores[:, :LANES]), softmax_rows(scores[:, LANES:])], axis=1)


def by_head(x, reduce):
    k = x.shape[0] // 2
    return [reduce(x[h * k : (h + 1) * k], axis=0, keepdims=True) for h in range(2)]


def char_attend_turned(keys, q, allowed):
    scores = jnp.where(allowed, nt(keys, q) * 0.125, masked_score)
    k = scores.shape[0] // 2
    out = []
    for h in range(2):
        part = scores[h * k : (h + 1) * k]
        shifted = jnp.exp(part - jnp.max(part, axis=0, keepdims=True))
        out.append(shifted / jnp.sum(shifted, axis=0, keepdims=True))
    return jnp.concatenate(out, axis=0)


def pool_weights(states, query, valid):
    scores = jnp.sum(states * query, axis=-1, keepdims=True)
    scores = jnp.where(valid > 0.5, scores, masked_score).reshape(-1, SLOTS, 1)
    shifted = jnp.exp(scores - jnp.max(scores, axis=1, keepdims=True))
    return shifted / jnp.sum(shifted, axis=1, keepdims=True)


def of_layer(first, gain, shift, query):
    layer = 0 if first else 1
    return gain[layer], shift[layer], query[layer : layer + 1, :]


def begin(copies):
    copies = [pltpu.make_async_copy(*c) for c in copies]
    for copy in copies:
        copy.start()
    return copies


def finish(copies):
    for copy in copies:
        copy.wait()


def part_copies(parts, raw, row, rows, at, sems):
    each = 32 // len(parts)
    return [
        (part.at[:, pl.ds(row, rows)], raw.at[pl.ds(each * k, each), pl.ds(at, rows)], sems.at[k])
        for k, part in enumerate(parts)
    ]


def char_forward_kernel(first, x_first, count, *refs):
    me, lens, source = refs[:3]
    parts, refs = refs[3 : 3 + count], refs[3 + count :]
    gain, shift, query = of_layer(first, *refs[:3])
    qkv_out, mixed_out, after_out, next_out, extra_out, pooled_out, delta_out = refs[3:10]
    mats, refs = refs[10:15], refs[15:]
    hidden_here, raw, table, sems_a, sems_f, sems_e = refs
    m_qkv, m_out, m_up, m_proj, m_down = mats
    rows_all = qkv_out.shape[0]
    near = begin(part_copies(parts, raw, 0, 64, 0, sems_a))
    if first:
        near += begin(part_copies(parts, raw, C_EMB[0], 16, C_EMB[0], sems_e))
    far = begin(part_copies(parts, raw, 64, 160, 64, sems_f))
    finish(near)
    assemble(x_first, me, 0, raw, (m_qkv, m_out, None, None, None))
    if first:
        for k in range(32):
            table[k * 16 : k * 16 + 16, :] = raw[k, C_EMB[0] : C_EMB[0] + 16, :]
    for chunk in range(rows_all // CHUNK):
        span = slice(chunk * CHUNK, (chunk + 1) * CHUNK)
        halves = CHUNK // LANES
        masks = [char_masks(lens, chunk * (CHUNK // SLOTS) + 8 * h) for h in range(halves)]
        if first:
            sides = []
            for h in range(halves):
                ids = source[pl.ds(chunk * halves + h, 1), :]
                column = to_column(char_positions(ids, me, x_first).astype(F32)).astype(jnp.int32)
                lane = iota((LANES, 512), 1)
                left = jnp.where(lane == column, 1.0, 0.0).astype(BF)
                right = jnp.where(lane == column + 8, 1.0, 0.0).astype(BF)
                sides.append(jnp.concatenate([nn(left, table[...]), nn(right, table[...])], axis=1))
            x = jnp.concatenate(sides, axis=0)
            extra_out[span] = x
        else:
            x = source[span]
        hat, _ = norm_parts(x)
        normed = (hat * gain[0:1] + shift[0:1]).astype(BF)
        qkv_out[span] = nt(normed, m_qkv[...]).astype(BF)
        sides = []
        for h in range(halves):
            base = chunk * CHUNK + h * LANES
            allowed = jnp.concatenate([masks[h][1]] * 2, axis=1)
            pairs = []
            for pair in range(2):
                q, k, v = char_heads(qkv_out, base, pair)
                attend = char_attend(q, two_heads(k), allowed)
                pairs.append(nn(attend.astype(BF), two_heads(v)))
            sides.append(jnp.concatenate(pairs, axis=1))
        mixed = jnp.concatenate(sides, axis=0).astype(BF)
        mixed_out[span] = mixed
        after = x + nt(mixed, m_out[...])
        after_out[span] = after
        hat, _ = norm_parts(after)
        normed = (hat * gain[1:2] + shift[1:2]).astype(BF)
        if chunk == 0:
            finish(far)
            assemble(x_first, me, 0, raw, (None, None, m_up, m_proj, m_down))
        hidden_here[span] = nt(normed, m_up[...])
        states = after_out[span] + nt(gelu_value(hidden_here[span]).astype(BF), m_down[...])
        next_out[span] = states
        if not first:
            extra_out[span] = states.astype(BF)
        weights = pool_weights(states, query, jnp.concatenate([m[0] for m in masks], axis=0))
        pooled = jnp.sum(weights * states.reshape(-1, SLOTS, 256), axis=1).astype(BF)
        words = slice(chunk * (CHUNK // SLOTS), (chunk + 1) * (CHUNK // SLOTS))
        pooled_out[words] = pooled
        delta_out[words] = nt(pooled, m_proj[...])


def char_heads(qkv, base, pair):
    return (
        qkv[base : base + LANES, t * 256 + pair * LANES : t * 256 + (pair + 1) * LANES] for t in range(3)
    )


def char_forward(first, x_first, me, lens, source, parts, gain, shift, query):
    words = lens.shape[1]
    rows = words * SLOTS
    big = [(768, BF), (256, BF), (256, F32), (256, F32), (256, F32) if first else (256, BF)]
    held = C_ROWS + (16 if first else 0)
    shapes = [whole((rows, 1024), F32)] if not first else []
    out = pl.pallas_call(
        partial(char_forward_kernel, first, x_first, len(parts)),
        in_specs=[smem, smem, vmem] + [anywhere] * len(parts) + [vmem] * 3,
        out_specs=[vmem] * (12 + len(shapes)),
        out_shape=[whole((rows, c), t) for c, t in big]
        + [whole((words, 256), BF), whole((words, 512), F32)]
        + [whole(s, BF) for s in MATS]
        + shapes,
        scratch_shapes=([pltpu.VMEM((rows, 1024), F32)] if first else [])
        + [pltpu.VMEM((32, held, LANES), BF), pltpu.VMEM((512, LANES) if first else (16, LANES), BF)]
        + [pltpu.SemaphoreType.DMA((8,))] * 3,
        compiler_params=pltpu.CompilerParams(vmem_limit_bytes=VMEM),
        cost_estimate=cost(COST_FORWARD, 12e6),
    )(me, lens, source, *parts, gain, shift, query)
    qkv, mixed, after, states, extra, pooled, delta = out[:7]
    mats, hidden = out[7:12], out[12:]
    if first:
        return (extra, qkv, mixed, after, states, pooled, *hidden), delta, mats
    return (source, qkv, mixed, after, states, pooled, *hidden), delta, mats, extra


MATS = ((768, 256), (256, 256), (1024, 256), (512, 256), (256, 1024))


def pool_back(states, query, valid, grad):
    weights = pool_weights(states, query, valid)
    cube = states.reshape(-1, SLOTS, 256)
    wide = grad.reshape(-1, 1, 256)
    by_weight = jnp.sum(cube * wide, axis=-1, keepdims=True)
    by_score = weights * (by_weight - jnp.sum(weights * by_weight, axis=1, keepdims=True))
    added = weights * wide + by_score * query.reshape(1, 1, 256)
    by_query = jnp.sum((by_score * cube).reshape(states.shape), axis=0, keepdims=True)
    return added.reshape(states.shape), by_query


def accumulate(ref, value, chunk):
    if chunk == 0:
        ref[...] = value
    else:
        ref[...] += value


def char_feed_kernel(first, x_first, at, me, lens, word_own, word_other, *refs):
    pooled_in, grad_in, next_in, after_in, m_up, m_proj, m_down = refs[:7]
    gain, shift, query = of_layer(first, *refs[7:10])
    refs = refs[10:]
    if first:
        word_out, refs = refs[0], refs[1:]
    else:
        hidden_in, refs = refs[0], refs[1:]
    grad_out, keep, send, vectors, t_up, t_proj, t_down, a_up, a_proj, a_down = refs
    rows_all = grad_out.shape[0]
    words_all = rows_all // SLOTS
    word_grad = jnp.where(
        me[2] == (0 if first else 1),
        word_own[at[0] * words_all : (at[0] + 1) * words_all],
        word_other[at[1] * words_all : (at[1] + 1) * words_all],
    )
    if first:
        word_out[...] = word_grad
    vectors[...] = jnp.zeros(vectors.shape, F32)
    low_word = word_grad.astype(BF)
    a_proj[...] = tn(low_word, pooled_in[...])
    grad_pooled = nn(low_word, m_proj[...])
    for chunk in range(rows_all // CHUNK):
        span = slice(chunk * CHUNK, (chunk + 1) * CHUNK)
        words = CHUNK // SLOTS
        valid = [valid_keys(lens, chunk * words + 8 * h) for h in range(CHUNK // LANES)]
        valid = jnp.concatenate([to_column(jnp.where(v, 1.0, 0.0)) for v in valid], axis=0)
        added, by_query = pool_back(next_in[span], query, valid, grad_pooled[chunk * words : (chunk + 1) * words])
        grad = grad_in[span].astype(F32) + added
        vectors[4:5, :] += by_query
        low = grad.astype(BF)
        hat, root = norm_parts(after_in[span])
        normed = (hat * gain[1:2] + shift[1:2]).astype(BF)
        act, slope = gelu_both(nt(normed, m_up[...]) if first else hidden_in[span])
        accumulate(a_down, tn(low, act.astype(BF)), chunk)
        by_hidden = (slope * nn(low, m_down[...])).astype(BF)
        accumulate(a_up, tn(normed, by_hidden), chunk)
        back, by_gain, by_shift = norm_back(nn(by_hidden, m_up[...]), hat, root, gain[1:2])
        grad_out[span] = grad + back
        vectors[1:2, :] += by_gain
        vectors[3:4, :] += by_shift
    t_up[...] = a_up[...].T.astype(BF)
    t_proj[...] = a_proj[...].astype(BF)
    t_down[...] = a_down[...].astype(BF)
    put_char(x_first, me, keep, send, F_SPAN[0], (None, None, t_up, t_proj, t_down))


def char_feed(first, x_first, me, lens, grad, words, at, saved, mats, vectors):
    after, states, pooled, *hidden = saved
    rows = after.shape[0]
    outs = [whole((rows, 256), F32)]
    if first:
        outs = [whole((rows // SLOTS, 512), F32)] + outs
    held = F_SPAN[1]
    return pl.pallas_call(
        partial(char_feed_kernel, first, x_first, at),
        in_specs=[smem, smem] + [vmem] * (12 + len(hidden)),
        out_specs=[vmem] * (len(outs) + 3),
        out_shape=outs + [whole((16, held, LANES), BF)] * 2 + [whole((8, 256), F32)],
        scratch_shapes=[pltpu.VMEM(MATS[k], BF) for k in (2, 3, 4)]
        + [pltpu.VMEM(x, F32) for x in ((256, 1024), (512, 256), (256, 1024))],
        compiler_params=pltpu.CompilerParams(vmem_limit_bytes=VMEM),
        cost_estimate=cost(COST_FEED, 12e6),
    )(me, lens, *words, pooled, grad, states, after, *mats[2:], *vectors, *hidden)


def char_mix_kernel(first, x_first, me, lens, grad_in, mixed_in, qkv_in, x_in, m_qkv, m_out, *refs):
    gain, shift, _ = of_layer(first, *refs[:3])
    vec_feed, refs = refs[3], refs[4:]
    if first:
        ids, word_0, word_1, char_1, keep, send, vectors = refs[:7]
        refs = refs[7:]
    else:
        keep_feed, send_feed, grad_out, keep, send, vectors = refs[:6]
        refs = refs[6:]
    t_qkv, t_out, a_qkv, a_out, a_table = refs
    rows_all = grad_in.shape[0]
    vectors[...] = vec_feed[...]
    for chunk in range(rows_all // CHUNK):
        span = slice(chunk * CHUNK, (chunk + 1) * CHUNK)
        grad = grad_in[span]
        low = grad.astype(BF)
        accumulate(a_out, tn(low, mixed_in[span]), chunk)
        by_mixed = nn(low, m_out[...]).astype(BF)
        sides = []
        for h in range(CHUNK // LANES):
            base = chunk * CHUNK + h * LANES
            valid, _, same = char_masks(lens, chunk * (CHUNK // SLOTS) + 8 * h)
            allowed = jnp.concatenate([same & (valid > 0.5)] * 2, axis=0)
            by_q, by_k, by_v = [], [], []
            for pair in range(2):
                q, k, v = char_heads(qkv_in, base, pair)
                keys = two_heads(k)
                attend = char_attend_turned(keys, q, allowed)
                g = by_mixed[h * LANES : (h + 1) * LANES, pair * LANES : (pair + 1) * LANES]
                by_attend = nt(two_heads(v), g)
                product = attend * by_attend
                inner = [jnp.broadcast_to(t, (LANES, LANES)) for t in by_head(product, jnp.sum)]
                by_scores = (product - attend * jnp.concatenate(inner, axis=0)).astype(BF)
                by_v.append(join_heads(nn(attend.astype(BF), g)))
                by_q.append(tn(by_scores, keys) * 0.125)
                by_k.append(join_heads(nn(by_scores, q)) * 0.125)
            sides.append(jnp.concatenate(by_q + by_k + by_v, axis=1))
        by_qkv = jnp.concatenate(sides, axis=0).astype(BF)
        hat, root = norm_parts(x_in[span])
        normed = (hat * gain[0:1] + shift[0:1]).astype(BF)
        accumulate(a_qkv, tn(normed, by_qkv), chunk)
        back, by_gain, by_shift = norm_back(nn(by_qkv, m_qkv[...]), hat, root, gain[0:1])
        grad = grad + back
        vectors[0:1, :] += by_gain
        vectors[2:3, :] += by_shift
        if first:
            for h in range(CHUNK // LANES):
                at = char_positions(ids[pl.ds(chunk * (CHUNK // LANES) + h, 1), :], me, x_first)
                row = iota((512, LANES), 0)
                part = grad[h * LANES : (h + 1) * LANES]
                high = part.astype(BF)
                rest = (part - high.astype(F32)).astype(BF)
                both = jnp.concatenate([high, rest], axis=0)
                for side in range(2):
                    hot = jnp.where(row == at + 8 * side, 1.0, 0.0).astype(BF)
                    hot = jnp.concatenate([hot, hot], axis=1)
                    accumulate(a_table, nn(hot, both[:, side * LANES : (side + 1) * LANES]), chunk + h + side)
        else:
            grad_out[span] = grad
    t_qkv[...] = a_qkv[...].T.astype(BF)
    t_out[...] = a_out[...].astype(BF)
    put_char(x_first, me, keep, send, A_SPAN[0], (t_qkv, t_out, None, None, None))
    if first:
        row = A_SPAN[1]
        for k in range(16):
            keep[k, row : row + E_ROWS, :] = a_table[k * 16 : k * 16 + 16, :].astype(BF)
            send[k, row : row + E_ROWS, :] = a_table[256 + k * 16 : 272 + k * 16, :].astype(BF)
        word = jnp.concatenate([word_0[0:4], word_1[0:4]], axis=0)
        char = jnp.concatenate([vectors[...], char_1[...]], axis=0)
        tiles = [x[:, t * LANES : (t + 1) * LANES] for x in (word, char) for t in range(x.shape[1] // LANES)]
        vector = split_vector(jnp.concatenate(tiles, axis=0))
        send[16] = vector[:80]
        send[17, 0:48, :] = vector[80:]
        send[17, 48:, :] = jnp.zeros((32, LANES), BF)
    else:
        keep[:, F_SPAN[0] :, :] = keep_feed[...]
        send[:, F_SPAN[0] :, :] = send_feed[...]


def char_mix(first, x_first, me, lens, grad, saved, mats, vectors, others):
    x, qkv, mixed = saved
    rows = x.shape[0]
    if first:
        outs, held, sends = [], A_SPAN[1] + E_ROWS, 18
    else:
        outs, held, sends = [whole((rows, 256), F32)], C_ROWS, 16
    return pl.pallas_call(
        partial(char_mix_kernel, first, x_first),
        in_specs=[smem, smem] + [vmem] * (9 + len(others)),
        out_specs=[vmem] * (len(outs) + 3),
        out_shape=outs
        + [whole((16, held, LANES), BF), whole((sends, held, LANES), BF), whole((8, 256), F32)],
        scratch_shapes=[pltpu.VMEM(MATS[k], BF) for k in (0, 1)]
        + [pltpu.VMEM(x, F32) for x in ((256, 768), (256, 256), (512 if first else 8, LANES))],
        compiler_params=pltpu.CompilerParams(vmem_limit_bytes=VMEM),
        cost_estimate=cost(COST_MIX, 12e6),
    )(me, lens, grad, mixed, qkv, x, *mats[:2], *vectors, *others)


def fetch_word(me, parts, upper, down, sems):
    for k, part in enumerate(parts):
        rc, far, ry, rx = k >> 3, (k >> 2) & 1, (k >> 1) & 1, k & 1

        def one(s, _, part=part, rc=rc, far=far, ry=ry, rx=rx):
            w, n = ((far * 2 + s) * 2 + rx) ^ me[0], (ry * 2 + rc) ^ me[1]
            block = part.at[s]
            column = pl.ds(pl.multiple_of(n * LANES, LANES), LANES)
            for which, base, (row, rows) in ((0, 0, W_QKV), (1, 1536, W_OUT), (2, 2048, W_UP)):
                to = pl.ds(pl.multiple_of(base + w * rows, 64), rows)
                pltpu.make_async_copy(block.at[pl.ds(row, rows)], upper.at[to, column], sems.at[which]).start()
            for t in range(4):
                column = pl.ds(pl.multiple_of(n * 512 + t * LANES, LANES), LANES)
                to = pl.ds(pl.multiple_of(w * 64, 64), 64)
                pltpu.make_async_copy(
                    block.at[pl.ds(W_DOWN[0] + 64 * t, 64)], down.at[to, column], sems.at[3]
                ).start()
            return 0

        lax.fori_loop(0, 2, one, 0)
    return [
        pltpu.make_async_copy(ref, ref, sems.at[k])
        for k, ref in enumerate((upper.at[pl.ds(0, 1536)], upper.at[pl.ds(1536, 512)], upper.at[pl.ds(2048, 2048)], down))
    ]


def word_allowed(docs, words):
    shape = (words, 2 * words)
    i, j = iota(shape, 0), iota(shape, 1) % words
    end = 0
    of_i, of_j = jnp.zeros(shape, jnp.int32), jnp.zeros(shape, jnp.int32)
    for k in range(docs.shape[1]):
        end = end + docs[0, k]
        of_i = of_i + (i >= end).astype(jnp.int32)
        of_j = of_j + (j >= end).astype(jnp.int32)
    return (of_i == of_j) & (j <= i)


def by_half(x, reduce, fill):
    low = low_half(x.shape)
    left = reduce(jnp.where(low, x, fill), axis=-1, keepdims=True)
    right = reduce(jnp.where(low, fill, x), axis=-1, keepdims=True)
    return jnp.where(low, left, right)


def word_attend(q, keys, allowed):
    scores = jnp.where(allowed, nt(q, keys) * 0.125, masked_score)
    shifted = jnp.exp(scores - by_half(scores, jnp.max, 2 * masked_score))
    return shifted / by_half(shifted, jnp.sum, 0.0)


def word_forward_body(w1, coming, upper, down, gain, shift, allowed):
    hat, root = norm_parts(w1)
    normed = (hat * gain[0:1] + shift[0:1]).astype(BF)
    await_one(coming, 0)
    qkv = nt(normed, upper[0:1536, :]).astype(BF)
    rows = w1.shape[0] // len(allowed)
    mixed = []
    for r, pairs in enumerate(allowed):
        heads = []
        for pair in range(4):
            q, k, v = word_heads(qkv, r * rows, rows, pair)
            attend = word_attend(q, two_heads(k), pairs)
            heads.append(nn(attend.astype(BF), two_heads(v)))
        mixed.append(jnp.concatenate(heads, axis=1))
    mixed = jnp.concatenate(mixed, axis=0).astype(BF)
    await_one(coming, 1)
    w2 = w1 + nt(mixed, upper[1536:2048, :])
    hat, root = norm_parts(w2)
    normed = (hat * gain[1:2] + shift[1:2]).astype(BF)
    await_one(coming, 2)
    hidden = nt(normed, upper[2048:4096, :])
    await_one(coming, 3)
    w3 = w2 + nt(gelu_value(hidden).astype(BF), down[...])
    return qkv, mixed, w2, hidden, w3


def word_heads(qkv, row, rows, pair):
    return (qkv[row : row + rows, t * 512 + pair * LANES : t * 512 + (pair + 1) * LANES] for t in range(3))


def await_one(coming, k):
    if coming is not None:
        coming[k].wait()


def word_backward_body(grad, w1, qkv, w2, hidden, upper, down, gain, shift, allowed, vectors):
    low_2 = grad.astype(BF)
    act, slope = gelu_both(hidden)
    by_hidden = (slope * nn(low_2, down[...])).astype(BF)
    hat, root = norm_parts(w2)
    normed_2 = (hat * gain[1:2] + shift[1:2]).astype(BF)
    back, by_gain, by_shift = norm_back(nn(by_hidden, upper[2048:4096, :]), hat, root, gain[1:2])
    grad = grad + back
    vectors[1:2, :] = by_gain
    vectors[3:4, :] = by_shift
    low_1 = grad.astype(BF)
    by_mixed = nn(low_1, upper[1536:2048, :]).astype(BF)
    rows = w1.shape[0] // len(allowed)
    sides = []
    for r, pairs in enumerate(allowed):
        by_q, by_k, by_v = [], [], []
        for pair in range(4):
            q, k, v = word_heads(qkv, r * rows, rows, pair)
            keys = two_heads(k)
            attend = word_attend(q, keys, pairs)
            g = by_mixed[r * rows : (r + 1) * rows, pair * LANES : (pair + 1) * LANES]
            by_attend = nt(g, two_heads(v))
            product = attend * by_attend
            by_scores = (product - attend * by_half(product, jnp.sum, 0.0)).astype(BF)
            by_v.append(join_heads(tn(attend.astype(BF), g)))
            by_q.append(nn(by_scores, keys) * 0.125)
            by_k.append(join_heads(tn(by_scores, q)) * 0.125)
        sides.append(jnp.concatenate(by_q + by_k + by_v, axis=1))
    by_qkv = jnp.concatenate(sides, axis=0).astype(BF)
    hat, root = norm_parts(w1)
    normed_1 = (hat * gain[0:1] + shift[0:1]).astype(BF)
    back, by_gain, by_shift = norm_back(nn(by_qkv, upper[0:1536, :]), hat, root, gain[0:1])
    vectors[0:1, :] = by_gain
    vectors[2:3, :] = by_shift
    return grad + back, (normed_1, by_qkv, low_1, normed_2, by_hidden, act.astype(BF), low_2)


FACTORS = (512, 1536, 512, 512, 2048, 2048, 512)


def word_weights_kernel(firsts, me, mixed_0, mixed_1, *refs):
    normed_1, by_qkv, low_1, normed_2, by_hidden, act, low_2, keep_out, send_out, keep, send, sems = refs
    leaving = []

    def leave(row, rows):
        span = pl.ds(row, rows)
        k = len(leaving)
        leaving.extend(
            begin(
                [
                    (a.at[:, span], b.at[:, span], sems.at[k + n])
                    for n, (a, b) in enumerate(((send, send_out), (keep, keep_out)))
                ]
            )
        )

    mw, my, mc = me[0], me[1] >> 1, me[1] & 1
    mixed = jnp.where(me[2] == 0, mixed_0[...], mixed_1[...])

    def put(w, row, rows, blocks):
        for y in range(2):
            at = place(w ^ mw, y ^ my, firsts[row // 384])
            zero, one = blocks(2 * y), blocks(2 * y + 1)
            keep[at, row : row + rows, :] = jnp.where(mc == 0, zero, one)
            send[at, row : row + rows, :] = jnp.where(mc == 0, one, zero)

    for pair in range(4):
        columns = slice(pair * LANES, (pair + 1) * LANES)
        part = tn(low_2[:, columns], act[...]).astype(BF)
        for k in range(2):
            for t in range(4):
                put(
                    2 * pair + k,
                    W_DOWN[0] + 64 * t,
                    64,
                    lambda n: part[k * 64 : k * 64 + 64, n * 512 + t * LANES : n * 512 + (t + 1) * LANES],
                )
    leave(*(W_DOWN[0], 256))
    for w in range(8):
        part = tn(by_hidden[:, w * 256 : (w + 1) * 256], normed_2[...]).astype(BF)
        for k in range(2):
            put(
                w,
                W_UP[0] + 128 * k,
                128,
                lambda n: part[k * 128 : k * 128 + 128, n * LANES : (n + 1) * LANES],
            )
    leave(*W_UP)
    for pair in range(4):
        columns = slice(pair * LANES, (pair + 1) * LANES)
        part = tn(low_1[:, columns], mixed).astype(BF)
        for k in range(2):
            put(
                2 * pair + k,
                W_OUT[0],
                64,
                lambda n: part[k * 64 : k * 64 + 64, n * LANES : (n + 1) * LANES],
            )
    leave(*W_OUT)
    for pair in range(4):
        part = tn(by_qkv[:, pair * 384 : (pair + 1) * 384], normed_1[...]).astype(BF)
        for k in range(2):
            put(
                2 * pair + k,
                W_QKV[0],
                192,
                lambda n: part[k * 192 : (k + 1) * 192, n * LANES : (n + 1) * LANES],
            )
    leave(*W_QKV)
    finish(leaving)


def word_weights(firsts, me, mixed_0, mixed_1, factors):
    return pl.pallas_call(
        partial(word_weights_kernel, firsts),
        in_specs=[smem] + [vmem] * 9,
        out_specs=[anywhere] * 2,
        out_shape=[whole((16, W_ROWS, LANES), BF)] * 2,
        scratch_shapes=[pltpu.VMEM((16, W_ROWS, LANES), BF)] * 2 + [pltpu.SemaphoreType.DMA((8,))],
        compiler_params=pltpu.CompilerParams(vmem_limit_bytes=VMEM),
        cost_estimate=cost(2e9, 9e6),
    )(me, mixed_0, mixed_1, *factors)


def joined(refs):
    return jnp.concatenate([ref[...] for ref in refs], axis=0) if len(refs) > 1 else refs[0][...]


def swapped(x, count):
    half = x.shape[0] // 2
    return jnp.concatenate([x[half:], x[:half]], axis=0) if count == 2 else x


UPPER, DOWN = (4096, 512), (512, 2048)
word_scratch = [pltpu.SemaphoreType.DMA((4,))]


def word_fetch_kernel(me, *refs):
    *parts, upper, down, sems = refs
    finish(fetch_word(me, parts, upper, down, sems))


def word_fetch(me, parts):
    return pl.pallas_call(
        word_fetch_kernel,
        in_specs=[smem] + [anywhere] * 16,
        out_specs=[vmem] * 2,
        out_shape=[whole(UPPER, BF), whole(DOWN, BF)],
        scratch_shapes=word_scratch,
        compiler_params=pltpu.CompilerParams(vmem_limit_bytes=VMEM),
    )(me, *parts)


def word_call(kernel, count, tables, operands, outs, scratch, flops, alias=None):
    return pl.pallas_call(
        partial(kernel, count),
        in_specs=[smem] * len(tables) + [anywhere if x.shape[1:] == (W_ROWS, LANES) else vmem for x in operands],
        out_specs=[vmem] * len(outs),
        out_shape=[whole(shape, dtype) for shape, dtype in outs],
        scratch_shapes=scratch,
        input_output_aliases=alias or {},
        compiler_params=pltpu.CompilerParams(vmem_limit_bytes=VMEM),
        cost_estimate=cost(flops, 16e6),
    )(*tables, *operands)


def word_first_kernel(count, me, *refs):
    docs, states, deltas, parts = refs[:count], refs[count : 2 * count], refs[2 * count : 3 * count], refs[3 * count :]
    gain, shift, w1_out, qkv_out, mixed_out, w2_out, hidden_out, w3_out, upper, down, sems = parts[16:]
    coming = fetch_word(me, parts[:16], upper, down, sems)

    @pl.when(me[2] == 0)
    def _():
        w1 = jnp.concatenate([a[0].astype(F32) + b[...] for a, b in zip(states, deltas)], axis=0)
        w1_out[...] = w1
        allowed = [word_allowed(d, w1.shape[0] // count) for d in docs]
        qkv, mixed, w2, hidden, w3 = word_forward_body(w1, coming, upper, down, gain[0], shift[0], allowed)
        qkv_out[...] = qkv
        mixed_out[...] = mixed
        w2_out[...] = w2
        hidden_out[...] = hidden
        w3_out[...] = w3

    @pl.when(me[2] != 0)
    def _():
        finish(coming)
        w3_out[...] = jnp.zeros(w3_out.shape, F32)


def word_first(me, docs, states, deltas, parts, gain, shift):
    count = len(docs)
    words = count * deltas[0].shape[0]
    shapes = [(512, F32), (1536, BF), (512, BF), (512, F32), (2048, F32), (512, F32)]
    return word_call(
        word_first_kernel,
        count,
        [me, *docs],
        [*states, *deltas, *parts, gain, shift],
        [((words, c), t) for c, t in shapes] + [(UPPER, BF), (DOWN, BF)],
        word_scratch,
        1e9,
    )


def word_last_kernel(count, me, *refs):
    docs, w_in, deltas = refs[:count], refs[count], refs[count + 1 : 2 * count + 1]
    cots, parts = refs[2 * count + 1 : 3 * count + 1], refs[3 * count + 1 :]
    upper, down, gain, shift, out_own, out_other, grad_out, vectors, mixed_out = parts[:9]
    factors = parts[9:]
    vectors[...] = jnp.zeros(vectors.shape, F32)

    @pl.when(me[2] == 1)
    def _():
        w1 = swapped(w_in[...], count) + joined(deltas)
        rows = w1.shape[0] // count
        allowed = [word_allowed(d, rows) for d in docs]
        gains, shifts = gain[1], shift[1]
        qkv, mixed, w2, hidden, w3 = word_forward_body(w1, None, upper, down, gains, shifts, allowed)
        out_own[...] = w3[:rows].astype(BF)
        out_other[...] = w3[(count - 1) * rows :].astype(BF)
        grad = jnp.concatenate([c[1].astype(F32) for c in cots], axis=0)
        mixed_out[...] = mixed
        grad, made = word_backward_body(grad, w1, qkv, w2, hidden, upper, down, gains, shifts, allowed, vectors)
        grad_out[...] = grad
        for ref, value in zip(factors, made):
            ref[...] = value

    @pl.when(me[2] != 1)
    def _():
        for ref in (out_own, out_other, grad_out):
            ref[...] = jnp.zeros(ref.shape, ref.dtype)


def word_last(me, docs, w_in, deltas, cots, mats, gain, shift):
    count = len(docs)
    words = w_in.shape[0]
    row = words // count
    return word_call(
        word_last_kernel,
        count,
        [me, *docs],
        [w_in, *deltas, *cots, *mats, gain, shift],
        [((row, 512), BF)] * 2
        + [((words, 512), F32), ((8, 512), F32), ((words, 512), BF)]
        + [((words, c), BF) for c in FACTORS],
        [],
        2e9,
    )


def word_back_kernel(count, me, *refs):
    docs, (grad_in, w1, qkv, w2, hidden), parts = refs[:count], refs[count : count + 5], refs[count + 5 :]
    upper, down, gain, shift = parts[:4]
    held, parts_out = parts[4:11], parts[11:]
    grad_own, grad_other, vectors = parts_out[:3]
    factors = parts_out[3:]
    vectors[...] = jnp.zeros(vectors.shape, F32)

    @pl.when(me[2] == 0)
    def _():
        rows = w1.shape[0] // count
        grad, made = word_backward_body(
            swapped(grad_in[...], count),
            w1[...],
            qkv[...],
            w2[...],
            hidden[...],
            upper,
            down,
            gain[0],
            shift[0],
            [word_allowed(d, rows) for d in docs],
            vectors,
        )
        grad_own[...] = grad[:rows]
        grad_other[...] = grad[(count - 1) * rows :]
        for ref, value in zip(factors, made):
            ref[...] = value

    @pl.when(me[2] != 0)
    def _():
        for ref in (grad_own, grad_other):
            ref[...] = jnp.zeros(ref.shape, F32)
        for ref, value in zip(factors, held):
            ref[...] = value[...]


def word_back(me, docs, grad, saved, mats, gain, shift, held):
    count = len(docs)
    words = grad.shape[0]
    return word_call(
        word_back_kernel,
        count,
        [me, *docs],
        [grad, *saved, *mats, gain, shift, *held],
        [((words // count, 512), F32)] * 2 + [((8, 512), F32)] + [((words, c), BF) for c in FACTORS],
        [],
        2e9,
    )


def swap(x, axis, flip):
    return lax.ppermute(x, axis, [(k, k ^ flip) for k in range(lax.axis_size(axis))])


def over_x(x):
    return swap(x, "wide", 1)


def over_y(x):
    return swap(x, "narrow", 2)


def over_core(x):
    return swap(x, "narrow", 1)


def over_pair(x):
    return swap(x, "wide", 2)


def after(x, *others):
    return lax.optimization_barrier((x, *others))[0]


def add(*terms):
    total = terms[0].astype(F32)
    for term in terms[1:]:
        total = total + term.astype(F32)
    return total.astype(BF)


def gather_z(block):
    return jnp.stack([block] + [swap(block, "wide", 2 * k) for k in (1, 2, 3)])


def gather_one(z, x_first):
    return jnp.concatenate([z, (over_x if x_first else over_y)(z)], axis=0)


def gather_two(first, x_first):
    return first, (over_y if x_first else over_x)(first)


def gather_core(parts):
    return (*parts, *[over_core(part) for part in parts])


def two(x, x_first):
    return (over_y if x_first else over_x)(x)


def one(x, x_first):
    return (over_x if x_first else over_y)(x)


def cut(matrices, table):
    qkv, out, up, down, proj, *words = matrices

    def split(m):
        r, c = m.shape
        return m.T.reshape(8, c // 8, 4, r // 4).transpose(0, 2, 1, 3)

    def paired(m):
        b = split(m)
        c = b.shape[2]
        return b.reshape(8, 4, 2, c // 2, 64).transpose(0, 1, 3, 2, 4).reshape(8, 4, c // 2, LANES)

    def tiled(m):
        b = split(m)
        c, r = b.shape[2:]
        return b.reshape(8, 4, c, r // LANES, LANES).transpose(0, 1, 3, 2, 4).reshape(8, 4, -1, LANES)

    char = [paired(qkv), paired(out), paired(up), paired(proj), tiled(down)]
    if table is not None:
        char.append(table.reshape(8, 4, 8, 2, LANES).transpose(0, 1, 3, 2, 4).reshape(8, 4, 16, LANES))
    word = [tiled(m) for m in words]
    return [ordered(jnp.concatenate(x, axis=2)) for x in (char, word)]


def ordered(blocks):
    b = blocks.reshape(4, 2, 2, 2, *blocks.shape[2:]).transpose(3, 2, 1, 0, 4, 5)
    return b.reshape(32, *blocks.shape[2:])


def uncut(blocks, is_char, with_table):
    b = blocks.reshape(2, 2, 2, 4, *blocks.shape[1:]).transpose(3, 2, 1, 0, 4, 5)
    b = b.reshape(8, 4, *blocks.shape[1:])

    def joined(x):
        c, r = x.shape[2:]
        return x.transpose(0, 2, 1, 3).reshape(8 * c, 4 * r).T

    def paired(x):
        c = x.shape[2]
        return joined(x.reshape(8, 4, c, 2, 64).transpose(0, 1, 3, 2, 4).reshape(8, 4, 2 * c, 64))

    def tiled(x, tiles):
        c = x.shape[2] // tiles
        return joined(x.reshape(8, 4, tiles, c, LANES).transpose(0, 1, 3, 2, 4).reshape(8, 4, c, tiles * LANES))

    def rows(span, count=None):
        return b[:, :, span[0] : span[0] + (count or span[1])]

    if not is_char:
        return [tiled(rows(W_QKV), 1), tiled(rows(W_OUT), 1), tiled(rows(W_UP), 1), tiled(rows(W_DOWN, 256), 4)], None
    table = None
    if with_table:
        table = rows(C_EMB).reshape(32, 2, 8, LANES).transpose(0, 2, 1, 3).reshape(256, 256)
    qkv, out, up, proj = (paired(rows(span)) for span in C_PAIRED)
    return [qkv, out, up, tiled(rows(C_DOWN, 64), 2), proj], table


def over_xy(x):
    flip = lax.axis_size("narrow") + 2
    return lax.ppermute(x, ("wide", "narrow"), [(k, k ^ flip) for k in range(lax.axis_size(("wide", "narrow")))])


together = lax.optimization_barrier


def whole_chip(z):
    return [z, over_x(z), over_y(z), over_xy(z)]


def both_cores(near):
    near = jnp.concatenate(near, axis=0)
    return near, over_core(near)


def direct_program(
    word_states, character_ids, word_lengths, doc_lengths, embedding, weights, vectors, char_cot, word_cot
):
    char_gains, char_shifts, pool_query, word_gains, word_shifts = vectors
    vectors_char = (char_gains, char_shifts, pool_query)
    vectors_word = (word_gains, word_shifts)
    width = char_cot.shape[3]
    wide = lax.axis_index("wide")
    me = jnp.stack([wide, lax.axis_index("narrow"), (wide >> 1) & 1]).astype(jnp.int32)
    firsts = (True, False)
    f0, f1 = firsts
    c01, mine, theirs = pack(me, weights, embedding)
    pair = jnp.stack([word_states[0], word_cot[0]])
    ids = character_ids.reshape(-1, LANES)
    word = jnp.stack([mine, over_pair(theirs)])
    along = [c01] + [swap(c01, "wide", 2 * k) for k in (1, 2, 3)]
    z0 = jnp.stack([c[:HELD_0] for c in along])
    z0, along, word, ids, pair = together((z0, along, word, ids, pair))
    z1 = jnp.stack([c[HELD_0:] for c in along])
    near_0 = whole_chip(z0)
    far = swap(word, "wide", 4)
    word_near = whole_chip(word)
    near_0, far, word_near, z1 = together((near_0, far, word_near, z1))
    char_0 = both_cores(near_0)
    far_near = whole_chip(far)
    word_cores = [over_core(part) for part in word_near]
    char_0, word_cores, pair, doc_lengths = together((char_0, word_cores, pair, doc_lengths))
    other_pair = over_pair(pair)
    other_docs = over_pair(doc_lengths)
    saved_0, delta_0, mats_0 = char_forward(True, True, me, word_lengths, ids, char_0, *vectors_char)
    delta_0, far_near, z1, other_pair, other_docs = together((delta_0, far_near, z1, other_pair, other_docs))
    far_cores = [over_core(part) for part in far_near]
    other_delta_0 = over_pair(delta_0)
    far_cores, other_delta_0, z1 = together((far_cores, other_delta_0, z1))
    near_1 = whole_chip(z1)
    word_parts = [*word_near, *far_near, *word_cores, *far_cores]
    docs = [doc_lengths, other_docs]
    pairs = [pair, other_pair]
    *word_saved, w3, upper, down = word_first(me, docs, pairs, [delta_0, other_delta_0], word_parts, *vectors_word)
    near_1, w3 = together((near_1, w3))
    char_1 = both_cores(near_1)
    char_1, states = together((char_1, saved_0[4]))
    saved_1, delta_1, mats_1, char_out = char_forward(False, True, me, word_lengths, states, char_1, *vectors_char)
    other_w3 = over_pair(w3)
    other_delta_1 = over_pair(delta_1)
    out_own, out_other, grad_1, word_vec_1, mixed_1, *held = word_last(
        me, docs, other_w3, [delta_1, other_delta_1], pairs, (upper, down), *vectors_word
    )
    w1, qkv, mixed_0, w2, hidden = word_saved
    got_1 = over_pair(grad_1)
    grad_own, grad_other, word_vec_0, *factors = word_back(
        me, docs, got_1, (w1, qkv, w2, hidden), (upper, down), *vectors_word, held
    )
    keep, send = word_weights(firsts, me, mixed_0, mixed_1, factors)
    got = over_core(send)
    got_0 = over_pair(grad_other)
    out_other = over_pair(out_other)
    cot = char_cot[0].reshape(-1, width)
    cot, keep, grad_1, got_1 = together((cot, keep, grad_1, got_1))
    grad, keep_f1, send_f1, vec_1 = char_feed(
        False, True, me, word_lengths, cot, (grad_1, got_1), (0, 1), saved_1[3:], mats_1, vectors_char
    )
    got, got_0, out_other, grad = together((got, got_0, out_other, grad))
    pieces = []
    for h in range(2):
        span = slice(384 * h, 384 * h + 384)
        pieces += [add(keep[k : k + 8, span], got[k : k + 8, span]) for k in (0, 8)]
    pieces, grad = together((pieces, grad))
    pieces[1], pieces[3] = two(pieces[1], f0), two(pieces[3], f1)
    grad, keep_1, send_1, char_vec_1 = char_mix(
        False, True, me, word_lengths, grad, saved_1[:3], mats_1, vectors_char, (vec_1, keep_f1, send_f1)
    )
    pieces, grad, send_1, keep_1 = together((pieces, grad, send_1, keep_1))
    got = over_core(send_1)
    pieces = [add(a[k : k + 4], b[k : k + 4]) for a, b in (pieces[:2], pieces[2:]) for k in (0, 4)]
    pieces, grad, got, keep_1 = together((pieces, grad, got, keep_1))
    pieces[1], pieces[3] = one(pieces[1], f0), one(pieces[3], f1)
    own_1, *away_1 = fold_cores(keep_1, got)
    own_1, away_1, grad = together((own_1, away_1, grad))
    away_1 = [over_x(away_1[0]), over_y(away_1[1]), over_xy(away_1[2])]
    word_grad, grad, keep_f0, send_f0, vec_0 = char_feed(
        True, True, me, word_lengths, grad, (grad_own, got_0), (0, 0), saved_0[3:], mats_0, vectors_char
    )
    pieces, grad, away_1, send_f0, keep_f0 = together((pieces, grad, away_1, send_f0, keep_f0))
    got_f0 = over_core(send_f0)
    ours, away = (
        jnp.concatenate([add(a[k : k + 2], b[k : k + 2]) for a, b in (pieces[:2], pieces[2:])], axis=1) for k in (0, 2)
    )
    second = fold_chips(own_1, *away_1)
    ours, away, second, grad = together((ours, away, second, grad))
    away = swap(away, "wide", 4)
    second = [second[0]] + [swap(second[k], "wide", 2 * k) for k in (1, 2, 3)]
    keep_0, send_0, _ = char_mix(
        True,
        True,
        me,
        word_lengths,
        grad,
        saved_0[:3],
        mats_0,
        vectors_char,
        (vec_0, ids, word_vec_0, word_vec_1, char_vec_1),
    )
    second, got_f0, send_0, keep_0 = together((second, got_f0, send_0, keep_0))
    got_0 = over_core(send_0)
    own_0, *away_0 = fold_one(keep_f0, got_f0, keep_0, got_0, send_0)
    ours, away = (add(ours[k : k + 1], away[k : k + 1]) for k in (0, 1))
    sent = away_0[0]
    moved = (over_x(away_0[0]), over_y(away_0[1]), over_xy(away_0[2]))
    away = over_pair(away)
    moved, ours = together((moved, ours))
    own_0, *away_0 = fold_two(own_0, sent, *moved)
    first = [own_0, away_0[0]] + [swap(away_0[k - 1], "wide", 2 * k) for k in (1, 2, 3)]
    out = unpack(me, [*first, *second, ours, away, out_own, out_other], weights, embedding, vectors)
    return (char_out, out[-1], word_grad, out[9], *out[:9], *out[10:15])


def plain_program(
    word_states, character_ids, word_lengths, doc_lengths, embedding, weights, vectors, char_cot, word_cot
):
    char_gains, char_shifts, pool_query, word_gains, word_shifts = vectors
    width = char_cot.shape[3]
    both = ("wide", "narrow")
    firsts = (True, True)
    at = [jnp.array([0, 0, layer], jnp.int32) for layer in range(2)]
    table = lax.all_gather(embedding, both, axis=0, tiled=True)
    full = [lax.all_gather(lax.all_gather(m, "narrow", axis=1, tiled=True), "wide", axis=2, tiled=True) for m in weights]
    chars, words = [], []
    for layer in range(2):
        char, word = cut([m[layer] for m in full], table if layer == 0 else None)
        chars.append([char[8 * k : 8 * k + 8] for k in range(4)])
        words.append([word[k : k + 2] for c in (0, 16) for z in (0, 2) for k in range(c + z, c + z + 16, 4)])
    ids = character_ids.reshape(-1, LANES)
    vectors_char = (char_gains, char_shifts, pool_query)
    vectors_word = (word_gains, word_shifts)
    saved_0, delta_0, mats_0 = char_forward(True, True, at[0], word_lengths, ids, chars[0], *vectors_char)
    states = saved_0[4]
    saved_1, delta_1, mats_1, char_out = char_forward(False, True, at[0], word_lengths, states, chars[1], *vectors_char)
    docs = [doc_lengths]
    pair = [jnp.stack([word_states[0], word_cot[0]])]
    *word_saved, w3, upper, down = word_first(at[0], docs, pair, [delta_0], words[0], *vectors_word)
    word_out, _, grad_1, word_vec_1, mixed_1, *held = word_last(
        at[1], docs, w3, [delta_1], pair, word_fetch(at[1], words[1]), *vectors_word
    )
    word_mats = (upper, down)
    w1, qkv, mixed_0, w2, hidden = word_saved
    grad_0, _, word_vec_0, *factors = word_back(
        at[0], docs, grad_1, (w1, qkv, w2, hidden), word_mats, *vectors_word, held
    )
    words = [word_weights(firsts, at[0], mixed, mixed, made) for mixed, made in ((mixed_0, factors), (mixed_1, held))]
    cot = char_cot[0].reshape(-1, width)
    grad, keep_f, send_f, vec_1 = char_feed(
        False, True, at[1], word_lengths, cot, (grad_1, grad_1), (0, 0), saved_1[3:], mats_1, vectors_char
    )
    grad, keep_1, send_1, char_vec_1 = char_mix(
        False, True, at[1], word_lengths, grad, saved_1[:3], mats_1, vectors_char, (vec_1, keep_f, send_f)
    )
    word_grad, grad, keep_f, send_f, vec_0 = char_feed(
        True, True, at[0], word_lengths, grad, (grad_0, grad_0), (0, 0), saved_0[3:], mats_0, vectors_char
    )
    keep_0, send_0, _ = char_mix(
        True,
        True,
        at[0],
        word_lengths,
        grad,
        saved_0[:3],
        mats_0,
        vectors_char,
        (vec_0, ids, word_vec_0, word_vec_1, char_vec_1),
    )
    summed = lax.psum(whole_vector(send_0[16:].reshape(-1, LANES)[:128]), both)
    keep_0, send_0 = (
        jnp.concatenate([a[:16, :64], f, a[:16, 64:]], axis=1) for a, f in ((keep_0, keep_f), (send_0, send_f))
    )
    blocks = ((keep_0, send_0), (keep_1, send_1), *words)
    full = [uncut(jnp.concatenate(g), k < 2, k == 0) for k, g in enumerate(blocks)]
    matrix_grads = [
        lax.psum_scatter(
            lax.psum_scatter(jnp.stack([a, b]), "wide", scatter_dimension=2, tiled=True),
            "narrow",
            scatter_dimension=1,
            tiled=True,
        ).astype(F32)
        for a, b in zip(full[0][0] + full[2][0], full[1][0] + full[3][0])
    ]
    embedding_grad = lax.psum_scatter(full[0][1].astype(F32), both, scatter_dimension=0, tiled=True)
    word_vectors = summed[:32].reshape(4, 2, 4, LANES).transpose(1, 2, 0, 3).reshape(2, 4, 512)
    char_vectors = summed[32:].reshape(2, 2, 8, LANES).transpose(1, 2, 0, 3).reshape(2, 8, 256)
    return (
        char_out,
        word_out,
        word_grad,
        embedding_grad,
        *matrix_grads,
        char_vectors[:, 0:2],
        char_vectors[:, 2:4],
        char_vectors[:, 4],
        word_vectors[:, 0:2],
        word_vectors[:, 2:4],
    )


def on_device(direct, *arguments):
    char_cot, word_cot = arguments[19:]
    program = direct_program if direct else plain_program
    char_out, word_out, word_grad, *rest = program(
        *arguments[:5], arguments[5:14], arguments[14:19], char_cot, word_cot
    )
    return (char_out.reshape(char_cot.shape), word_out[None], word_grad[None], *rest)


def solution(mesh):
    rows = ("wide", "narrow")
    matrix = P(None, "narrow", "wide")
    by_rows = P(rows)
    return jax.shard_map(
        partial(on_device, mesh.shape["wide"] == 8 and mesh.shape["narrow"] == 4),
        mesh=mesh,
        in_specs=(by_rows,) * 5 + (matrix,) * 9 + (P(),) * 5 + (by_rows,) * 2,
        out_specs=(by_rows,) * 4 + (matrix,) * 9 + (P(),) * 5,
        check_vma=False,
    )
```

```python
from functools import partial

import jax
import jax.numpy as jnp
from jax import lax
from jax.experimental import pallas as pl
from jax.experimental.pallas import tpu as pltpu
from jax.sharding import PartitionSpec as P

F32 = jnp.float32
BF = jnp.bfloat16
SLOTS = 16
masked_score = -1e30
ROOT = 0.7978845608028654
CUBE = 0.044715
LANES = 128
C_QKV, C_OUT, C_UP, C_PROJ, C_DOWN, C_EMB = (0, 48), (48, 16), (64, 64), (128, 32), (160, 32), (224, 16)
C_PAIRED = (C_QKV, C_OUT, C_UP, C_PROJ)
C_ROWS = 224
HELD_0 = C_ROWS + 16
W_QKV, W_OUT, W_UP, W_DOWN = (0, 192), (192, 64), (256, 256), (512, 64)
W_ROWS = 768
CHUNK = 512
VMEM, SMALL, LARGE = 24 << 20, 12 << 20, 60 << 20
COST_FORWARD, COST_FEED, COST_MIX = 2e9, 2e9, 2e9
A_SPAN, F_SPAN = (0, 64), (64, 160)
E_ROWS = 16


def dot(left, right, l, r):
    return lax.dot_general(left, right, (((l,), (r,)), ((), ())), preferred_element_type=F32)


def nn(left, right):
    return dot(left, right, 1, 0)


def nt(left, right):
    return dot(left, right, 1, 1)


def tn(left, right):
    return dot(left, right, 0, 0)


def iota(shape, dim):
    return lax.broadcasted_iota(jnp.int32, shape, dim)


def norm_parts(states):
    centre = states - jnp.mean(states, axis=-1, keepdims=True)
    spread = jnp.mean(centre * centre, axis=-1, keepdims=True)
    root = lax.rsqrt(spread + 1e-05)
    return centre * root, root


def norm_back(grad, hat, root, gain):
    scaled = grad * gain
    inner = scaled - jnp.mean(scaled, axis=-1, keepdims=True)
    back = root * (inner - hat * jnp.mean(scaled * hat, axis=-1, keepdims=True))
    return back, jnp.sum(grad * hat, axis=0, keepdims=True), jnp.sum(grad, axis=0, keepdims=True)


def gelu_value(h):
    return 0.5 * h * (1.0 + jnp.tanh(ROOT * (h + CUBE * h * h * h)))


def gelu_both(h):
    square = h * h
    t = jnp.tanh(ROOT * (h + CUBE * square * h))
    half = 0.5 * (1.0 + t)
    slope = half + 0.5 * h * (1.0 - t * t) * (ROOT * (1.0 + 3.0 * CUBE * square))
    return h * half, slope


def softmax_rows(scores):
    shifted = jnp.exp(scores - jnp.max(scores, axis=-1, keepdims=True))
    return shifted / jnp.sum(shifted, axis=-1, keepdims=True)


def low_half(shape):
    return iota(shape, len(shape) - 1) % LANES < 64


def two_heads(x):
    low = low_half(x.shape)
    zero = jnp.zeros_like(x)
    return jnp.concatenate([jnp.where(low, x, zero), jnp.where(low, zero, x)], axis=0)


def join_heads(x):
    k = x.shape[0] // 2
    return jnp.where(low_half((k, LANES)), x[:k], x[k:])


def place(rw, ry, x_first):
    rx, rz = rw & 1, rw >> 1
    return ry * 8 + rx * 4 + rz if x_first else rx * 8 + ry * 4 + rz


def unplace(q, s, x_first):
    a, rz = s >> 2, s & 3
    rx, ry = (a, q) if x_first else (q, a)
    return rz * 2 + rx, ry


def begin(copies):
    copies = [pltpu.make_async_copy(*c) for c in copies]
    for copy in copies:
        copy.start()
    return copies


def finish(copies):
    for copy in copies:
        copy.wait()


def pack_kernel(*refs):
    c0, mine, theirs = refs[10:13]
    cq, co, cu, cd, cp, wq, wo, wu, wd, emb = refs[13:23]
    finish(begin([(a, b, refs[23].at[k]) for k, (a, b) in enumerate(zip(refs[:10], refs[13:23]))]))

    def turned(x):
        return x.astype(F32).T

    for layer, (c, base) in enumerate(((c0, 0), (mine, W_ROWS))):
        for t, (row, rows) in zip((turned(cq[layer]), co[layer], turned(cu[layer]), turned(cp[layer])), C_PAIRED):
            t = t.astype(F32)
            c[base + row : base + row + rows, :] = jnp.concatenate([t[:rows], t[rows:]], axis=1).astype(BF)
        for k in range(2):
            row = base + C_DOWN[0] + 32 * k
            c[row : row + 32, :] = cd[layer, :, k * LANES : (k + 1) * LANES]
    e = emb[...].astype(F32)
    theirs[W_ROWS:, :] = mine[W_ROWS:, :]
    c0[C_EMB[0] : C_EMB[0] + 16, :] = jnp.concatenate([e[:, :LANES], e[:, LANES:]], axis=0).astype(BF)
    own = (lax.axis_index("wide") >> 1) & 1
    for layer, w in ((own, mine), (1 - own, theirs)):
        w[W_QKV[0] : W_QKV[0] + 192, :] = wq[layer]
        w[W_OUT[0] : W_OUT[0] + 64, :] = wo[layer]
        w[W_UP[0] : W_UP[0] + 256, :] = turned(wu[layer]).astype(BF)
        for k in range(4):
            row = W_DOWN[0] + 64 * k
            w[row : row + 64, :] = wd[layer, :, k * LANES : (k + 1) * LANES]


def whole(shape, dtype):
    return jax.ShapeDtypeStruct(shape, dtype)


def cost(flops, moved):
    return pl.CostEstimate(flops=int(flops), bytes_accessed=int(moved), transcendentals=0)


smem = pl.BlockSpec(memory_space=pltpu.SMEM)
vmem = pl.BlockSpec(memory_space=pltpu.VMEM)
anywhere = pl.BlockSpec(memory_space=pl.ANY)
TURNED = (1, 3, 5, 6, 8)


def pack(weights, embedding):
    weights = [m.swapaxes(1, 2) if k in TURNED else m for k, m in enumerate(weights)]
    return pl.pallas_call(
        pack_kernel,
        in_specs=[anywhere] * 10,
        out_shape=(
            whole((HELD_0, LANES), BF),
            whole((W_ROWS + C_ROWS, LANES), BF),
            whole((W_ROWS + C_ROWS, LANES), BF),
        ),
        scratch_shapes=[pltpu.VMEM(m.shape, BF) for m in (*weights, embedding)] + [pltpu.SemaphoreType.DMA((10,))],
        compiler_params=pltpu.CompilerParams(vmem_limit_bytes=LARGE),
        cost_estimate=cost(0, 4e6),
    )(*weights, embedding)


def split_vector(x):
    high = x.astype(BF)
    return jnp.concatenate([high, (x - high.astype(F32)).astype(BF)], axis=0)


def whole_vector(x):
    return x[:64].astype(F32) + x[64:].astype(F32)


def unpack_kernel(me, *refs):
    first, second, own_word, other_word, own_out, other_out = refs[:5], refs[5:9], *refs[9:13]
    cq, co, cu, cd, cp, wq, wo, wu, wd, emb, cg, cs, pq, wg, ws, word_out = refs[13:]
    layer_now = me[2]
    word_out[...] = jnp.where(layer_now == 1, own_out[...], other_out[...])
    c0 = [first[k][0 : C_ROWS + 16, :].astype(F32) for k in (0, 2, 3, 4)]
    c0 = (c0[0] + c0[1]) + (c0[2] + c0[3])
    c1 = (second[0][...].astype(F32) + second[1][...].astype(F32)) + (
        second[2][...].astype(F32) + second[3][...].astype(F32)
    )
    v = [whole_vector(ref[C_ROWS + 16 :, :]) for ref in first[1:5]]
    v = (v[0] + v[1]) + (v[2] + v[3])
    for layer, c in enumerate((c0, c1)):
        for k, ref, (row, rows) in zip((0, 1, 2, 4), (cq, co, cu, cp), C_PAIRED):
            t = c[row : row + rows, :]
            t = jnp.concatenate([t[:, :64], t[:, 64:]], axis=0)
            ref[layer] = t if k in TURNED else t.T
        for k in range(2):
            row = C_DOWN[0] + 32 * k
            cd[layer, :, k * LANES : (k + 1) * LANES] = c[row : row + 32, :]
        for t in range(4):
            row = 8 * t + 4 * layer
            wg[layer, :, t * LANES : (t + 1) * LANES] = v[row : row + 2]
            ws[layer, :, t * LANES : (t + 1) * LANES] = v[row + 2 : row + 4]
        for t in range(2):
            row = 32 + 16 * t + 8 * layer
            cg[layer, :, t * LANES : (t + 1) * LANES] = v[row : row + 2]
            cs[layer, :, t * LANES : (t + 1) * LANES] = v[row + 2 : row + 4]
            pq[layer : layer + 1, t * LANES : (t + 1) * LANES] = v[row + 4 : row + 5]
    e = c0[C_EMB[0] : C_EMB[0] + 16, :]
    emb[...] = jnp.concatenate([e[:8], e[8:]], axis=1)
    for layer, w in ((layer_now, own_word), (1 - layer_now, other_word)):
        wq[layer] = w[0, W_QKV[0] : W_QKV[0] + 192, :].astype(F32)
        wo[layer] = w[0, W_OUT[0] : W_OUT[0] + 64, :].astype(F32)
        wu[layer] = w[0, W_UP[0] : W_UP[0] + 256, :].astype(F32).T
        for k in range(4):
            row = W_DOWN[0] + 64 * k
            wd[layer, :, k * LANES : (k + 1) * LANES] = w[0, row : row + 64, :].astype(F32)


def unpack(me, blocks, weights, embedding, vectors):
    shapes = [m.shape for m in weights]
    shapes = [(a, c, b) if k in TURNED else (a, b, c) for k, (a, b, c) in enumerate(shapes)]
    shapes += [embedding.shape] + [v.shape for v in vectors]
    out = pl.pallas_call(
        unpack_kernel,
        in_specs=[smem] + [vmem] * len(blocks),
        out_shape=tuple(whole(x, F32) for x in shapes) + (whole(blocks[-1].shape, BF),),
        cost_estimate=cost(0, 8e6),
    )(me, *blocks)
    return [x.swapaxes(1, 2) if k in TURNED else x for k, x in enumerate(out)]


def fold_one_kernel(keep_f, got_f, keep_a, got_a, sent_a, ours, *away):
    vector = [jnp.concatenate([ref[16], ref[17, 0:48, :]], axis=0) for ref in (sent_a, got_a)]
    vector = split_vector(whole_vector(vector[0]) + whole_vector(vector[1]))
    for part, ref in enumerate((ours, *away)):
        for k in range(4):
            at, row = 4 * part + k, k * HELD_0
            ref[row : row + 64, :] = (keep_a[at, 0:64, :].astype(F32) + got_a[at, 0:64, :].astype(F32)).astype(BF)
            ref[row + 64 : row + 224, :] = (keep_f[at].astype(F32) + got_f[at].astype(F32)).astype(BF)
            ref[row + 224 : row + 240, :] = (
                keep_a[at, 64:80, :].astype(F32) + got_a[at, 64:80, :].astype(F32)
            ).astype(BF)
        if part > 0:
            ref[4 * HELD_0 :, :] = vector


def fold_one(*operands):
    return pl.pallas_call(
        fold_one_kernel,
        out_shape=[whole((4 * HELD_0, LANES), BF)] + [whole((4 * HELD_0 + 128, LANES), BF)] * 3,
        compiler_params=pltpu.CompilerParams(vmem_limit_bytes=SMALL),
        cost_estimate=cost(0, 4e6),
    )(*operands)


def fold_two_kernel(ours, sent, over_x, over_y, over_xy, own, *away):
    vector = [whole_vector(ref[4 * HELD_0 :, :]) for ref in (sent, over_x, over_y, over_xy)]
    vector = split_vector((vector[0] + vector[1]) + (vector[2] + vector[3]))
    for k, ref in enumerate((own, *away)):
        row = k * HELD_0
        near = [r[row : row + HELD_0, :].astype(F32) for r in (ours, over_x, over_y, over_xy)]
        ref[0:HELD_0, :] = ((near[0] + near[1]) + (near[2] + near[3])).astype(BF)
        if k > 0:
            ref[HELD_0:, :] = vector


def fold_two(*operands):
    return pl.pallas_call(
        fold_two_kernel,
        out_shape=[whole((HELD_0, LANES), BF)] + [whole((HELD_0 + 128, LANES), BF)] * 3,
        compiler_params=pltpu.CompilerParams(vmem_limit_bytes=SMALL),
        cost_estimate=cost(0, 4e6),
    )(*operands)


def fold_cores_kernel(keep, got, *out):
    for part, ref in enumerate(out):
        for k in range(4):
            ref[k] = (keep[4 * part + k].astype(F32) + got[4 * part + k].astype(F32)).astype(BF)


def fold_cores(keep, got):
    return pl.pallas_call(
        fold_cores_kernel,
        out_shape=[whole((4, *keep.shape[1:]), BF)] * 4,
        compiler_params=pltpu.CompilerParams(vmem_limit_bytes=SMALL),
        cost_estimate=cost(0, 4e6),
    )(keep, got)


def fold_chips_kernel(ours, over_x, over_y, over_xy, *out):
    for k, ref in enumerate(out):
        near = ours[k].astype(F32) + over_x[k].astype(F32)
        ref[...] = (near + (over_y[k].astype(F32) + over_xy[k].astype(F32))).astype(BF)


def fold_chips(*operands):
    return pl.pallas_call(
        fold_chips_kernel,
        out_shape=[whole(operands[0].shape[1:], BF)] * 4,
        compiler_params=pltpu.CompilerParams(vmem_limit_bytes=SMALL),
        cost_estimate=cost(0, 2e6),
    )(*operands)


def assemble(x_first, me, span, raw, mats):
    mw, my, mc = me[0], me[1] >> 1, me[1] & 1
    for w in range(8):
        for y in range(2):
            at = place(w ^ mw, y ^ my, x_first)
            cores = (mc * 16 + at, (1 - mc) * 16 + at)
            for ref, (row, rows) in zip(mats[:4], C_PAIRED):
                if ref is None:
                    continue
                row = row - span
                zero, one = (raw[k, row : row + rows, :] for k in cores)
                first = w * 2 * rows
                columns = slice(y * LANES, (y + 1) * LANES)
                ref[first : first + rows, columns] = jnp.concatenate([zero[:, :64], one[:, :64]], axis=1)
                ref[first + rows : first + 2 * rows, columns] = jnp.concatenate(
                    [zero[:, 64:], one[:, 64:]], axis=1
                )
            if mats[4] is None:
                continue
            for c, k in enumerate(cores):
                for t in range(2):
                    column = (2 * y + c) * 256 + t * LANES
                    row = C_DOWN[0] + 32 * t - span
                    mats[4][w * 32 : w * 32 + 32, column : column + LANES] = raw[k, row : row + 32, :]

def put_char(x_first, me, keep, send, span, mats):
    mw, my, mc = me[0], me[1] >> 1, me[1] & 1

    def put(at, row, rows, zero, one):
        row = row - span
        keep[at, row : row + rows, :] = jnp.where(mc == 0, zero, one)
        send[at, row : row + rows, :] = jnp.where(mc == 0, one, zero)

    for w in range(8):
        for y in range(2):
            at = place(w ^ mw, y ^ my, x_first)
            for ref, (row, rows) in zip(mats[:4], C_PAIRED):
                if ref is None:
                    continue
                columns = slice(y * LANES, (y + 1) * LANES)
                top = ref[w * 2 * rows : w * 2 * rows + rows, columns]
                bottom = ref[w * 2 * rows + rows : w * 2 * rows + 2 * rows, columns]
                put(
                    at,
                    row,
                    rows,
                    jnp.concatenate([top[:, :64], bottom[:, :64]], axis=1),
                    jnp.concatenate([top[:, 64:], bottom[:, 64:]], axis=1),
                )
            if mats[4] is None:
                continue
            for t in range(2):
                zero, one = (
                    mats[4][w * 32 : w * 32 + 32, (2 * y + c) * 256 + t * LANES : (2 * y + c) * 256 + (t + 1) * LANES]
                    for c in range(2)
                )
                put(at, C_DOWN[0] + 32 * t, 32, zero, one)


def char_positions(ids, me, x_first):
    device = ids >> 3
    rw = (device >> 2) ^ me[0]
    rn = (device & 3) ^ me[1]
    return ((rn & 1) * 16 + place(rw, rn >> 1, x_first)) * 16 + (ids & 7)


def valid_keys(lens, first):
    lane = iota((1, LANES), 1)
    length = jnp.zeros((1, LANES), jnp.int32)
    for k in range(8):
        length = jnp.where(lane // SLOTS == k, lens[0, first + k], length)
    return lane % SLOTS < length


def to_column(row):
    square = (LANES, LANES)
    return jnp.sum(jnp.where(iota(square, 0) == iota(square, 1), row, 0.0), axis=-1, keepdims=True)


def char_masks(lens, first):
    same = iota((LANES, LANES), 0) // SLOTS == iota((LANES, LANES), 1) // SLOTS
    valid = valid_keys(lens, first)
    return to_column(jnp.where(valid, 1.0, 0.0)), same & valid, same


def char_attend(q, keys, allowed):
    scores = jnp.where(allowed, nt(q, keys) * 0.125, masked_score)
    return jnp.concatenate([softmax_rows(scores[:, :LANES]), softmax_rows(scores[:, LANES:])], axis=1)


def by_head(x, reduce):
    k = x.shape[0] // 2
    return [reduce(x[h * k : (h + 1) * k], axis=0, keepdims=True) for h in range(2)]


def char_attend_turned(keys, q, allowed):
    scores = jnp.where(allowed, nt(keys, q) * 0.125, masked_score)
    k = scores.shape[0] // 2
    out = []
    for h in range(2):
        part = scores[h * k : (h + 1) * k]
        shifted = jnp.exp(part - jnp.max(part, axis=0, keepdims=True))
        out.append(shifted / jnp.sum(shifted, axis=0, keepdims=True))
    return jnp.concatenate(out, axis=0)


def pool_weights(states, query, valid):
    scores = jnp.sum(states * query, axis=-1, keepdims=True)
    scores = jnp.where(valid > 0.5, scores, masked_score).reshape(-1, SLOTS, 1)
    shifted = jnp.exp(scores - jnp.max(scores, axis=1, keepdims=True))
    return shifted / jnp.sum(shifted, axis=1, keepdims=True)


def of_layer(first, gain, shift, query):
    layer = 0 if first else 1
    return gain[layer], shift[layer], query[layer : layer + 1, :]


def part_copies(parts, raw, row, rows, at, sems):
    each = 32 // len(parts)
    return [
        (part.at[:, pl.ds(row, rows)], raw.at[pl.ds(each * k, each), pl.ds(at, rows)], sems.at[k])
        for k, part in enumerate(parts)
    ]


def char_forward_kernel(first, x_first, count, *refs):
    me, lens, source = refs[:3]
    parts, refs = refs[3 : 3 + count], refs[3 + count :]
    gain, shift, query = of_layer(first, *refs[:3])
    qkv_out, mixed_out, after_out, next_out, extra_out, pooled_out, delta_out = refs[3:10]
    mats, refs = refs[10:15], refs[15:]
    hidden_here, raw, table, sems_a, sems_f, sems_e = refs
    m_qkv, m_out, m_up, m_proj, m_down = mats
    rows_all = qkv_out.shape[0]
    near = begin(part_copies(parts, raw, 0, 64, 0, sems_a))
    if first:
        near += begin(part_copies(parts, raw, C_EMB[0], 16, C_EMB[0], sems_e))
    far = begin(part_copies(parts, raw, 64, 160, 64, sems_f))
    finish(near)
    assemble(x_first, me, 0, raw, (m_qkv, m_out, None, None, None))
    if first:
        for k in range(32):
            table[k * 16 : k * 16 + 16, :] = raw[k, C_EMB[0] : C_EMB[0] + 16, :]
    for chunk in range(rows_all // CHUNK):
        span = slice(chunk * CHUNK, (chunk + 1) * CHUNK)
        halves = CHUNK // LANES
        masks = [char_masks(lens, chunk * (CHUNK // SLOTS) + 8 * h) for h in range(halves)]
        if first:
            sides = []
            for h in range(halves):
                ids = source[pl.ds(chunk * halves + h, 1), :]
                column = to_column(char_positions(ids, me, x_first).astype(F32)).astype(jnp.int32)
                lane = iota((LANES, 512), 1)
                left = jnp.where(lane == column, 1.0, 0.0).astype(BF)
                right = jnp.where(lane == column + 8, 1.0, 0.0).astype(BF)
                sides.append(jnp.concatenate([nn(left, table[...]), nn(right, table[...])], axis=1))
            x = jnp.concatenate(sides, axis=0)
            extra_out[span] = x
        else:
            x = source[span]
        hat, _ = norm_parts(x)
        normed = (hat * gain[0:1] + shift[0:1]).astype(BF)
        qkv_out[span] = nt(normed, m_qkv[...]).astype(BF)
        blocks = char_blocks(qkv_out, chunk)
        allowed = stacked([jnp.concatenate([m[1]] * 2, axis=1) for m in masks for _ in range(2)])
        scores = jnp.where(allowed, stacked([nt(q, k) for q, k, _ in blocks]) * 0.125, masked_score)
        attend = [softmax_rows(scores[:, :LANES]).astype(BF), softmax_rows(scores[:, LANES:]).astype(BF)]
        attend = jnp.concatenate(attend, axis=1)
        mixed = [nn(attend[n * LANES : (n + 1) * LANES], v) for n, (_, _, v) in enumerate(blocks)]
        mixed = in_rows(mixed, halves).astype(BF)
        mixed_out[span] = mixed
        after = x + nt(mixed, m_out[...])
        after_out[span] = after
        hat, _ = norm_parts(after)
        normed = (hat * gain[1:2] + shift[1:2]).astype(BF)
        if chunk == 0:
            finish(far)
            assemble(x_first, me, 0, raw, (None, None, m_up, m_proj, m_down))
        hidden_here[span] = nt(normed, m_up[...])
        states = after_out[span] + nt(gelu_value(hidden_here[span]).astype(BF), m_down[...])
        next_out[span] = states
        if not first:
            extra_out[span] = states.astype(BF)
        weights = pool_weights(states, query, jnp.concatenate([m[0] for m in masks], axis=0))
        pooled = jnp.sum(weights * states.reshape(-1, SLOTS, 256), axis=1).astype(BF)
        words = slice(chunk * (CHUNK // SLOTS), (chunk + 1) * (CHUNK // SLOTS))
        pooled_out[words] = pooled
        delta_out[words] = nt(pooled, m_proj[...])


def char_blocks(qkv, chunk):
    blocks = []
    for h in range(CHUNK // LANES):
        for pair in range(2):
            q, k, v = char_heads(qkv, chunk * CHUNK + h * LANES, pair)
            blocks.append((q, two_heads(k), two_heads(v)))
    return blocks


def char_heads(qkv, base, pair):
    return (
        qkv[base : base + LANES, t * 256 + pair * LANES : t * 256 + (pair + 1) * LANES] for t in range(3)
    )


def char_forward(first, x_first, me, lens, source, parts, gain, shift, query):
    words = lens.shape[1]
    rows = words * SLOTS
    big = [(768, BF), (256, BF), (256, F32), (256, F32), (256, F32) if first else (256, BF)]
    held = C_ROWS + (16 if first else 0)
    shapes = [whole((rows, 1024), F32)] if not first else []
    out = pl.pallas_call(
        partial(char_forward_kernel, first, x_first, len(parts)),
        in_specs=[smem, smem, vmem] + [anywhere] * len(parts) + [vmem] * 3,
        out_specs=[vmem] * (12 + len(shapes)),
        out_shape=[whole((rows, c), t) for c, t in big]
        + [whole((words, 256), BF), whole((words, 512), F32)]
        + [whole(s, BF) for s in MATS]
        + shapes,
        scratch_shapes=([pltpu.VMEM((rows, 1024), F32)] if first else [])
        + [pltpu.VMEM((32, held, LANES), BF), pltpu.VMEM((512, LANES) if first else (16, LANES), BF)]
        + [pltpu.SemaphoreType.DMA((8,))] * 3,
        compiler_params=pltpu.CompilerParams(vmem_limit_bytes=VMEM),
        cost_estimate=cost(COST_FORWARD, 12e6),
    )(me, lens, source, *parts, gain, shift, query)
    qkv, mixed, after, states, extra, pooled, delta = out[:7]
    mats, hidden = out[7:12], out[12:]
    if first:
        return (extra, qkv, mixed, after, states, pooled, *hidden), delta, mats
    return (source, qkv, mixed, after, states, pooled, *hidden), delta, mats, extra


MATS = ((768, 256), (256, 256), (1024, 256), (512, 256), (256, 1024))


def pool_back(states, query, valid, grad):
    weights = pool_weights(states, query, valid)
    cube = states.reshape(-1, SLOTS, 256)
    wide = grad.reshape(-1, 1, 256)
    by_weight = jnp.sum(cube * wide, axis=-1, keepdims=True)
    by_score = weights * (by_weight - jnp.sum(weights * by_weight, axis=1, keepdims=True))
    added = weights * wide + by_score * query.reshape(1, 1, 256)
    by_query = jnp.sum((by_score * cube).reshape(states.shape), axis=0, keepdims=True)
    return added.reshape(states.shape), by_query


def accumulate(ref, value, chunk):
    if chunk == 0:
        ref[...] = value
    else:
        ref[...] += value


def char_feed_kernel(first, x_first, at, me, lens, word_own, word_other, *refs):
    pooled_in, grad_in, next_in, after_in, m_up, m_proj, m_down = refs[:7]
    gain, shift, query = of_layer(first, *refs[7:10])
    refs = refs[10:]
    if first:
        word_out, refs = refs[0], refs[1:]
    else:
        hidden_in, refs = refs[0], refs[1:]
    grad_out, keep, send, vectors, t_up, t_proj, t_down, a_up, a_proj, a_down = refs
    rows_all = grad_out.shape[0]
    words_all = rows_all // SLOTS
    word_grad = jnp.where(
        me[2] == (0 if first else 1),
        word_own[at[0] * words_all : (at[0] + 1) * words_all],
        word_other[at[1] * words_all : (at[1] + 1) * words_all],
    )
    if first:
        word_out[...] = word_grad
    vectors[...] = jnp.zeros(vectors.shape, F32)
    low_word = word_grad.astype(BF)
    a_proj[...] = tn(low_word, pooled_in[...])
    grad_pooled = nn(low_word, m_proj[...])
    for chunk in range(rows_all // CHUNK):
        span = slice(chunk * CHUNK, (chunk + 1) * CHUNK)
        words = CHUNK // SLOTS
        valid = [valid_keys(lens, chunk * words + 8 * h) for h in range(CHUNK // LANES)]
        valid = jnp.concatenate([to_column(jnp.where(v, 1.0, 0.0)) for v in valid], axis=0)
        added, by_query = pool_back(next_in[span], query, valid, grad_pooled[chunk * words : (chunk + 1) * words])
        grad = grad_in[span].astype(F32) + added
        vectors[4:5, :] += by_query
        low = grad.astype(BF)
        hat, root = norm_parts(after_in[span])
        normed = (hat * gain[1:2] + shift[1:2]).astype(BF)
        act, slope = gelu_both(nt(normed, m_up[...]) if first else hidden_in[span])
        accumulate(a_down, tn(low, act.astype(BF)), chunk)
        by_hidden = (slope * nn(low, m_down[...])).astype(BF)
        accumulate(a_up, tn(normed, by_hidden), chunk)
        back, by_gain, by_shift = norm_back(nn(by_hidden, m_up[...]), hat, root, gain[1:2])
        grad_out[span] = grad + back
        vectors[1:2, :] += by_gain
        vectors[3:4, :] += by_shift
    t_up[...] = a_up[...].T.astype(BF)
    t_proj[...] = a_proj[...].astype(BF)
    t_down[...] = a_down[...].astype(BF)
    put_char(x_first, me, keep, send, F_SPAN[0], (None, None, t_up, t_proj, t_down))


def char_feed(first, x_first, me, lens, grad, words, at, saved, mats, vectors):
    after, states, pooled, *hidden = saved
    rows = after.shape[0]
    outs = [whole((rows, 256), F32)]
    if first:
        outs = [whole((rows // SLOTS, 512), F32)] + outs
    held = F_SPAN[1]
    return pl.pallas_call(
        partial(char_feed_kernel, first, x_first, at),
        in_specs=[smem, smem] + [vmem] * (12 + len(hidden)),
        out_specs=[vmem] * (len(outs) + 3),
        out_shape=outs + [whole((16, held, LANES), BF)] * 2 + [whole((8, 256), F32)],
        scratch_shapes=[pltpu.VMEM(MATS[k], BF) for k in (2, 3, 4)]
        + [pltpu.VMEM(x, F32) for x in ((256, 1024), (512, 256), (256, 1024))],
        compiler_params=pltpu.CompilerParams(vmem_limit_bytes=VMEM),
        cost_estimate=cost(COST_FEED, 12e6),
    )(me, lens, *words, pooled, grad, states, after, *mats[2:], *vectors, *hidden)


def char_mix_kernel(first, x_first, me, lens, grad_in, mixed_in, qkv_in, x_in, m_qkv, m_out, *refs):
    gain, shift, _ = of_layer(first, *refs[:3])
    vec_feed, refs = refs[3], refs[4:]
    if first:
        ids, word_0, word_1, char_1, keep, send, vectors = refs[:7]
        refs = refs[7:]
    else:
        keep_feed, send_feed, grad_out, keep, send, vectors = refs[:6]
        refs = refs[6:]
    t_qkv, t_out, a_qkv, a_out, a_table = refs
    rows_all = grad_in.shape[0]
    vectors[...] = vec_feed[...]
    for chunk in range(rows_all // CHUNK):
        span = slice(chunk * CHUNK, (chunk + 1) * CHUNK)
        grad = grad_in[span]
        low = grad.astype(BF)
        accumulate(a_out, tn(low, mixed_in[span]), chunk)
        by_mixed = nn(low, m_out[...]).astype(BF)
        blocks = char_blocks(qkv_in, chunk)
        masks = [char_masks(lens, chunk * (CHUNK // SLOTS) + 8 * h) for h in range(CHUNK // LANES)]
        allowed = jnp.concatenate([same & (valid > 0.5) for valid, _, same in masks for _ in range(2)], axis=1)
        grads = [
            by_mixed[h * LANES : (h + 1) * LANES, pair * LANES : (pair + 1) * LANES]
            for h in range(CHUNK // LANES)
            for pair in range(2)
        ]
        spans = [slice(n * LANES, (n + 1) * LANES) for n in range(len(blocks))]
        scores = jnp.concatenate([nt(k, q) for q, k, _ in blocks], axis=1)
        by_attend = jnp.concatenate([nt(v, g) for g, (_, _, v) in zip(grads, blocks)], axis=1)
        attend, by_scores = [], []
        for h in range(2):
            part = jnp.where(allowed, scores[h * LANES : (h + 1) * LANES] * 0.125, masked_score)
            shifted = jnp.exp(part - jnp.max(part, axis=0, keepdims=True))
            part = shifted / jnp.sum(shifted, axis=0, keepdims=True)
            product = part * by_attend[h * LANES : (h + 1) * LANES]
            by_scores.append((product - part * jnp.sum(product, axis=0, keepdims=True)).astype(BF))
            attend.append(part.astype(BF))
        attend, by_scores = stacked(attend), stacked(by_scores)
        by_q = [tn(by_scores[:, n], k) * 0.125 for n, (_, k, _) in zip(spans, blocks)]
        by_k = [join_heads(nn(by_scores[:, n], q)) * 0.125 for n, (q, _, _) in zip(spans, blocks)]
        by_v = [join_heads(nn(attend[:, n], g)) for n, g in zip(spans, grads)]
        by_qkv = jnp.concatenate([in_rows(x, CHUNK // LANES) for x in (by_q, by_k, by_v)], axis=1).astype(BF)
        hat, root = norm_parts(x_in[span])
        normed = (hat * gain[0:1] + shift[0:1]).astype(BF)
        accumulate(a_qkv, tn(normed, by_qkv), chunk)
        back, by_gain, by_shift = norm_back(nn(by_qkv, m_qkv[...]), hat, root, gain[0:1])
        grad = grad + back
        vectors[0:1, :] += by_gain
        vectors[2:3, :] += by_shift
        if first:
            for h in range(CHUNK // LANES):
                at = char_positions(ids[pl.ds(chunk * (CHUNK // LANES) + h, 1), :], me, x_first)
                row = iota((512, LANES), 0)
                part = grad[h * LANES : (h + 1) * LANES]
                high = part.astype(BF)
                rest = (part - high.astype(F32)).astype(BF)
                both = jnp.concatenate([high, rest], axis=0)
                for side in range(2):
                    hot = jnp.where(row == at + 8 * side, 1.0, 0.0).astype(BF)
                    hot = jnp.concatenate([hot, hot], axis=1)
                    accumulate(a_table, nn(hot, both[:, side * LANES : (side + 1) * LANES]), chunk + h + side)
        else:
            grad_out[span] = grad
    t_qkv[...] = a_qkv[...].T.astype(BF)
    t_out[...] = a_out[...].astype(BF)
    put_char(x_first, me, keep, send, A_SPAN[0], (t_qkv, t_out, None, None, None))
    if first:
        row = A_SPAN[1]
        for k in range(16):
            keep[k, row : row + E_ROWS, :] = a_table[k * 16 : k * 16 + 16, :].astype(BF)
            send[k, row : row + E_ROWS, :] = a_table[256 + k * 16 : 272 + k * 16, :].astype(BF)
        word = jnp.concatenate([word_0[0:4], word_1[0:4]], axis=0)
        char = jnp.concatenate([vectors[...], char_1[...]], axis=0)
        tiles = [x[:, t * LANES : (t + 1) * LANES] for x in (word, char) for t in range(x.shape[1] // LANES)]
        vector = split_vector(jnp.concatenate(tiles, axis=0))
        send[16] = vector[:80]
        send[17, 0:48, :] = vector[80:]
        send[17, 48:, :] = jnp.zeros((32, LANES), BF)
    else:
        keep[:, F_SPAN[0] :, :] = keep_feed[...]
        send[:, F_SPAN[0] :, :] = send_feed[...]


def char_mix(first, x_first, me, lens, grad, saved, mats, vectors, others):
    x, qkv, mixed = saved
    rows = x.shape[0]
    if first:
        outs, held, sends = [], A_SPAN[1] + E_ROWS, 18
    else:
        outs, held, sends = [whole((rows, 256), F32)], C_ROWS, 16
    return pl.pallas_call(
        partial(char_mix_kernel, first, x_first),
        in_specs=[smem, smem] + [vmem] * (9 + len(others)),
        out_specs=[vmem] * (len(outs) + 3),
        out_shape=outs
        + [whole((16, held, LANES), BF), whole((sends, held, LANES), BF), whole((8, 256), F32)],
        scratch_shapes=[pltpu.VMEM(MATS[k], BF) for k in (0, 1)]
        + [pltpu.VMEM(x, F32) for x in ((256, 768), (256, 256), (512 if first else 8, LANES))],
        compiler_params=pltpu.CompilerParams(vmem_limit_bytes=VMEM),
        cost_estimate=cost(COST_MIX, 12e6),
    )(me, lens, grad, mixed, qkv, x, *mats[:2], *vectors, *others)


def char_middle_kernel(me, lens, *refs):
    mix_in, refs = refs[:12], refs[12:]
    feed_in, refs = refs[:11], refs[11:]
    mix_out, feed_out, refs = refs[:3], refs[3:8], refs[8:]
    grad_here, mix_scratch, feed_scratch = refs[0], refs[1:6], refs[6:]
    char_mix_kernel(False, True, me, lens, *mix_in, grad_here, *mix_out, *mix_scratch)
    char_feed_kernel(True, True, (0, 0), me, lens, *feed_in[:3], grad_here, *feed_in[3:], *feed_out, *feed_scratch)


def char_middle(me, lens, grad, saved_1, mats_1, vectors, others, words, saved_0, mats_0):
    x, qkv, mixed = saved_1
    after, states, pooled = saved_0
    rows = x.shape[0]
    return pl.pallas_call(
        char_middle_kernel,
        in_specs=[smem, smem] + [vmem] * 23,
        out_specs=[vmem] * 8,
        out_shape=[whole((16, C_ROWS, LANES), BF)] * 2
        + [whole((8, 256), F32), whole((rows // SLOTS, 512), F32), whole((rows, 256), F32)]
        + [whole((16, F_SPAN[1], LANES), BF)] * 2
        + [whole((8, 256), F32)],
        scratch_shapes=[pltpu.VMEM((rows, 256), F32)]
        + [pltpu.VMEM(MATS[k], BF) for k in (0, 1)]
        + [pltpu.VMEM(x, F32) for x in ((256, 768), (256, 256), (8, LANES))]
        + [pltpu.VMEM(MATS[k], BF) for k in (2, 3, 4)]
        + [pltpu.VMEM(x, F32) for x in ((256, 1024), (512, 256), (256, 1024))],
        compiler_params=pltpu.CompilerParams(vmem_limit_bytes=VMEM),
        cost_estimate=cost(COST_MIX + COST_FEED, 24e6),
    )(
        *(me, lens, grad, mixed, qkv, x, *mats_1[:2], *vectors, *others),
        *(*words, pooled, states, after, *mats_0[2:], *vectors),
    )


def fetch_word(me, parts, upper, down, sems):
    for k, part in enumerate(parts):
        rc, far, ry, rx = k >> 3, (k >> 2) & 1, (k >> 1) & 1, k & 1

        def one(s, _, part=part, rc=rc, far=far, ry=ry, rx=rx):
            w, n = ((far * 2 + s) * 2 + rx) ^ me[0], (ry * 2 + rc) ^ me[1]
            block = part.at[s]
            column = pl.ds(pl.multiple_of(n * LANES, LANES), LANES)
            for which, base, (row, rows) in ((0, 0, W_QKV), (1, 1536, W_OUT), (2, 2048, W_UP)):
                to = pl.ds(pl.multiple_of(base + w * rows, 64), rows)
                pltpu.make_async_copy(block.at[pl.ds(row, rows)], upper.at[to, column], sems.at[which]).start()
            for t in range(4):
                column = pl.ds(pl.multiple_of(n * 512 + t * LANES, LANES), LANES)
                to = pl.ds(pl.multiple_of(w * 64, 64), 64)
                pltpu.make_async_copy(
                    block.at[pl.ds(W_DOWN[0] + 64 * t, 64)], down.at[to, column], sems.at[3]
                ).start()
            return 0

        lax.fori_loop(0, 2, one, 0)
    return [
        pltpu.make_async_copy(ref, ref, sems.at[k])
        for k, ref in enumerate((upper.at[pl.ds(0, 1536)], upper.at[pl.ds(1536, 512)], upper.at[pl.ds(2048, 2048)], down))
    ]


def word_allowed(docs, words):
    shape = (words, 2 * words)
    i, j = iota(shape, 0).astype(F32), (iota(shape, 1) % words).astype(F32)
    end = jnp.zeros((1, 1), F32)
    of_i, of_j = jnp.zeros(shape, jnp.int32), jnp.zeros(shape, jnp.int32)
    for k in range(docs.shape[1]):
        end = end + docs[:, k : k + 1]
        of_i = of_i + (i >= end).astype(jnp.int32)
        of_j = of_j + (j >= end).astype(jnp.int32)
    return (of_i == of_j) & (j <= i)


def docs_of(states, documents):
    return [x[2, 0:1, 0:documents].astype(F32) for x in states]


def by_half(x, reduce, fill):
    low = low_half(x.shape)
    left = reduce(jnp.where(low, x, fill), axis=-1, keepdims=True)
    right = reduce(jnp.where(low, fill, x), axis=-1, keepdims=True)
    return jnp.where(low, left, right)


def word_blocks(qkv, allowed):
    rows = qkv.shape[0] // len(allowed)
    blocks = []
    for r in range(len(allowed)):
        for pair in range(4):
            q, k, v = word_heads(qkv, r * rows, rows, pair)
            blocks.append((q, two_heads(k), two_heads(v)))
    return blocks, jnp.concatenate([pairs for pairs in allowed for _ in range(4)], axis=0)


def stacked(parts):
    return jnp.concatenate(parts, axis=0)


def in_rows(parts, count):
    each = len(parts) // count
    return stacked([jnp.concatenate(parts[r * each : (r + 1) * each], axis=1) for r in range(count)])


def word_attend(blocks, allowed):
    scores = jnp.where(allowed, stacked([nt(q, k) for q, k, _ in blocks]) * 0.125, masked_score)
    shifted = jnp.exp(scores - by_half(scores, jnp.max, 2 * masked_score))
    return shifted / by_half(shifted, jnp.sum, 0.0)


def word_forward_body(w1, coming, upper, down, gain, shift, allowed):
    hat, root = norm_parts(w1)
    normed = (hat * gain[0:1] + shift[0:1]).astype(BF)
    await_one(coming, 0)
    qkv = nt(normed, upper[0:1536, :]).astype(BF)
    rows = w1.shape[0] // len(allowed)
    blocks, pairs = word_blocks(qkv, allowed)
    attend = word_attend(blocks, pairs).astype(BF)
    mixed = [nn(attend[n * rows : (n + 1) * rows], v) for n, (_, _, v) in enumerate(blocks)]
    mixed = in_rows(mixed, len(allowed)).astype(BF)
    await_one(coming, 1)
    w2 = w1 + nt(mixed, upper[1536:2048, :])
    hat, root = norm_parts(w2)
    normed = (hat * gain[1:2] + shift[1:2]).astype(BF)
    await_one(coming, 2)
    hidden = nt(normed, upper[2048:4096, :])
    await_one(coming, 3)
    w3 = w2 + nt(gelu_value(hidden).astype(BF), down[...])
    return qkv, mixed, w2, hidden, w3


def word_heads(qkv, row, rows, pair):
    return (qkv[row : row + rows, t * 512 + pair * LANES : t * 512 + (pair + 1) * LANES] for t in range(3))


def await_one(coming, k):
    if coming is not None:
        coming[k].wait()


def word_backward_body(grad, w1, qkv, w2, hidden, upper, down, gain, shift, allowed, vectors):
    low_2 = grad.astype(BF)
    act, slope = gelu_both(hidden)
    by_hidden = (slope * nn(low_2, down[...])).astype(BF)
    hat, root = norm_parts(w2)
    normed_2 = (hat * gain[1:2] + shift[1:2]).astype(BF)
    back, by_gain, by_shift = norm_back(nn(by_hidden, upper[2048:4096, :]), hat, root, gain[1:2])
    grad = grad + back
    vectors[1:2, :] = by_gain
    vectors[3:4, :] = by_shift
    low_1 = grad.astype(BF)
    by_mixed = nn(low_1, upper[1536:2048, :]).astype(BF)
    rows = w1.shape[0] // len(allowed)
    blocks, pairs = word_blocks(qkv, allowed)
    spans = [slice(n * rows, (n + 1) * rows) for n in range(len(blocks))]
    grads = [
        by_mixed[r * rows : (r + 1) * rows, pair * LANES : (pair + 1) * LANES]
        for r in range(len(allowed))
        for pair in range(4)
    ]
    attend = word_attend(blocks, pairs)
    product = attend * stacked([nt(g, v) for g, (_, _, v) in zip(grads, blocks)])
    by_scores = (product - attend * by_half(product, jnp.sum, 0.0)).astype(BF)
    attend = attend.astype(BF)
    by_q = [nn(by_scores[n], k) * 0.125 for n, (_, k, _) in zip(spans, blocks)]
    by_k = [join_heads(tn(by_scores[n], q)) * 0.125 for n, (q, _, _) in zip(spans, blocks)]
    by_v = [join_heads(tn(attend[n], g)) for n, g in zip(spans, grads)]
    by_qkv = jnp.concatenate([in_rows(x, len(allowed)) for x in (by_q, by_k, by_v)], axis=1).astype(BF)
    hat, root = norm_parts(w1)
    normed_1 = (hat * gain[0:1] + shift[0:1]).astype(BF)
    back, by_gain, by_shift = norm_back(nn(by_qkv, upper[0:1536, :]), hat, root, gain[0:1])
    vectors[0:1, :] = by_gain
    vectors[2:3, :] = by_shift
    return grad + back, (normed_1, by_qkv, low_1, normed_2, by_hidden, act.astype(BF), low_2)


FACTORS = (512, 1536, 512, 512, 2048, 2048, 512)


def word_weights_kernel(firsts, me, mixed_0, mixed_1, *refs):
    normed_1, by_qkv, low_1, normed_2, by_hidden, act, low_2, keep_out, send_out, keep, send, sems = refs
    leaving = []

    def leave(row, rows):
        span = pl.ds(row, rows)
        k = len(leaving)
        leaving.extend(
            begin(
                [
                    (a.at[:, span], b.at[:, span], sems.at[k + n])
                    for n, (a, b) in enumerate(((send, send_out), (keep, keep_out)))
                ]
            )
        )

    mw, my, mc = me[0], me[1] >> 1, me[1] & 1
    mixed = jnp.where(me[2] == 0, mixed_0[...], mixed_1[...])

    def put(w, row, rows, blocks):
        for y in range(2):
            at = place(w ^ mw, y ^ my, firsts[row // 384])
            zero, one = blocks(2 * y), blocks(2 * y + 1)
            keep[at, row : row + rows, :] = jnp.where(mc == 0, zero, one)
            send[at, row : row + rows, :] = jnp.where(mc == 0, one, zero)

    for pair in range(4):
        columns = slice(pair * LANES, (pair + 1) * LANES)
        part = tn(low_2[:, columns], act[...]).astype(BF)
        for k in range(2):
            for t in range(4):
                put(
                    2 * pair + k,
                    W_DOWN[0] + 64 * t,
                    64,
                    lambda n: part[k * 64 : k * 64 + 64, n * 512 + t * LANES : n * 512 + (t + 1) * LANES],
                )
    leave(*(W_DOWN[0], 256))
    for w in range(8):
        part = tn(by_hidden[:, w * 256 : (w + 1) * 256], normed_2[...]).astype(BF)
        for k in range(2):
            put(
                w,
                W_UP[0] + 128 * k,
                128,
                lambda n: part[k * 128 : k * 128 + 128, n * LANES : (n + 1) * LANES],
            )
    leave(*W_UP)
    for pair in range(4):
        columns = slice(pair * LANES, (pair + 1) * LANES)
        part = tn(low_1[:, columns], mixed).astype(BF)
        for k in range(2):
            put(
                2 * pair + k,
                W_OUT[0],
                64,
                lambda n: part[k * 64 : k * 64 + 64, n * LANES : (n + 1) * LANES],
            )
    leave(*W_OUT)
    for pair in range(4):
        part = tn(by_qkv[:, pair * 384 : (pair + 1) * 384], normed_1[...]).astype(BF)
        for k in range(2):
            put(
                2 * pair + k,
                W_QKV[0],
                192,
                lambda n: part[k * 192 : (k + 1) * 192, n * LANES : (n + 1) * LANES],
            )
    leave(*W_QKV)
    finish(leaving)


def word_weights(firsts, me, mixed_0, mixed_1, factors):
    return pl.pallas_call(
        partial(word_weights_kernel, firsts),
        in_specs=[smem] + [vmem] * 9,
        out_specs=[anywhere] * 2,
        out_shape=[whole((16, W_ROWS, LANES), BF)] * 2,
        scratch_shapes=[pltpu.VMEM((16, W_ROWS, LANES), BF)] * 2 + [pltpu.SemaphoreType.DMA((8,))],
        compiler_params=pltpu.CompilerParams(vmem_limit_bytes=VMEM),
        cost_estimate=cost(2e9, 9e6),
    )(me, mixed_0, mixed_1, *factors)


def both_deltas(refs):
    own = refs[0][...]
    return stacked([own, nt(refs[1][...], refs[2][...])]) if len(refs) > 1 else own


def swapped(x, count):
    half = x.shape[0] // 2
    return jnp.concatenate([x[half:], x[:half]], axis=0) if count == 2 else x


UPPER, DOWN = (4096, 512), (512, 2048)
word_scratch = [pltpu.SemaphoreType.DMA((4,))]


def word_fetch_kernel(me, *refs):
    *parts, upper, down, sems = refs
    finish(fetch_word(me, parts, upper, down, sems))


def word_fetch(me, parts):
    return pl.pallas_call(
        word_fetch_kernel,
        in_specs=[smem] + [anywhere] * 16,
        out_specs=[vmem] * 2,
        out_shape=[whole(UPPER, BF), whole(DOWN, BF)],
        scratch_shapes=word_scratch,
        compiler_params=pltpu.CompilerParams(vmem_limit_bytes=VMEM),
    )(me, *parts)


def word_call(kernel, count, documents, tables, operands, outs, scratch, flops, alias=None):
    return pl.pallas_call(
        partial(kernel, count, documents),
        in_specs=[smem] * len(tables) + [anywhere if x.shape[1:] == (W_ROWS, LANES) else vmem for x in operands],
        out_specs=[vmem] * len(outs),
        out_shape=[whole(shape, dtype) for shape, dtype in outs],
        scratch_shapes=scratch,
        input_output_aliases=alias or {},
        compiler_params=pltpu.CompilerParams(vmem_limit_bytes=VMEM),
        cost_estimate=cost(flops, 16e6),
    )(*tables, *operands)


def word_first_kernel(count, documents, me, *refs):
    states, refs = refs[:count], refs[count:]
    deltas, parts = refs[: 2 * count - 1], refs[2 * count - 1 :]
    docs = docs_of(states, documents)
    gain, shift, w1_out, qkv_out, mixed_out, w2_out, hidden_out, w3_out, upper, down, sems = parts[16:]
    coming = fetch_word(me, parts[:16], upper, down, sems)

    @pl.when(me[2] == 0)
    def _():
        w1 = stacked([a[0].astype(F32) for a in states]) + both_deltas(deltas)
        w1_out[...] = w1
        allowed = [word_allowed(d, w1.shape[0] // count) for d in docs]
        qkv, mixed, w2, hidden, w3 = word_forward_body(w1, coming, upper, down, gain[0], shift[0], allowed)
        qkv_out[...] = qkv
        mixed_out[...] = mixed
        w2_out[...] = w2
        hidden_out[...] = hidden
        w3_out[...] = w3

    @pl.when(me[2] != 0)
    def _():
        finish(coming)
        w3_out[...] = jnp.zeros(w3_out.shape, F32)


def word_first(me, documents, states, deltas, parts, gain, shift):
    count = len(states)
    words = count * deltas[0].shape[0]
    shapes = [(512, F32), (1536, BF), (512, BF), (512, F32), (2048, F32), (512, F32)]
    return word_call(
        word_first_kernel,
        count,
        documents,
        [me],
        [*states, *deltas, *parts, gain, shift],
        [((words, c), t) for c, t in shapes] + [(UPPER, BF), (DOWN, BF)],
        word_scratch,
        1e9,
    )


def word_last_kernel(count, documents, me, *refs):
    w_in, deltas, refs = refs[0], refs[1 : 2 * count], refs[2 * count :]
    cots, parts = refs[:count], refs[count:]
    docs = docs_of(cots, documents)
    upper, down, gain, shift, out_own, out_other, grad_out, vectors, mixed_out = parts[:9]
    factors = parts[9:]
    vectors[...] = jnp.zeros(vectors.shape, F32)

    @pl.when(me[2] == 1)
    def _():
        w1 = swapped(w_in[...], count) + both_deltas(deltas)
        rows = w1.shape[0] // count
        allowed = [word_allowed(d, rows) for d in docs]
        gains, shifts = gain[1], shift[1]
        qkv, mixed, w2, hidden, w3 = word_forward_body(w1, None, upper, down, gains, shifts, allowed)
        out_own[...] = w3[:rows].astype(BF)
        out_other[...] = w3[(count - 1) * rows :].astype(BF)
        grad = jnp.concatenate([c[1].astype(F32) for c in cots], axis=0)
        mixed_out[...] = mixed
        grad, made = word_backward_body(grad, w1, qkv, w2, hidden, upper, down, gains, shifts, allowed, vectors)
        grad_out[...] = grad
        for ref, value in zip(factors, made):
            ref[...] = value

    @pl.when(me[2] != 1)
    def _():
        for ref in (out_own, out_other, grad_out):
            ref[...] = jnp.zeros(ref.shape, ref.dtype)


def word_last(me, documents, w_in, deltas, cots, mats, gain, shift):
    count = len(cots)
    words = w_in.shape[0]
    row = words // count
    return word_call(
        word_last_kernel,
        count,
        documents,
        [me],
        [w_in, *deltas, *cots, *mats, gain, shift],
        [((row, 512), BF)] * 2
        + [((words, 512), F32), ((8, 512), F32), ((words, 512), BF)]
        + [((words, c), BF) for c in FACTORS],
        [],
        2e9,
    )


def word_back_kernel(count, documents, me, *refs):
    states, (grad_in, w1, qkv, w2, hidden), parts = refs[:count], refs[count : count + 5], refs[count + 5 :]
    docs = docs_of(states, documents)
    upper, down, gain, shift = parts[:4]
    held, parts_out = parts[4:11], parts[11:]
    grad_own, grad_other, vectors = parts_out[:3]
    factors = parts_out[3:]
    vectors[...] = jnp.zeros(vectors.shape, F32)

    @pl.when(me[2] == 0)
    def _():
        rows = w1.shape[0] // count
        grad, made = word_backward_body(
            swapped(grad_in[...], count),
            w1[...],
            qkv[...],
            w2[...],
            hidden[...],
            upper,
            down,
            gain[0],
            shift[0],
            [word_allowed(d, rows) for d in docs],
            vectors,
        )
        grad_own[...] = grad[:rows]
        grad_other[...] = grad[(count - 1) * rows :]
        for ref, value in zip(factors, made):
            ref[...] = value

    @pl.when(me[2] != 0)
    def _():
        for ref in (grad_own, grad_other):
            ref[...] = jnp.zeros(ref.shape, F32)
        for ref, value in zip(factors, held):
            ref[...] = value[...]


def word_back(me, documents, states, grad, saved, mats, gain, shift, held):
    count = len(states)
    words = grad.shape[0]
    return word_call(
        word_back_kernel,
        count,
        documents,
        [me],
        [*states, grad, *saved, *mats, gain, shift, *held],
        [((words // count, 512), F32)] * 2 + [((8, 512), F32)] + [((words, c), BF) for c in FACTORS],
        [],
        2e9,
    )


def swap(x, axis, flip):
    return lax.ppermute(x, axis, [(k, k ^ flip) for k in range(lax.axis_size(axis))])


def over_x(x):
    return swap(x, "wide", 1)


def over_y(x):
    return swap(x, "narrow", 2)


def over_core(x):
    return swap(x, "narrow", 1)


def over_pair(x):
    return swap(x, "wide", 2)


def after(x, *others):
    return lax.optimization_barrier((x, *others))[0]


def add(*terms):
    total = terms[0].astype(F32)
    for term in terms[1:]:
        total = total + term.astype(F32)
    return total.astype(BF)


def gather_z(block):
    return jnp.stack([block] + [swap(block, "wide", 2 * k) for k in (1, 2, 3)])


def gather_one(z, x_first):
    return jnp.concatenate([z, (over_x if x_first else over_y)(z)], axis=0)


def gather_two(first, x_first):
    return first, (over_y if x_first else over_x)(first)


def gather_core(parts):
    return (*parts, *[over_core(part) for part in parts])


def two(x, x_first):
    return (over_y if x_first else over_x)(x)


def one(x, x_first):
    return (over_x if x_first else over_y)(x)


def cut(matrices, table):
    qkv, out, up, down, proj, *words = matrices

    def split(m):
        r, c = m.shape
        return m.T.reshape(8, c // 8, 4, r // 4).transpose(0, 2, 1, 3)

    def paired(m):
        b = split(m)
        c = b.shape[2]
        return b.reshape(8, 4, 2, c // 2, 64).transpose(0, 1, 3, 2, 4).reshape(8, 4, c // 2, LANES)

    def tiled(m):
        b = split(m)
        c, r = b.shape[2:]
        return b.reshape(8, 4, c, r // LANES, LANES).transpose(0, 1, 3, 2, 4).reshape(8, 4, -1, LANES)

    char = [paired(qkv), paired(out), paired(up), paired(proj), tiled(down)]
    if table is not None:
        char.append(table.reshape(8, 4, 8, 2, LANES).transpose(0, 1, 3, 2, 4).reshape(8, 4, 16, LANES))
    word = [tiled(m) for m in words]
    return [ordered(jnp.concatenate(x, axis=2)) for x in (char, word)]


def ordered(blocks):
    b = blocks.reshape(4, 2, 2, 2, *blocks.shape[2:]).transpose(3, 2, 1, 0, 4, 5)
    return b.reshape(32, *blocks.shape[2:])


def uncut(blocks, is_char, with_table):
    b = blocks.reshape(2, 2, 2, 4, *blocks.shape[1:]).transpose(3, 2, 1, 0, 4, 5)
    b = b.reshape(8, 4, *blocks.shape[1:])

    def joined(x):
        c, r = x.shape[2:]
        return x.transpose(0, 2, 1, 3).reshape(8 * c, 4 * r).T

    def paired(x):
        c = x.shape[2]
        return joined(x.reshape(8, 4, c, 2, 64).transpose(0, 1, 3, 2, 4).reshape(8, 4, 2 * c, 64))

    def tiled(x, tiles):
        c = x.shape[2] // tiles
        return joined(x.reshape(8, 4, tiles, c, LANES).transpose(0, 1, 3, 2, 4).reshape(8, 4, c, tiles * LANES))

    def rows(span, count=None):
        return b[:, :, span[0] : span[0] + (count or span[1])]

    if not is_char:
        return [tiled(rows(W_QKV), 1), tiled(rows(W_OUT), 1), tiled(rows(W_UP), 1), tiled(rows(W_DOWN, 256), 4)], None
    table = None
    if with_table:
        table = rows(C_EMB).reshape(32, 2, 8, LANES).transpose(0, 2, 1, 3).reshape(256, 256)
    qkv, out, up, proj = (paired(rows(span)) for span in C_PAIRED)
    return [qkv, out, up, tiled(rows(C_DOWN, 64), 2), proj], table


def over_xy(x):
    flip = lax.axis_size("narrow") + 2
    return lax.ppermute(x, ("wide", "narrow"), [(k, k ^ flip) for k in range(lax.axis_size(("wide", "narrow")))])


together = lax.optimization_barrier


def whole_chip(z):
    return [z, over_x(z), over_y(z), over_xy(z)]


def both_cores(near):
    near = jnp.concatenate(near, axis=0)
    return near, over_core(near)


def three(word_states, word_cot, doc_lengths):
    words, width = word_states.shape[1:]
    docs = jnp.pad(doc_lengths.astype(BF), ((0, words - 1), (0, width - doc_lengths.shape[1])))
    return jnp.stack([word_states[0], word_cot[0], docs])


def direct_program(
    word_states, character_ids, word_lengths, doc_lengths, embedding, weights, vectors, char_cot, word_cot
):
    char_gains, char_shifts, pool_query, word_gains, word_shifts = vectors
    vectors_char = (char_gains, char_shifts, pool_query)
    vectors_word = (word_gains, word_shifts)
    width = char_cot.shape[3]
    wide = lax.axis_index("wide")
    me = jnp.stack([wide, lax.axis_index("narrow"), (wide >> 1) & 1]).astype(jnp.int32)
    firsts = (True, False)
    f0, f1 = firsts
    c0, mine, theirs = pack(weights, embedding)
    pair = three(word_states, word_cot, doc_lengths)
    ids = character_ids.reshape(-1, LANES)
    got = over_pair(theirs)
    z0 = gather_z(c0)
    word = jnp.stack([mine, got])
    z0, word, ids, pair = together((z0, word, ids, pair))
    near_0 = whole_chip(z0)
    far = swap(word, "wide", 4)
    word_near = whole_chip(word[:, :W_ROWS])
    near_0, far, word_near = together((near_0, far, word_near))
    char_0 = both_cores(near_0)
    far_near = whole_chip(far[:, :W_ROWS])
    word_cores = [over_core(part) for part in word_near]
    char_0, word_cores, pair = together((char_0, word_cores, pair))
    other_pair = over_pair(pair)
    saved_0, delta_0, mats_0 = char_forward(True, True, me, word_lengths, ids, char_0, *vectors_char)
    other_delta_0 = over_pair(saved_0[5])
    other_delta_0, far_near, other_pair, word, far = together((other_delta_0, far_near, other_pair, word, far))
    z1 = jnp.concatenate([word[:, W_ROWS:], far[:, W_ROWS:]], axis=0)
    far_cores = [over_core(part) for part in far_near]
    far_cores, z1 = together((far_cores, z1))
    near_1 = whole_chip(z1)
    word_parts = [*word_near, *far_near, *word_cores, *far_cores]
    docs = doc_lengths.shape[1]
    pairs = [pair, other_pair]
    *word_saved, w3, upper, down = word_first(me, docs, pairs, [delta_0, other_delta_0, mats_0[3]], word_parts, *vectors_word)
    near_1, w3 = together((near_1, w3))
    char_1 = both_cores(near_1)
    char_1, states = together((char_1, saved_0[4]))
    saved_1, delta_1, mats_1, char_out = char_forward(False, True, me, word_lengths, states, char_1, *vectors_char)
    other_w3 = over_pair(w3)
    other_delta_1 = over_pair(saved_1[5])
    out_own, out_other, grad_1, word_vec_1, mixed_1, *held = word_last(
        me, docs, other_w3, [delta_1, other_delta_1, mats_1[3]], pairs, (upper, down), *vectors_word
    )
    w1, qkv, mixed_0, w2, hidden = word_saved
    got_1 = over_pair(grad_1)
    grad_own, grad_other, word_vec_0, *factors = word_back(
        me, docs, pairs, got_1, (w1, qkv, w2, hidden), (upper, down), *vectors_word, held
    )
    keep, send = word_weights(firsts, me, mixed_0, mixed_1, factors)
    got = over_core(send)
    got_0 = over_pair(grad_other)
    out_other = over_pair(out_other)
    cot = char_cot[0].reshape(-1, width)
    cot, keep, grad_1, got_1 = together((cot, keep, grad_1, got_1))
    grad, keep_f1, send_f1, vec_1 = char_feed(
        False, True, me, word_lengths, cot, (grad_1, got_1), (0, 1), saved_1[3:], mats_1, vectors_char
    )
    got, got_0, out_other, grad = together((got, got_0, out_other, grad))
    pieces = []
    for h in range(2):
        span = slice(384 * h, 384 * h + 384)
        pieces += [add(keep[k : k + 8, span], got[k : k + 8, span]) for k in (0, 8)]
    pieces, grad = together((pieces, grad))
    pieces[1], pieces[3] = two(pieces[1], f0), two(pieces[3], f1)
    keep_1, send_1, char_vec_1, word_grad, grad, keep_f0, send_f0, vec_0 = char_middle(
        me,
        word_lengths,
        grad,
        saved_1[:3],
        mats_1,
        vectors_char,
        (vec_1, keep_f1, send_f1),
        (grad_own, got_0),
        saved_0[3:],
        mats_0,
    )
    pieces, grad, send_1, send_f0 = together((pieces, grad, send_1, send_f0))
    got_1 = over_core(send_1)
    got_f0 = over_core(send_f0)
    pieces = [add(a[k : k + 4], b[k : k + 4]) for a, b in (pieces[:2], pieces[2:]) for k in (0, 4)]
    pieces, grad, got_1, got_f0, keep_1 = together((pieces, grad, got_1, got_f0, keep_1))
    pieces[1], pieces[3] = one(pieces[1], f0), one(pieces[3], f1)
    own_1, *away_1 = fold_cores(keep_1, got_1)
    own_1, away_1, grad = together((own_1, away_1, grad))
    away_1 = [over_x(away_1[0]), over_y(away_1[1]), over_xy(away_1[2])]
    keep_0, send_0, _ = char_mix(
        True,
        True,
        me,
        word_lengths,
        grad,
        saved_0[:3],
        mats_0,
        vectors_char,
        (vec_0, ids, word_vec_0, word_vec_1, char_vec_1),
    )
    pieces, send_0 = together((pieces, send_0))
    got_0 = over_core(send_0)
    ours, away = (
        jnp.concatenate([add(a[k : k + 2], b[k : k + 2]) for a, b in (pieces[:2], pieces[2:])], axis=1) for k in (0, 2)
    )
    got_0, away = together((got_0, away))
    away = swap(away, "wide", 4)
    own_0, *away_0 = fold_one(keep_f0, got_f0, keep_0, got_0, send_0)
    away_0, away_1 = together((away_0, away_1))
    sent = away_0[0]
    moved = (over_x(away_0[0]), over_y(away_0[1]), over_xy(away_0[2]))
    second = fold_chips(own_1, *away_1)
    second = [second[0]] + [swap(second[k], "wide", 2 * k) for k in (1, 2, 3)]
    moved, second = together((moved, second))
    own_0, *away_0 = fold_two(own_0, sent, *moved)
    away_0, away = together((away_0, away))
    ours, away = (add(ours[k : k + 1], away[k : k + 1]) for k in (0, 1))
    away = over_pair(away)
    first = [own_0, away_0[0]] + [swap(away_0[k - 1], "wide", 2 * k) for k in (1, 2, 3)]
    out = unpack(me, [*first, *second, ours, away, out_own, out_other], weights, embedding, vectors)
    return (char_out, out[-1], word_grad, out[9], *out[:9], *out[10:15])


def plain_program(
    word_states, character_ids, word_lengths, doc_lengths, embedding, weights, vectors, char_cot, word_cot
):
    char_gains, char_shifts, pool_query, word_gains, word_shifts = vectors
    width = char_cot.shape[3]
    both = ("wide", "narrow")
    firsts = (True, True)
    at = [jnp.array([0, 0, layer], jnp.int32) for layer in range(2)]
    table = lax.all_gather(embedding, both, axis=0, tiled=True)
    full = [lax.all_gather(lax.all_gather(m, "narrow", axis=1, tiled=True), "wide", axis=2, tiled=True) for m in weights]
    chars, words = [], []
    for layer in range(2):
        char, word = cut([m[layer] for m in full], table if layer == 0 else None)
        chars.append([char[8 * k : 8 * k + 8] for k in range(4)])
        words.append([word[k : k + 2] for c in (0, 16) for z in (0, 2) for k in range(c + z, c + z + 16, 4)])
    ids = character_ids.reshape(-1, LANES)
    vectors_char = (char_gains, char_shifts, pool_query)
    vectors_word = (word_gains, word_shifts)
    saved_0, delta_0, mats_0 = char_forward(True, True, at[0], word_lengths, ids, chars[0], *vectors_char)
    states = saved_0[4]
    saved_1, delta_1, mats_1, char_out = char_forward(False, True, at[0], word_lengths, states, chars[1], *vectors_char)
    docs = doc_lengths.shape[1]
    pair = [three(word_states, word_cot, doc_lengths)]
    *word_saved, w3, upper, down = word_first(at[0], docs, pair, [delta_0], words[0], *vectors_word)
    word_out, _, grad_1, word_vec_1, mixed_1, *held = word_last(
        at[1], docs, w3, [delta_1], pair, word_fetch(at[1], words[1]), *vectors_word
    )
    word_mats = (upper, down)
    w1, qkv, mixed_0, w2, hidden = word_saved
    grad_0, _, word_vec_0, *factors = word_back(
        at[0], docs, pair, grad_1, (w1, qkv, w2, hidden), word_mats, *vectors_word, held
    )
    words = [word_weights(firsts, at[0], mixed, mixed, made) for mixed, made in ((mixed_0, factors), (mixed_1, held))]
    cot = char_cot[0].reshape(-1, width)
    grad, keep_f, send_f, vec_1 = char_feed(
        False, True, at[1], word_lengths, cot, (grad_1, grad_1), (0, 0), saved_1[3:], mats_1, vectors_char
    )
    grad, keep_1, send_1, char_vec_1 = char_mix(
        False, True, at[1], word_lengths, grad, saved_1[:3], mats_1, vectors_char, (vec_1, keep_f, send_f)
    )
    word_grad, grad, keep_f, send_f, vec_0 = char_feed(
        True, True, at[0], word_lengths, grad, (grad_0, grad_0), (0, 0), saved_0[3:], mats_0, vectors_char
    )
    keep_0, send_0, _ = char_mix(
        True,
        True,
        at[0],
        word_lengths,
        grad,
        saved_0[:3],
        mats_0,
        vectors_char,
        (vec_0, ids, word_vec_0, word_vec_1, char_vec_1),
    )
    summed = lax.psum(whole_vector(send_0[16:].reshape(-1, LANES)[:128]), both)
    keep_0, send_0 = (
        jnp.concatenate([a[:16, :64], f, a[:16, 64:]], axis=1) for a, f in ((keep_0, keep_f), (send_0, send_f))
    )
    blocks = ((keep_0, send_0), (keep_1, send_1), *words)
    full = [uncut(jnp.concatenate(g), k < 2, k == 0) for k, g in enumerate(blocks)]
    matrix_grads = [
        lax.psum_scatter(
            lax.psum_scatter(jnp.stack([a, b]), "wide", scatter_dimension=2, tiled=True),
            "narrow",
            scatter_dimension=1,
            tiled=True,
        ).astype(F32)
        for a, b in zip(full[0][0] + full[2][0], full[1][0] + full[3][0])
    ]
    embedding_grad = lax.psum_scatter(full[0][1].astype(F32), both, scatter_dimension=0, tiled=True)
    word_vectors = summed[:32].reshape(4, 2, 4, LANES).transpose(1, 2, 0, 3).reshape(2, 4, 512)
    char_vectors = summed[32:].reshape(2, 2, 8, LANES).transpose(1, 2, 0, 3).reshape(2, 8, 256)
    return (
        char_out,
        word_out,
        word_grad,
        embedding_grad,
        *matrix_grads,
        char_vectors[:, 0:2],
        char_vectors[:, 2:4],
        char_vectors[:, 4],
        word_vectors[:, 0:2],
        word_vectors[:, 2:4],
    )


def on_device(direct, *arguments):
    char_cot, word_cot = arguments[19:]
    program = direct_program if direct else plain_program
    char_out, word_out, word_grad, *rest = program(
        *arguments[:5], arguments[5:14], arguments[14:19], char_cot, word_cot
    )
    return (char_out.reshape(char_cot.shape), word_out[None], word_grad[None], *rest)


def solution(mesh):
    rows = ("wide", "narrow")
    matrix = P(None, "narrow", "wide")
    by_rows = P(rows)
    return jax.shard_map(
        partial(on_device, mesh.shape["wide"] == 8 and mesh.shape["narrow"] == 4),
        mesh=mesh,
        in_specs=(by_rows,) * 5 + (matrix,) * 9 + (P(),) * 5 + (by_rows,) * 2,
        out_specs=(by_rows,) * 4 + (matrix,) * 9 + (P(),) * 5,
        check_vma=False,
    )
```

```python
from functools import partial

import jax
import jax.numpy as jnp
from jax import lax
from jax.experimental import pallas as pl
from jax.experimental.pallas import tpu as pltpu
from jax.sharding import PartitionSpec as P

F32 = jnp.float32
BF = jnp.bfloat16
SLOTS = 16
masked_score = -1e30
ROOT = 0.7978845608028654
CUBE = 0.044715
LANES = 128
C_QKV, C_OUT, C_UP, C_PROJ, C_DOWN, C_EMB = (0, 48), (48, 16), (64, 64), (128, 32), (160, 32), (224, 16)
C_PAIRED = (C_QKV, C_OUT, C_UP, C_PROJ)
C_ROWS = 224
HELD_0 = C_ROWS + 16
W_QKV, W_OUT, W_UP, W_DOWN = (0, 192), (192, 64), (256, 256), (512, 64)
W_ROWS = 768
CHUNK = 512
VMEM, SMALL, LARGE = 24 << 20, 12 << 20, 60 << 20
COST_FORWARD, COST_FEED, COST_MIX = 2e9, 2e9, 2e9
A_SPAN, F_SPAN = (0, 64), (64, 160)
E_ROWS = 16


def dot(left, right, l, r):
    return lax.dot_general(left, right, (((l,), (r,)), ((), ())), preferred_element_type=F32)


def nn(left, right):
    return dot(left, right, 1, 0)


def nt(left, right):
    return dot(left, right, 1, 1)


def tn(left, right):
    return dot(left, right, 0, 0)


def iota(shape, dim):
    return lax.broadcasted_iota(jnp.int32, shape, dim)


def norm_parts(states):
    centre = states - jnp.mean(states, axis=-1, keepdims=True)
    spread = jnp.mean(centre * centre, axis=-1, keepdims=True)
    root = lax.rsqrt(spread + 1e-05)
    return centre * root, root


def norm_back(grad, hat, root, gain):
    scaled = grad * gain
    inner = scaled - jnp.mean(scaled, axis=-1, keepdims=True)
    back = root * (inner - hat * jnp.mean(scaled * hat, axis=-1, keepdims=True))
    return back, jnp.sum(grad * hat, axis=0, keepdims=True), jnp.sum(grad, axis=0, keepdims=True)


def gelu_value(h):
    return 0.5 * h * (1.0 + jnp.tanh(ROOT * (h + CUBE * h * h * h)))


def gelu_both(h):
    square = h * h
    t = jnp.tanh(ROOT * (h + CUBE * square * h))
    half = 0.5 * (1.0 + t)
    slope = half + 0.5 * h * (1.0 - t * t) * (ROOT * (1.0 + 3.0 * CUBE * square))
    return h * half, slope


def softmax_rows(scores):
    shifted = jnp.exp(scores - jnp.max(scores, axis=-1, keepdims=True))
    return shifted / jnp.sum(shifted, axis=-1, keepdims=True)


def low_half(shape):
    return iota(shape, len(shape) - 1) % LANES < 64


def two_heads(x):
    low = low_half(x.shape)
    zero = jnp.zeros_like(x)
    return jnp.concatenate([jnp.where(low, x, zero), jnp.where(low, zero, x)], axis=0)


def join_heads(x):
    k = x.shape[0] // 2
    return jnp.where(low_half((k, LANES)), x[:k], x[k:])


def place(rw, ry, x_first):
    rx, rz = rw & 1, rw >> 1
    return ry * 8 + rx * 4 + rz if x_first else rx * 8 + ry * 4 + rz


def begin(copies):
    copies = [pltpu.make_async_copy(*c) for c in copies]
    for copy in copies:
        copy.start()
    return copies


def finish(copies):
    for copy in copies:
        copy.wait()


def pack_kernel(*refs):
    c0, mine, theirs = refs[10:13]
    cq, co, cu, cd, cp, wq, wo, wu, wd, emb = refs[13:23]
    finish(begin([(a, b, refs[23].at[k]) for k, (a, b) in enumerate(zip(refs[:10], refs[13:23]))]))

    def turned(x):
        return x.astype(F32).T

    for layer, (c, base) in enumerate(((c0, 0), (mine, W_ROWS))):
        for t, (row, rows) in zip((turned(cq[layer]), co[layer], turned(cu[layer]), turned(cp[layer])), C_PAIRED):
            t = t.astype(F32)
            c[base + row : base + row + rows, :] = jnp.concatenate([t[:rows], t[rows:]], axis=1).astype(BF)
        for k in range(2):
            row = base + C_DOWN[0] + 32 * k
            c[row : row + 32, :] = cd[layer, :, k * LANES : (k + 1) * LANES]
    e = emb[...].astype(F32)
    theirs[W_ROWS:, :] = mine[W_ROWS:, :]
    c0[C_EMB[0] : C_EMB[0] + 16, :] = jnp.concatenate([e[:, :LANES], e[:, LANES:]], axis=0).astype(BF)
    own = (lax.axis_index("wide") >> 1) & 1
    for layer, w in ((own, mine), (1 - own, theirs)):
        w[W_QKV[0] : W_QKV[0] + 192, :] = wq[layer]
        w[W_OUT[0] : W_OUT[0] + 64, :] = wo[layer]
        w[W_UP[0] : W_UP[0] + 256, :] = turned(wu[layer]).astype(BF)
        for k in range(4):
            row = W_DOWN[0] + 64 * k
            w[row : row + 64, :] = wd[layer, :, k * LANES : (k + 1) * LANES]


def whole(shape, dtype):
    return jax.ShapeDtypeStruct(shape, dtype)


def cost(flops, moved):
    return pl.CostEstimate(flops=int(flops), bytes_accessed=int(moved), transcendentals=0)


smem = pl.BlockSpec(memory_space=pltpu.SMEM)
vmem = pl.BlockSpec(memory_space=pltpu.VMEM)
anywhere = pl.BlockSpec(memory_space=pl.ANY)
TURNED = (1, 3, 5, 6, 8)


def pack(weights, embedding):
    weights = [m.swapaxes(1, 2) if k in TURNED else m for k, m in enumerate(weights)]
    return pl.pallas_call(
        pack_kernel,
        in_specs=[anywhere] * 10,
        out_shape=(
            whole((HELD_0, LANES), BF),
            whole((W_ROWS + C_ROWS, LANES), BF),
            whole((W_ROWS + C_ROWS, LANES), BF),
        ),
        scratch_shapes=[pltpu.VMEM(m.shape, BF) for m in (*weights, embedding)] + [pltpu.SemaphoreType.DMA((10,))],
        compiler_params=pltpu.CompilerParams(vmem_limit_bytes=LARGE),
        cost_estimate=cost(0, 4e6),
    )(*weights, embedding)


def low_vector(x):
    return x.astype(BF)


def whole_vector(x):
    return x.astype(F32)


def unpack_kernel(me, *refs):
    first, (own_word, other_word, own_out, other_out) = refs[:5], refs[5:9]
    cq, co, cu, cd, cp, wq, wo, wu, wd, emb, cg, cs, pq, wg, ws, word_out = refs[9:]
    layer_now = me[2]
    word_out[...] = jnp.where(layer_now == 1, own_out[...], other_out[...])
    both = [first[k][0 : HELD_0 + C_ROWS, :].astype(F32) for k in (0, 2, 3, 4)]
    both = (both[0] + both[1]) + (both[2] + both[3])
    c0, c1 = both[:HELD_0], both[HELD_0:]
    v = [whole_vector(ref[HELD_0 + C_ROWS :, :]) for ref in first[1:5]]
    v = (v[0] + v[1]) + (v[2] + v[3])
    for layer, c in enumerate((c0, c1)):
        for k, ref, (row, rows) in zip((0, 1, 2, 4), (cq, co, cu, cp), C_PAIRED):
            t = c[row : row + rows, :]
            t = jnp.concatenate([t[:, :64], t[:, 64:]], axis=0)
            ref[layer] = t if k in TURNED else t.T
        for k in range(2):
            row = C_DOWN[0] + 32 * k
            cd[layer, :, k * LANES : (k + 1) * LANES] = c[row : row + 32, :]
        for t in range(4):
            row = 8 * t + 4 * layer
            wg[layer, :, t * LANES : (t + 1) * LANES] = v[row : row + 2]
            ws[layer, :, t * LANES : (t + 1) * LANES] = v[row + 2 : row + 4]
        for t in range(2):
            row = 32 + 16 * t + 8 * layer
            cg[layer, :, t * LANES : (t + 1) * LANES] = v[row : row + 2]
            cs[layer, :, t * LANES : (t + 1) * LANES] = v[row + 2 : row + 4]
            pq[layer : layer + 1, t * LANES : (t + 1) * LANES] = v[row + 4 : row + 5]
    e = c0[C_EMB[0] : C_EMB[0] + 16, :]
    emb[...] = jnp.concatenate([e[:8], e[8:]], axis=1)
    for layer, w in ((layer_now, own_word), (1 - layer_now, other_word)):
        wq[layer] = w[0, W_QKV[0] : W_QKV[0] + 192, :].astype(F32)
        wo[layer] = w[0, W_OUT[0] : W_OUT[0] + 64, :].astype(F32)
        wu[layer] = w[0, W_UP[0] : W_UP[0] + 256, :].astype(F32).T
        for k in range(4):
            row = W_DOWN[0] + 64 * k
            wd[layer, :, k * LANES : (k + 1) * LANES] = w[0, row : row + 64, :].astype(F32)


def unpack(me, blocks, weights, embedding, vectors):
    shapes = [m.shape for m in weights]
    shapes = [(a, c, b) if k in TURNED else (a, b, c) for k, (a, b, c) in enumerate(shapes)]
    shapes += [embedding.shape] + [v.shape for v in vectors]
    out = pl.pallas_call(
        unpack_kernel,
        in_specs=[smem] + [vmem] * len(blocks),
        out_shape=tuple(whole(x, F32) for x in shapes) + (whole(blocks[-1].shape, BF),),
        cost_estimate=cost(0, 8e6),
    )(me, *blocks)
    return [x.swapaxes(1, 2) if k in TURNED else x for k, x in enumerate(out)]


def fold_one_kernel(keep_f, got_f, keep_a, got_a, sent_a, ours, *away):
    vector = [ref[16, 0:64, :] for ref in (sent_a, got_a)]
    vector = low_vector(whole_vector(vector[0]) + whole_vector(vector[1]))
    for part, ref in enumerate((ours, *away)):
        for k in range(4):
            at, row = 4 * part + k, k * HELD_0
            ref[row : row + 64, :] = (keep_a[at, 0:64, :].astype(F32) + got_a[at, 0:64, :].astype(F32)).astype(BF)
            ref[row + 64 : row + 224, :] = (keep_f[at].astype(F32) + got_f[at].astype(F32)).astype(BF)
            ref[row + 224 : row + 240, :] = (
                keep_a[at, 64:80, :].astype(F32) + got_a[at, 64:80, :].astype(F32)
            ).astype(BF)
        if part > 0:
            ref[4 * HELD_0 :, :] = vector


def fold_one(*operands):
    return pl.pallas_call(
        fold_one_kernel,
        out_shape=[whole((4 * HELD_0, LANES), BF)] + [whole((4 * HELD_0 + 64, LANES), BF)] * 3,
        compiler_params=pltpu.CompilerParams(vmem_limit_bytes=SMALL),
        cost_estimate=cost(0, 4e6),
    )(*operands)


def fold_two_kernel(ours, sent, over_x, over_y, over_xy, ours_1, x_1, y_1, xy_1, own, *away):
    vector = [whole_vector(ref[4 * HELD_0 :, :]) for ref in (sent, over_x, over_y, over_xy)]
    vector = ((vector[0] + vector[1]) + (vector[2] + vector[3])).astype(BF)
    for k, ref in enumerate((own, *away)):
        row = k * HELD_0
        near = [r[row : row + HELD_0, :].astype(F32) for r in (ours, over_x, over_y, over_xy)]
        ref[0:HELD_0, :] = ((near[0] + near[1]) + (near[2] + near[3])).astype(BF)
        near = [r[k].astype(F32) for r in (ours_1, x_1, y_1, xy_1)]
        ref[HELD_0 : HELD_0 + C_ROWS, :] = ((near[0] + near[1]) + (near[2] + near[3])).astype(BF)
        if k > 0:
            ref[HELD_0 + C_ROWS :, :] = vector


def fold_two(*operands):
    rows = HELD_0 + C_ROWS
    return pl.pallas_call(
        fold_two_kernel,
        out_shape=[whole((rows, LANES), BF)] + [whole((rows + 64, LANES), BF)] * 3,
        compiler_params=pltpu.CompilerParams(vmem_limit_bytes=SMALL),
        cost_estimate=cost(0, 4e6),
    )(*operands)


def fold_cores_kernel(keep, got, *out):
    for part, ref in enumerate(out):
        for k in range(4):
            ref[k] = (keep[4 * part + k].astype(F32) + got[4 * part + k].astype(F32)).astype(BF)


def fold_cores(keep, got):
    return pl.pallas_call(
        fold_cores_kernel,
        out_shape=[whole((4, *keep.shape[1:]), BF)] * 4,
        compiler_params=pltpu.CompilerParams(vmem_limit_bytes=SMALL),
        cost_estimate=cost(0, 4e6),
    )(keep, got)


def assemble(x_first, me, span, raw, mats):
    mw, my, mc = me[0], me[1] >> 1, me[1] & 1
    for w in range(8):
        for y in range(2):
            at = place(w ^ mw, y ^ my, x_first)
            cores = (mc * 16 + at, (1 - mc) * 16 + at)
            for ref, (row, rows) in zip(mats[:4], C_PAIRED):
                if ref is None:
                    continue
                row = row - span
                zero, one = (raw[k, row : row + rows, :] for k in cores)
                first = w * 2 * rows
                columns = slice(y * LANES, (y + 1) * LANES)
                ref[first : first + rows, columns] = jnp.concatenate([zero[:, :64], one[:, :64]], axis=1)
                ref[first + rows : first + 2 * rows, columns] = jnp.concatenate(
                    [zero[:, 64:], one[:, 64:]], axis=1
                )
            if mats[4] is None:
                continue
            for c, k in enumerate(cores):
                for t in range(2):
                    column = (2 * y + c) * 256 + t * LANES
                    row = C_DOWN[0] + 32 * t - span
                    mats[4][w * 32 : w * 32 + 32, column : column + LANES] = raw[k, row : row + 32, :]

def put_char(x_first, me, keep, send, span, mats):
    mw, my, mc = me[0], me[1] >> 1, me[1] & 1

    def put(at, row, rows, zero, one):
        row = row - span
        keep[at, row : row + rows, :] = jnp.where(mc == 0, zero, one)
        send[at, row : row + rows, :] = jnp.where(mc == 0, one, zero)

    for w in range(8):
        for y in range(2):
            at = place(w ^ mw, y ^ my, x_first)
            for ref, (row, rows) in zip(mats[:4], C_PAIRED):
                if ref is None:
                    continue
                columns = slice(y * LANES, (y + 1) * LANES)
                top = ref[w * 2 * rows : w * 2 * rows + rows, columns]
                bottom = ref[w * 2 * rows + rows : w * 2 * rows + 2 * rows, columns]
                put(
                    at,
                    row,
                    rows,
                    jnp.concatenate([top[:, :64], bottom[:, :64]], axis=1),
                    jnp.concatenate([top[:, 64:], bottom[:, 64:]], axis=1),
                )
            if mats[4] is None:
                continue
            for t in range(2):
                zero, one = (
                    mats[4][w * 32 : w * 32 + 32, (2 * y + c) * 256 + t * LANES : (2 * y + c) * 256 + (t + 1) * LANES]
                    for c in range(2)
                )
                put(at, C_DOWN[0] + 32 * t, 32, zero, one)


def char_positions(ids, me, x_first):
    device = ids >> 3
    rw = (device >> 2) ^ me[0]
    rn = (device & 3) ^ me[1]
    return ((rn & 1) * 16 + place(rw, rn >> 1, x_first)) * 16 + (ids & 7)


def valid_keys(lens, first):
    lane = iota((1, LANES), 1)
    length = jnp.zeros((1, LANES), jnp.int32)
    for k in range(8):
        length = jnp.where(lane // SLOTS == k, lens[0, first + k], length)
    return lane % SLOTS < length


def to_column(row):
    square = (LANES, LANES)
    return jnp.sum(jnp.where(iota(square, 0) == iota(square, 1), row, 0.0), axis=-1, keepdims=True)


def char_masks(lens, first):
    same = iota((LANES, LANES), 0) // SLOTS == iota((LANES, LANES), 1) // SLOTS
    valid = valid_keys(lens, first)
    return to_column(jnp.where(valid, 1.0, 0.0)), same & valid, same


def pool_weights(states, query, valid):
    scores = jnp.sum(states * query, axis=-1, keepdims=True)
    scores = jnp.where(valid > 0.5, scores, masked_score).reshape(-1, SLOTS, 1)
    shifted = jnp.exp(scores - jnp.max(scores, axis=1, keepdims=True))
    return shifted / jnp.sum(shifted, axis=1, keepdims=True)


def of_layer(first, gain, shift, query):
    layer = 0 if first else 1
    return gain[layer], shift[layer], query[layer : layer + 1, :]


def part_copies(parts, raw, row, rows, at, sems):
    each = 32 // len(parts)
    return [
        (part.at[:, pl.ds(row, rows)], raw.at[pl.ds(each * k, each), pl.ds(at, rows)], sems.at[k])
        for k, part in enumerate(parts)
    ]


def char_forward_kernel(first, x_first, count, *refs):
    me, lens, source = refs[:3]
    parts, refs = refs[3 : 3 + count], refs[3 + count :]
    gain, shift, query = of_layer(first, *refs[:3])
    qkv_out, mixed_out, after_out, next_out, extra_out, pooled_out, delta_out = refs[3:10]
    mats, refs = refs[10:15], refs[15:]
    hidden_here, raw, table, sems_a, sems_f, sems_e = refs
    m_qkv, m_out, m_up, m_proj, m_down = mats
    rows_all = qkv_out.shape[0]
    near = begin(part_copies(parts, raw, 0, 64, 0, sems_a))
    if first:
        near += begin(part_copies(parts, raw, C_EMB[0], 16, C_EMB[0], sems_e))
    far = begin(part_copies(parts, raw, 64, 160, 64, sems_f))
    finish(near)
    assemble(x_first, me, 0, raw, (m_qkv, m_out, None, None, None))
    if first:
        for k in range(32):
            table[k * 16 : k * 16 + 16, :] = raw[k, C_EMB[0] : C_EMB[0] + 16, :]
    for chunk in range(rows_all // CHUNK):
        span = slice(chunk * CHUNK, (chunk + 1) * CHUNK)
        halves = CHUNK // LANES
        masks = [char_masks(lens, chunk * (CHUNK // SLOTS) + 8 * h) for h in range(halves)]
        if first:
            sides = []
            for h in range(halves):
                ids = source[pl.ds(chunk * halves + h, 1), :]
                column = to_column(char_positions(ids, me, x_first).astype(F32)).astype(jnp.int32)
                lane = iota((LANES, 512), 1)
                left = jnp.where(lane == column, 1.0, 0.0).astype(BF)
                right = jnp.where(lane == column + 8, 1.0, 0.0).astype(BF)
                sides.append(jnp.concatenate([nn(left, table[...]), nn(right, table[...])], axis=1))
            x = jnp.concatenate(sides, axis=0)
            extra_out[span] = x
        else:
            x = source[span]
        hat, _ = norm_parts(x)
        normed = (hat * gain[0:1] + shift[0:1]).astype(BF)
        qkv_out[span] = nt(normed, m_qkv[...]).astype(BF)
        blocks = char_blocks(qkv_out, chunk)
        allowed = stacked([jnp.concatenate([m[1]] * 2, axis=1) for m in masks for _ in range(2)])
        scores = jnp.where(allowed, stacked([nt(q, k) for q, k, _ in blocks]) * 0.125, masked_score)
        attend = [softmax_rows(scores[:, :LANES]).astype(BF), softmax_rows(scores[:, LANES:]).astype(BF)]
        attend = jnp.concatenate(attend, axis=1)
        mixed = [nn(attend[n * LANES : (n + 1) * LANES], v) for n, (_, _, v) in enumerate(blocks)]
        mixed = in_rows(mixed, halves).astype(BF)
        mixed_out[span] = mixed
        after = x + nt(mixed, m_out[...])
        after_out[span] = after
        hat, _ = norm_parts(after)
        normed = (hat * gain[1:2] + shift[1:2]).astype(BF)
        if chunk == 0:
            finish(far)
            assemble(x_first, me, 0, raw, (None, None, m_up, m_proj, m_down))
        hidden_here[span] = nt(normed, m_up[...])
        states = after_out[span] + nt(gelu_value(hidden_here[span]).astype(BF), m_down[...])
        next_out[span] = states
        if not first:
            extra_out[span] = states.astype(BF)
        weights = pool_weights(states, query, jnp.concatenate([m[0] for m in masks], axis=0))
        pooled = jnp.sum(weights * states.reshape(-1, SLOTS, 256), axis=1).astype(BF)
        words = slice(chunk * (CHUNK // SLOTS), (chunk + 1) * (CHUNK // SLOTS))
        pooled_out[words] = pooled
        delta_out[words] = nt(pooled, m_proj[...])


def char_blocks(qkv, chunk):
    blocks = []
    for h in range(CHUNK // LANES):
        for pair in range(2):
            q, k, v = char_heads(qkv, chunk * CHUNK + h * LANES, pair)
            blocks.append((q, two_heads(k), two_heads(v)))
    return blocks


def char_heads(qkv, base, pair):
    return (
        qkv[base : base + LANES, t * 256 + pair * LANES : t * 256 + (pair + 1) * LANES] for t in range(3)
    )


def char_forward(first, x_first, me, lens, source, parts, gain, shift, query):
    words = lens.shape[1]
    rows = words * SLOTS
    big = [(768, BF), (256, BF), (256, F32), (256, F32), (256, F32) if first else (256, BF)]
    held = C_ROWS + (16 if first else 0)
    shapes = [whole((rows, 1024), F32)] if not first else []
    out = pl.pallas_call(
        partial(char_forward_kernel, first, x_first, len(parts)),
        in_specs=[smem, smem, vmem] + [anywhere] * len(parts) + [vmem] * 3,
        out_specs=[vmem] * (12 + len(shapes)),
        out_shape=[whole((rows, c), t) for c, t in big]
        + [whole((words, 256), BF), whole((words, 512), F32)]
        + [whole(s, BF) for s in MATS]
        + shapes,
        scratch_shapes=([pltpu.VMEM((rows, 1024), F32)] if first else [])
        + [pltpu.VMEM((32, held, LANES), BF), pltpu.VMEM((512, LANES) if first else (16, LANES), BF)]
        + [pltpu.SemaphoreType.DMA((8,))] * 3,
        compiler_params=pltpu.CompilerParams(vmem_limit_bytes=VMEM),
        cost_estimate=cost(COST_FORWARD, 12e6),
    )(me, lens, source, *parts, gain, shift, query)
    qkv, mixed, after, states, extra, pooled, delta = out[:7]
    mats, hidden = out[7:12], out[12:]
    if first:
        return (extra, qkv, mixed, after, states, pooled, *hidden), delta, mats
    return (source, qkv, mixed, after, states, pooled, *hidden), delta, mats, extra


MATS = ((768, 256), (256, 256), (1024, 256), (512, 256), (256, 1024))


def pool_back(states, query, valid, grad):
    weights = pool_weights(states, query, valid)
    cube = states.reshape(-1, SLOTS, 256)
    wide = grad.reshape(-1, 1, 256)
    by_weight = jnp.sum(cube * wide, axis=-1, keepdims=True)
    by_score = weights * (by_weight - jnp.sum(weights * by_weight, axis=1, keepdims=True))
    added = weights * wide + by_score * query.reshape(1, 1, 256)
    by_query = jnp.sum((by_score * cube).reshape(states.shape), axis=0, keepdims=True)
    return added.reshape(states.shape), by_query


def accumulate(ref, value, chunk):
    if chunk == 0:
        ref[...] = value
    else:
        ref[...] += value


def char_feed_kernel(first, x_first, at, me, lens, word_own, word_other, *refs):
    pooled_in, grad_in, next_in, after_in, m_up, m_proj, m_down = refs[:7]
    gain, shift, query = of_layer(first, *refs[7:10])
    refs = refs[10:]
    if first:
        word_out, refs = refs[0], refs[1:]
    else:
        hidden_in, refs = refs[0], refs[1:]
    grad_out, keep, send, vectors, t_up, t_proj, t_down, a_up, a_proj, a_down = refs
    rows_all = grad_out.shape[0]
    words_all = rows_all // SLOTS
    word_grad = jnp.where(
        me[2] == (0 if first else 1),
        word_own[at[0] * words_all : (at[0] + 1) * words_all],
        word_other[at[1] * words_all : (at[1] + 1) * words_all],
    )
    if first:
        word_out[...] = word_grad
    vectors[...] = jnp.zeros(vectors.shape, F32)
    low_word = word_grad.astype(BF)
    a_proj[...] = tn(low_word, pooled_in[...])
    grad_pooled = nn(low_word, m_proj[...])
    for chunk in range(rows_all // CHUNK):
        span = slice(chunk * CHUNK, (chunk + 1) * CHUNK)
        words = CHUNK // SLOTS
        valid = [valid_keys(lens, chunk * words + 8 * h) for h in range(CHUNK // LANES)]
        valid = jnp.concatenate([to_column(jnp.where(v, 1.0, 0.0)) for v in valid], axis=0)
        added, by_query = pool_back(next_in[span], query, valid, grad_pooled[chunk * words : (chunk + 1) * words])
        grad = grad_in[span].astype(F32) + added
        vectors[4:5, :] += by_query
        low = grad.astype(BF)
        hat, root = norm_parts(after_in[span])
        normed = (hat * gain[1:2] + shift[1:2]).astype(BF)
        act, slope = gelu_both(nt(normed, m_up[...]) if first else hidden_in[span])
        accumulate(a_down, tn(low, act.astype(BF)), chunk)
        by_hidden = (slope * nn(low, m_down[...])).astype(BF)
        accumulate(a_up, tn(normed, by_hidden), chunk)
        back, by_gain, by_shift = norm_back(nn(by_hidden, m_up[...]), hat, root, gain[1:2])
        grad_out[span] = grad + back
        vectors[1:2, :] += by_gain
        vectors[3:4, :] += by_shift
    t_up[...] = a_up[...].T.astype(BF)
    t_proj[...] = a_proj[...].astype(BF)
    t_down[...] = a_down[...].astype(BF)
    put_char(x_first, me, keep, send, F_SPAN[0], (None, None, t_up, t_proj, t_down))


def char_feed(first, x_first, me, lens, grad, words, at, saved, mats, vectors):
    after, states, pooled, *hidden = saved
    rows = after.shape[0]
    outs = [whole((rows, 256), F32)]
    if first:
        outs = [whole((rows // SLOTS, 512), F32)] + outs
    held = F_SPAN[1]
    return pl.pallas_call(
        partial(char_feed_kernel, first, x_first, at),
        in_specs=[smem, smem] + [vmem] * (12 + len(hidden)),
        out_specs=[vmem] * (len(outs) + 3),
        out_shape=outs + [whole((16, held, LANES), BF)] * 2 + [whole((8, 256), F32)],
        scratch_shapes=[pltpu.VMEM(MATS[k], BF) for k in (2, 3, 4)]
        + [pltpu.VMEM(x, F32) for x in ((256, 1024), (512, 256), (256, 1024))],
        compiler_params=pltpu.CompilerParams(vmem_limit_bytes=VMEM),
        cost_estimate=cost(COST_FEED, 12e6),
    )(me, lens, *words, pooled, grad, states, after, *mats[2:], *vectors, *hidden)


def char_mix_kernel(first, x_first, me, lens, grad_in, mixed_in, qkv_in, x_in, m_qkv, m_out, *refs):
    gain, shift, _ = of_layer(first, *refs[:3])
    vec_feed, refs = refs[3], refs[4:]
    if first:
        ids, word_0, word_1, char_1, keep, send, vectors = refs[:7]
        refs = refs[7:]
    else:
        keep_feed, send_feed, grad_out, keep, send, vectors = refs[:6]
        refs = refs[6:]
    t_qkv, t_out, a_qkv, a_out, a_table = refs
    rows_all = grad_in.shape[0]
    vectors[...] = vec_feed[...]
    for chunk in range(rows_all // CHUNK):
        span = slice(chunk * CHUNK, (chunk + 1) * CHUNK)
        grad = grad_in[span]
        low = grad.astype(BF)
        accumulate(a_out, tn(low, mixed_in[span]), chunk)
        by_mixed = nn(low, m_out[...]).astype(BF)
        blocks = char_blocks(qkv_in, chunk)
        masks = [char_masks(lens, chunk * (CHUNK // SLOTS) + 8 * h) for h in range(CHUNK // LANES)]
        allowed = jnp.concatenate([same & (valid > 0.5) for valid, _, same in masks for _ in range(2)], axis=1)
        grads = [
            by_mixed[h * LANES : (h + 1) * LANES, pair * LANES : (pair + 1) * LANES]
            for h in range(CHUNK // LANES)
            for pair in range(2)
        ]
        spans = [slice(n * LANES, (n + 1) * LANES) for n in range(len(blocks))]
        scores = jnp.concatenate([nt(k, q) for q, k, _ in blocks], axis=1)
        by_attend = jnp.concatenate([nt(v, g) for g, (_, _, v) in zip(grads, blocks)], axis=1)
        attend, by_scores = [], []
        for h in range(2):
            part = jnp.where(allowed, scores[h * LANES : (h + 1) * LANES] * 0.125, masked_score)
            shifted = jnp.exp(part - jnp.max(part, axis=0, keepdims=True))
            part = shifted / jnp.sum(shifted, axis=0, keepdims=True)
            product = part * by_attend[h * LANES : (h + 1) * LANES]
            by_scores.append((product - part * jnp.sum(product, axis=0, keepdims=True)).astype(BF))
            attend.append(part.astype(BF))
        attend, by_scores = stacked(attend), stacked(by_scores)
        by_q = [tn(by_scores[:, n], k) * 0.125 for n, (_, k, _) in zip(spans, blocks)]
        by_k = [join_heads(nn(by_scores[:, n], q)) * 0.125 for n, (q, _, _) in zip(spans, blocks)]
        by_v = [join_heads(nn(attend[:, n], g)) for n, g in zip(spans, grads)]
        by_qkv = jnp.concatenate([in_rows(x, CHUNK // LANES) for x in (by_q, by_k, by_v)], axis=1).astype(BF)
        hat, root = norm_parts(x_in[span])
        normed = (hat * gain[0:1] + shift[0:1]).astype(BF)
        accumulate(a_qkv, tn(normed, by_qkv), chunk)
        back, by_gain, by_shift = norm_back(nn(by_qkv, m_qkv[...]), hat, root, gain[0:1])
        grad = grad + back
        vectors[0:1, :] += by_gain
        vectors[2:3, :] += by_shift
        if first:
            for h in range(CHUNK // LANES):
                at = char_positions(ids[pl.ds(chunk * (CHUNK // LANES) + h, 1), :], me, x_first)
                row = iota((512, LANES), 0)
                part = grad[h * LANES : (h + 1) * LANES]
                high = part.astype(BF)
                rest = (part - high.astype(F32)).astype(BF)
                both = jnp.concatenate([high, rest], axis=0)
                for side in range(2):
                    hot = jnp.where(row == at + 8 * side, 1.0, 0.0).astype(BF)
                    hot = jnp.concatenate([hot, hot], axis=1)
                    accumulate(a_table, nn(hot, both[:, side * LANES : (side + 1) * LANES]), chunk + h + side)
        else:
            grad_out[span] = grad
    t_qkv[...] = a_qkv[...].T.astype(BF)
    t_out[...] = a_out[...].astype(BF)
    put_char(x_first, me, keep, send, A_SPAN[0], (t_qkv, t_out, None, None, None))
    if first:
        row = A_SPAN[1]
        for k in range(16):
            keep[k, row : row + E_ROWS, :] = a_table[k * 16 : k * 16 + 16, :].astype(BF)
            send[k, row : row + E_ROWS, :] = a_table[256 + k * 16 : 272 + k * 16, :].astype(BF)
        word = jnp.concatenate([word_0[0:4], word_1[0:4]], axis=0)
        char = jnp.concatenate([vectors[...], char_1[...]], axis=0)
        tiles = [x[:, t * LANES : (t + 1) * LANES] for x in (word, char) for t in range(x.shape[1] // LANES)]
        vector = low_vector(jnp.concatenate(tiles, axis=0))
        held = send.shape[1]
        send[16, 0:64, :] = vector
        send[16, 64:, :] = jnp.zeros((held - 64, LANES), BF)
    else:
        keep[:, F_SPAN[0] :, :] = keep_feed[...]
        send[:, F_SPAN[0] :, :] = send_feed[...]


def char_mix(first, x_first, me, lens, grad, saved, mats, vectors, others):
    x, qkv, mixed = saved
    rows = x.shape[0]
    if first:
        outs, held, sends = [], A_SPAN[1] + E_ROWS, 17
    else:
        outs, held, sends = [whole((rows, 256), F32)], C_ROWS, 16
    return pl.pallas_call(
        partial(char_mix_kernel, first, x_first),
        in_specs=[smem, smem] + [vmem] * (9 + len(others)),
        out_specs=[vmem] * (len(outs) + 3),
        out_shape=outs
        + [whole((16, held, LANES), BF), whole((sends, held, LANES), BF), whole((8, 256), F32)],
        scratch_shapes=[pltpu.VMEM(MATS[k], BF) for k in (0, 1)]
        + [pltpu.VMEM(x, F32) for x in ((256, 768), (256, 256), (512 if first else 8, LANES))],
        compiler_params=pltpu.CompilerParams(vmem_limit_bytes=VMEM),
        cost_estimate=cost(COST_MIX, 12e6),
    )(me, lens, grad, mixed, qkv, x, *mats[:2], *vectors, *others)


def char_middle_kernel(me, lens, *refs):
    feed_1, refs = refs[:13], refs[13:]
    mix_1, refs = refs[:8], refs[8:]
    feed_0, refs = refs[:11], refs[11:]
    mix_out, feed_out, refs = refs[:3], refs[3:8], refs[8:]
    grad_feed, grad_mix, keep, send, vectors = refs[:5]
    mix_scratch, feed_scratch = refs[5:10], refs[10:]
    char_feed_kernel(
        False, True, (0, 1), me, lens, *feed_1, grad_feed, keep, send, vectors, *feed_scratch
    )
    mixed, qkv, x, m_qkv, m_out, *gains = mix_1
    char_mix_kernel(
        *(False, True, me, lens, grad_feed, mixed, qkv, x, m_qkv, m_out, *gains, vectors, keep, send),
        *(grad_mix, *mix_out, *mix_scratch),
    )
    char_feed_kernel(True, True, (0, 0), me, lens, *feed_0[:3], grad_mix, *feed_0[3:], *feed_out, *feed_scratch)


def char_middle(me, lens, grad, words_1, saved_1, mats_1, words_0, saved_0, mats_0, vectors):
    x, qkv, mixed, after_1, states_1, pooled_1, hidden_1 = saved_1
    after, states, pooled = saved_0
    rows = x.shape[0]
    feed = [whole((16, F_SPAN[1], LANES), BF)] * 2 + [whole((8, 256), F32)]
    return pl.pallas_call(
        char_middle_kernel,
        in_specs=[smem, smem] + [vmem] * 32,
        out_specs=[vmem] * 8,
        out_shape=[whole((16, C_ROWS, LANES), BF)] * 2
        + [whole((8, 256), F32), whole((rows // SLOTS, 512), F32), whole((rows, 256), F32)]
        + feed,
        scratch_shapes=[pltpu.VMEM((rows, 256), F32)] * 2
        + [pltpu.VMEM(x.shape, x.dtype) for x in feed]
        + [pltpu.VMEM(MATS[k], BF) for k in (0, 1)]
        + [pltpu.VMEM(x, F32) for x in ((256, 768), (256, 256), (8, LANES))]
        + [pltpu.VMEM(MATS[k], BF) for k in (2, 3, 4)]
        + [pltpu.VMEM(x, F32) for x in ((256, 1024), (512, 256), (256, 1024))],
        compiler_params=pltpu.CompilerParams(vmem_limit_bytes=VMEM),
        cost_estimate=cost(COST_MIX + 2 * COST_FEED, 36e6),
    )(
        *(me, lens, *words_1, pooled_1, grad, states_1, after_1, *mats_1[2:], *vectors, hidden_1),
        *(mixed, qkv, x, *mats_1[:2], *vectors),
        *(*words_0, pooled, states, after, *mats_0[2:], *vectors),
    )


def fetch_word(me, parts, upper, down, sems):
    for k, part in enumerate(parts):
        rc, far, ry, rx = k >> 3, (k >> 2) & 1, (k >> 1) & 1, k & 1

        def one(s, _, part=part, rc=rc, far=far, ry=ry, rx=rx):
            w, n = ((far * 2 + s) * 2 + rx) ^ me[0], (ry * 2 + rc) ^ me[1]
            block = part.at[s]
            column = pl.ds(pl.multiple_of(n * LANES, LANES), LANES)
            for which, base, (row, rows) in ((0, 0, W_QKV), (1, 1536, W_OUT), (2, 2048, W_UP)):
                to = pl.ds(pl.multiple_of(base + w * rows, 64), rows)
                pltpu.make_async_copy(block.at[pl.ds(row, rows)], upper.at[to, column], sems.at[which]).start()
            for t in range(4):
                column = pl.ds(pl.multiple_of(n * 512 + t * LANES, LANES), LANES)
                to = pl.ds(pl.multiple_of(w * 64, 64), 64)
                pltpu.make_async_copy(
                    block.at[pl.ds(W_DOWN[0] + 64 * t, 64)], down.at[to, column], sems.at[3]
                ).start()
            return 0

        lax.fori_loop(0, 2, one, 0)
    return [
        pltpu.make_async_copy(ref, ref, sems.at[k])
        for k, ref in enumerate((upper.at[pl.ds(0, 1536)], upper.at[pl.ds(1536, 512)], upper.at[pl.ds(2048, 2048)], down))
    ]


def word_allowed(docs, words):
    shape = (words, 2 * words)
    i, j = iota(shape, 0).astype(F32), (iota(shape, 1) % words).astype(F32)
    end = jnp.zeros((1, 1), F32)
    of_i, of_j = jnp.zeros(shape, jnp.int32), jnp.zeros(shape, jnp.int32)
    for k in range(docs.shape[1]):
        end = end + docs[:, k : k + 1]
        of_i = of_i + (i >= end).astype(jnp.int32)
        of_j = of_j + (j >= end).astype(jnp.int32)
    return (of_i == of_j) & (j <= i)


def docs_of(states, documents):
    return [x[2, 0:1, 0:documents].astype(F32) for x in states]


def by_half(x, reduce, fill):
    low = low_half(x.shape)
    left = reduce(jnp.where(low, x, fill), axis=-1, keepdims=True)
    right = reduce(jnp.where(low, fill, x), axis=-1, keepdims=True)
    return jnp.where(low, left, right)


def word_blocks(qkv, allowed):
    rows = qkv.shape[0] // len(allowed)
    blocks = []
    for r in range(len(allowed)):
        for pair in range(4):
            q, k, v = word_heads(qkv, r * rows, rows, pair)
            blocks.append((q, two_heads(k), two_heads(v)))
    return blocks, jnp.concatenate([pairs for pairs in allowed for _ in range(4)], axis=0)


def stacked(parts):
    return jnp.concatenate(parts, axis=0)


def in_rows(parts, count):
    each = len(parts) // count
    return stacked([jnp.concatenate(parts[r * each : (r + 1) * each], axis=1) for r in range(count)])


def word_attend(blocks, allowed):
    scores = jnp.where(allowed, stacked([nt(q, k) for q, k, _ in blocks]) * 0.125, masked_score)
    shifted = jnp.exp(scores - by_half(scores, jnp.max, 2 * masked_score))
    return shifted / by_half(shifted, jnp.sum, 0.0)


def word_forward_body(w1, coming, upper, down, gain, shift, allowed):
    hat, root = norm_parts(w1)
    normed = (hat * gain[0:1] + shift[0:1]).astype(BF)
    await_one(coming, 0)
    qkv = nt(normed, upper[0:1536, :]).astype(BF)
    rows = w1.shape[0] // len(allowed)
    blocks, pairs = word_blocks(qkv, allowed)
    attend = word_attend(blocks, pairs).astype(BF)
    mixed = [nn(attend[n * rows : (n + 1) * rows], v) for n, (_, _, v) in enumerate(blocks)]
    mixed = in_rows(mixed, len(allowed)).astype(BF)
    await_one(coming, 1)
    w2 = w1 + nt(mixed, upper[1536:2048, :])
    hat, root = norm_parts(w2)
    normed = (hat * gain[1:2] + shift[1:2]).astype(BF)
    await_one(coming, 2)
    hidden = nt(normed, upper[2048:4096, :])
    await_one(coming, 3)
    w3 = w2 + nt(gelu_value(hidden).astype(BF), down[...])
    return qkv, mixed, w2, hidden, w3


def word_heads(qkv, row, rows, pair):
    return (qkv[row : row + rows, t * 512 + pair * LANES : t * 512 + (pair + 1) * LANES] for t in range(3))


def await_one(coming, k):
    if coming is not None:
        coming[k].wait()


def word_backward_body(grad, w1, qkv, w2, hidden, upper, down, gain, shift, allowed, vectors):
    low_2 = grad.astype(BF)
    act, slope = gelu_both(hidden)
    by_hidden = (slope * nn(low_2, down[...])).astype(BF)
    hat, root = norm_parts(w2)
    normed_2 = (hat * gain[1:2] + shift[1:2]).astype(BF)
    back, by_gain, by_shift = norm_back(nn(by_hidden, upper[2048:4096, :]), hat, root, gain[1:2])
    grad = grad + back
    vectors[1:2, :] = by_gain
    vectors[3:4, :] = by_shift
    low_1 = grad.astype(BF)
    by_mixed = nn(low_1, upper[1536:2048, :]).astype(BF)
    rows = w1.shape[0] // len(allowed)
    blocks, pairs = word_blocks(qkv, allowed)
    spans = [slice(n * rows, (n + 1) * rows) for n in range(len(blocks))]
    grads = [
        by_mixed[r * rows : (r + 1) * rows, pair * LANES : (pair + 1) * LANES]
        for r in range(len(allowed))
        for pair in range(4)
    ]
    attend = word_attend(blocks, pairs)
    product = attend * stacked([nt(g, v) for g, (_, _, v) in zip(grads, blocks)])
    by_scores = (product - attend * by_half(product, jnp.sum, 0.0)).astype(BF)
    attend = attend.astype(BF)
    by_q = [nn(by_scores[n], k) * 0.125 for n, (_, k, _) in zip(spans, blocks)]
    by_k = [join_heads(tn(by_scores[n], q)) * 0.125 for n, (q, _, _) in zip(spans, blocks)]
    by_v = [join_heads(tn(attend[n], g)) for n, g in zip(spans, grads)]
    by_qkv = jnp.concatenate([in_rows(x, len(allowed)) for x in (by_q, by_k, by_v)], axis=1).astype(BF)
    hat, root = norm_parts(w1)
    normed_1 = (hat * gain[0:1] + shift[0:1]).astype(BF)
    back, by_gain, by_shift = norm_back(nn(by_qkv, upper[0:1536, :]), hat, root, gain[0:1])
    vectors[0:1, :] = by_gain
    vectors[2:3, :] = by_shift
    return grad + back, (normed_1, by_qkv, low_1, normed_2, by_hidden, act.astype(BF), low_2)


FACTORS = (512, 1536, 512, 512, 2048, 2048, 512)


def word_weights_kernel(firsts, me, mixed_0, mixed_1, *refs):
    normed_1, by_qkv, low_1, normed_2, by_hidden, act, low_2, keep_out, send_out, keep, send, sems = refs
    leaving = []

    def leave(row, rows):
        span = pl.ds(row, rows)
        k = len(leaving)
        leaving.extend(
            begin(
                [
                    (a.at[:, span], b.at[:, span], sems.at[k + n])
                    for n, (a, b) in enumerate(((send, send_out), (keep, keep_out)))
                ]
            )
        )

    mw, my, mc = me[0], me[1] >> 1, me[1] & 1
    mixed = jnp.where(me[2] == 0, mixed_0[...], mixed_1[...])

    def put(w, row, rows, blocks):
        for y in range(2):
            at = place(w ^ mw, y ^ my, firsts[row // 384])
            zero, one = blocks(2 * y), blocks(2 * y + 1)
            keep[at, row : row + rows, :] = jnp.where(mc == 0, zero, one)
            send[at, row : row + rows, :] = jnp.where(mc == 0, one, zero)

    for pair in range(4):
        columns = slice(pair * LANES, (pair + 1) * LANES)
        part = tn(low_2[:, columns], act[...]).astype(BF)
        for k in range(2):
            for t in range(4):
                put(
                    2 * pair + k,
                    W_DOWN[0] + 64 * t,
                    64,
                    lambda n: part[k * 64 : k * 64 + 64, n * 512 + t * LANES : n * 512 + (t + 1) * LANES],
                )
    leave(*(W_DOWN[0], 256))
    for w in range(8):
        part = tn(by_hidden[:, w * 256 : (w + 1) * 256], normed_2[...]).astype(BF)
        for k in range(2):
            put(
                w,
                W_UP[0] + 128 * k,
                128,
                lambda n: part[k * 128 : k * 128 + 128, n * LANES : (n + 1) * LANES],
            )
    leave(*W_UP)
    for pair in range(4):
        columns = slice(pair * LANES, (pair + 1) * LANES)
        part = tn(low_1[:, columns], mixed).astype(BF)
        for k in range(2):
            put(
                2 * pair + k,
                W_OUT[0],
                64,
                lambda n: part[k * 64 : k * 64 + 64, n * LANES : (n + 1) * LANES],
            )
    leave(*W_OUT)
    for pair in range(4):
        part = tn(by_qkv[:, pair * 384 : (pair + 1) * 384], normed_1[...]).astype(BF)
        for k in range(2):
            put(
                2 * pair + k,
                W_QKV[0],
                192,
                lambda n: part[k * 192 : (k + 1) * 192, n * LANES : (n + 1) * LANES],
            )
    leave(*W_QKV)
    finish(leaving)


def word_weights(firsts, me, mixed_0, mixed_1, factors):
    return pl.pallas_call(
        partial(word_weights_kernel, firsts),
        in_specs=[smem] + [vmem] * 9,
        out_specs=[anywhere] * 2,
        out_shape=[whole((16, W_ROWS, LANES), BF)] * 2,
        scratch_shapes=[pltpu.VMEM((16, W_ROWS, LANES), BF)] * 2 + [pltpu.SemaphoreType.DMA((8,))],
        compiler_params=pltpu.CompilerParams(vmem_limit_bytes=VMEM),
        cost_estimate=cost(2e9, 9e6),
    )(me, mixed_0, mixed_1, *factors)


def both_deltas(refs):
    own = refs[0][...]
    return stacked([own, nt(refs[1][...], refs[2][...])]) if len(refs) > 1 else own


def swapped(x, count):
    half = x.shape[0] // 2
    return jnp.concatenate([x[half:], x[:half]], axis=0) if count == 2 else x


UPPER, DOWN = (4096, 512), (512, 2048)
word_scratch = [pltpu.SemaphoreType.DMA((4,))]


def word_fetch_kernel(me, *refs):
    *parts, upper, down, sems = refs
    finish(fetch_word(me, parts, upper, down, sems))


def word_fetch(me, parts):
    return pl.pallas_call(
        word_fetch_kernel,
        in_specs=[smem] + [anywhere] * 16,
        out_specs=[vmem] * 2,
        out_shape=[whole(UPPER, BF), whole(DOWN, BF)],
        scratch_shapes=word_scratch,
        compiler_params=pltpu.CompilerParams(vmem_limit_bytes=VMEM),
    )(me, *parts)


def word_call(kernel, count, documents, tables, operands, outs, scratch, flops, alias=None):
    return pl.pallas_call(
        partial(kernel, count, documents),
        in_specs=[smem] * len(tables) + [anywhere if x.shape[1:] == (W_ROWS, LANES) else vmem for x in operands],
        out_specs=[vmem] * len(outs),
        out_shape=[whole(shape, dtype) for shape, dtype in outs],
        scratch_shapes=scratch,
        input_output_aliases=alias or {},
        compiler_params=pltpu.CompilerParams(vmem_limit_bytes=VMEM),
        cost_estimate=cost(flops, 16e6),
    )(*tables, *operands)


def word_first_kernel(count, documents, me, *refs):
    states, refs = refs[:count], refs[count:]
    deltas, parts = refs[: 2 * count - 1], refs[2 * count - 1 :]
    docs = docs_of(states, documents)
    gain, shift, w1_out, qkv_out, mixed_out, w2_out, hidden_out, w3_out, upper, down, sems = parts[16:]
    coming = fetch_word(me, parts[:16], upper, down, sems)

    @pl.when(me[2] == 0)
    def _():
        w1 = stacked([a[0].astype(F32) for a in states]) + both_deltas(deltas)
        w1_out[...] = w1
        allowed = [word_allowed(d, w1.shape[0] // count) for d in docs]
        qkv, mixed, w2, hidden, w3 = word_forward_body(w1, coming, upper, down, gain[0], shift[0], allowed)
        qkv_out[...] = qkv
        mixed_out[...] = mixed
        w2_out[...] = w2
        hidden_out[...] = hidden
        w3_out[...] = w3

    @pl.when(me[2] != 0)
    def _():
        finish(coming)
        w3_out[...] = jnp.zeros(w3_out.shape, F32)


def word_first(me, documents, states, deltas, parts, gain, shift):
    count = len(states)
    words = count * deltas[0].shape[0]
    shapes = [(512, F32), (1536, BF), (512, BF), (512, F32), (2048, F32), (512, F32)]
    return word_call(
        word_first_kernel,
        count,
        documents,
        [me],
        [*states, *deltas, *parts, gain, shift],
        [((words, c), t) for c, t in shapes] + [(UPPER, BF), (DOWN, BF)],
        word_scratch,
        1e9,
    )


def word_last_kernel(count, documents, me, *refs):
    w_in, deltas, refs = refs[0], refs[1 : 2 * count], refs[2 * count :]
    cots, parts = refs[:count], refs[count:]
    docs = docs_of(cots, documents)
    upper, down, gain, shift, out_own, out_other, grad_out, vectors, mixed_out = parts[:9]
    factors = parts[9:]
    vectors[...] = jnp.zeros(vectors.shape, F32)

    @pl.when(me[2] == 1)
    def _():
        w1 = swapped(w_in[...], count) + both_deltas(deltas)
        rows = w1.shape[0] // count
        allowed = [word_allowed(d, rows) for d in docs]
        gains, shifts = gain[1], shift[1]
        qkv, mixed, w2, hidden, w3 = word_forward_body(w1, None, upper, down, gains, shifts, allowed)
        out_own[...] = w3[:rows].astype(BF)
        out_other[...] = w3[(count - 1) * rows :].astype(BF)
        grad = jnp.concatenate([c[1].astype(F32) for c in cots], axis=0)
        mixed_out[...] = mixed
        grad, made = word_backward_body(grad, w1, qkv, w2, hidden, upper, down, gains, shifts, allowed, vectors)
        grad_out[...] = grad
        for ref, value in zip(factors, made):
            ref[...] = value

    @pl.when(me[2] != 1)
    def _():
        for ref in (out_own, out_other, grad_out):
            ref[...] = jnp.zeros(ref.shape, ref.dtype)


def word_last(me, documents, w_in, deltas, cots, mats, gain, shift):
    count = len(cots)
    words = w_in.shape[0]
    row = words // count
    return word_call(
        word_last_kernel,
        count,
        documents,
        [me],
        [w_in, *deltas, *cots, *mats, gain, shift],
        [((row, 512), BF)] * 2
        + [((words, 512), F32), ((8, 512), F32), ((words, 512), BF)]
        + [((words, c), BF) for c in FACTORS],
        [],
        2e9,
    )


def word_back_kernel(count, documents, me, *refs):
    states, (grad_in, w1, qkv, w2, hidden), parts = refs[:count], refs[count : count + 5], refs[count + 5 :]
    docs = docs_of(states, documents)
    upper, down, gain, shift = parts[:4]
    held, parts_out = parts[4:11], parts[11:]
    grad_own, grad_other, vectors = parts_out[:3]
    factors = parts_out[3:]
    vectors[...] = jnp.zeros(vectors.shape, F32)

    @pl.when(me[2] == 0)
    def _():
        rows = w1.shape[0] // count
        grad, made = word_backward_body(
            swapped(grad_in[...], count),
            w1[...],
            qkv[...],
            w2[...],
            hidden[...],
            upper,
            down,
            gain[0],
            shift[0],
            [word_allowed(d, rows) for d in docs],
            vectors,
        )
        grad_own[...] = grad[:rows]
        grad_other[...] = grad[(count - 1) * rows :]
        for ref, value in zip(factors, made):
            ref[...] = value

    @pl.when(me[2] != 0)
    def _():
        for ref in (grad_own, grad_other):
            ref[...] = jnp.zeros(ref.shape, F32)
        for ref, value in zip(factors, held):
            ref[...] = value[...]


def word_back(me, documents, states, grad, saved, mats, gain, shift, held):
    count = len(states)
    words = grad.shape[0]
    return word_call(
        word_back_kernel,
        count,
        documents,
        [me],
        [*states, grad, *saved, *mats, gain, shift, *held],
        [((words // count, 512), F32)] * 2 + [((8, 512), F32)] + [((words, c), BF) for c in FACTORS],
        [],
        2e9,
    )


def swap(x, axis, flip):
    return lax.ppermute(x, axis, [(k, k ^ flip) for k in range(lax.axis_size(axis))])


def over_x(x):
    return swap(x, "wide", 1)


def over_y(x):
    return swap(x, "narrow", 2)


def over_core(x):
    return swap(x, "narrow", 1)


def over_pair(x):
    return swap(x, "wide", 2)


def after(x, *others):
    return lax.optimization_barrier((x, *others))[0]


def add(*terms):
    total = terms[0].astype(F32)
    for term in terms[1:]:
        total = total + term.astype(F32)
    return total.astype(BF)


def gather_z(block):
    return jnp.stack([block] + [swap(block, "wide", 2 * k) for k in (1, 2, 3)])


def gather_core(parts):
    return (*parts, *[over_core(part) for part in parts])


def two(x, x_first):
    return (over_y if x_first else over_x)(x)


def one(x, x_first):
    return (over_x if x_first else over_y)(x)


def cut(matrices, table):
    qkv, out, up, down, proj, *words = matrices

    def split(m):
        r, c = m.shape
        return m.T.reshape(8, c // 8, 4, r // 4).transpose(0, 2, 1, 3)

    def paired(m):
        b = split(m)
        c = b.shape[2]
        return b.reshape(8, 4, 2, c // 2, 64).transpose(0, 1, 3, 2, 4).reshape(8, 4, c // 2, LANES)

    def tiled(m):
        b = split(m)
        c, r = b.shape[2:]
        return b.reshape(8, 4, c, r // LANES, LANES).transpose(0, 1, 3, 2, 4).reshape(8, 4, -1, LANES)

    char = [paired(qkv), paired(out), paired(up), paired(proj), tiled(down)]
    if table is not None:
        char.append(table.reshape(8, 4, 8, 2, LANES).transpose(0, 1, 3, 2, 4).reshape(8, 4, 16, LANES))
    word = [tiled(m) for m in words]
    return [ordered(jnp.concatenate(x, axis=2)) for x in (char, word)]


def ordered(blocks):
    b = blocks.reshape(4, 2, 2, 2, *blocks.shape[2:]).transpose(3, 2, 1, 0, 4, 5)
    return b.reshape(32, *blocks.shape[2:])


def uncut(blocks, is_char, with_table):
    b = blocks.reshape(2, 2, 2, 4, *blocks.shape[1:]).transpose(3, 2, 1, 0, 4, 5)
    b = b.reshape(8, 4, *blocks.shape[1:])

    def joined(x):
        c, r = x.shape[2:]
        return x.transpose(0, 2, 1, 3).reshape(8 * c, 4 * r).T

    def paired(x):
        c = x.shape[2]
        return joined(x.reshape(8, 4, c, 2, 64).transpose(0, 1, 3, 2, 4).reshape(8, 4, 2 * c, 64))

    def tiled(x, tiles):
        c = x.shape[2] // tiles
        return joined(x.reshape(8, 4, tiles, c, LANES).transpose(0, 1, 3, 2, 4).reshape(8, 4, c, tiles * LANES))

    def rows(span, count=None):
        return b[:, :, span[0] : span[0] + (count or span[1])]

    if not is_char:
        return [tiled(rows(W_QKV), 1), tiled(rows(W_OUT), 1), tiled(rows(W_UP), 1), tiled(rows(W_DOWN, 256), 4)], None
    table = None
    if with_table:
        table = rows(C_EMB).reshape(32, 2, 8, LANES).transpose(0, 2, 1, 3).reshape(256, 256)
    qkv, out, up, proj = (paired(rows(span)) for span in C_PAIRED)
    return [qkv, out, up, tiled(rows(C_DOWN, 64), 2), proj], table


def over_xy(x):
    flip = lax.axis_size("narrow") + 2
    return lax.ppermute(x, ("wide", "narrow"), [(k, k ^ flip) for k in range(lax.axis_size(("wide", "narrow")))])


together = lax.optimization_barrier


def whole_chip(z):
    return [z, over_x(z), over_y(z), over_xy(z)]


def both_cores(near):
    near = jnp.concatenate(near, axis=0)
    return near, over_core(near)


def three(word_states, word_cot, doc_lengths):
    words, width = word_states.shape[1:]
    docs = jnp.pad(doc_lengths.astype(BF), ((0, words - 1), (0, width - doc_lengths.shape[1])))
    return jnp.stack([word_states[0], word_cot[0], docs])


def direct_program(
    word_states, character_ids, word_lengths, doc_lengths, embedding, weights, vectors, char_cot, word_cot
):
    char_gains, char_shifts, pool_query, word_gains, word_shifts = vectors
    vectors_char = (char_gains, char_shifts, pool_query)
    vectors_word = (word_gains, word_shifts)
    width = char_cot.shape[3]
    wide = lax.axis_index("wide")
    me = jnp.stack([wide, lax.axis_index("narrow"), (wide >> 1) & 1]).astype(jnp.int32)
    firsts = (True, False)
    f0, f1 = firsts
    c0, mine, theirs = pack(weights, embedding)
    pair = three(word_states, word_cot, doc_lengths)
    ids = character_ids.reshape(-1, LANES)
    got = over_pair(theirs)
    z0 = gather_z(c0)
    word = jnp.stack([mine, got])
    z0, word, ids, pair = together((z0, word, ids, pair))
    near_0 = whole_chip(z0)
    far = swap(word, "wide", 4)
    word_near = whole_chip(word[:, :W_ROWS])
    other_pair = over_pair(pair)
    near_0, far, word_near, other_pair = together((near_0, far, word_near, other_pair))
    char_0 = gather_core(near_0)
    far_near = whole_chip(far[:, :W_ROWS])
    char_0, word_near = together((char_0, word_near))
    saved_0, delta_0, mats_0 = char_forward(True, True, me, word_lengths, ids, char_0, *vectors_char)
    delta_0, far_near, word, far, word_near, pooled = together((delta_0, far_near, word, far, word_near, saved_0[5]))
    other_delta_0 = over_pair(pooled)
    word_cores = [over_core(part) for part in word_near]
    far_cores = [over_core(part) for part in far_near]
    z1 = jnp.concatenate([word[:, W_ROWS:], far[:, W_ROWS:]], axis=0)
    word_cores, far_cores, other_delta_0, z1 = together((word_cores, far_cores, other_delta_0, z1))
    near_1 = whole_chip(z1)
    word_parts = [*word_near, *far_near, *word_cores, *far_cores]
    docs = doc_lengths.shape[1]
    pairs = [pair, other_pair]
    *word_saved, w3, upper, down = word_first(me, docs, pairs, [delta_0, other_delta_0, mats_0[3]], word_parts, *vectors_word)
    near_1, w3 = together((near_1, w3))
    char_1 = both_cores(near_1)
    char_1, states = together((char_1, saved_0[4]))
    saved_1, delta_1, mats_1, char_out = char_forward(False, True, me, word_lengths, states, char_1, *vectors_char)
    other_w3 = over_pair(w3)
    other_delta_1 = over_pair(saved_1[5])
    out_own, out_other, grad_1, word_vec_1, mixed_1, *held = word_last(
        me, docs, other_w3, [delta_1, other_delta_1, mats_1[3]], pairs, (upper, down), *vectors_word
    )
    w1, qkv, mixed_0, w2, hidden = word_saved
    got_1 = over_pair(grad_1)
    grad_own, grad_other, word_vec_0, *factors = word_back(
        me, docs, pairs, got_1, (w1, qkv, w2, hidden), (upper, down), *vectors_word, held
    )
    keep, send = word_weights(firsts, me, mixed_0, mixed_1, factors)
    got = over_core(send)
    got_0 = over_pair(grad_other)
    out_other = over_pair(out_other)
    cot = char_cot[0].reshape(-1, width)
    got, keep, got_0, out_other = together((got, keep, got_0, out_other))
    pieces = []
    for h in range(2):
        span = slice(384 * h, 384 * h + 384)
        pieces += [add(keep[k : k + 8, span], got[k : k + 8, span]) for k in (0, 8)]
    pieces, cot = together((pieces, cot))
    pieces[1], pieces[3] = two(pieces[1], f0), two(pieces[3], f1)
    keep_1, send_1, char_vec_1, word_grad, grad, keep_f0, send_f0, vec_0 = char_middle(
        me, word_lengths, cot, (grad_1, got_1), saved_1, mats_1, (grad_own, got_0), saved_0[3:], mats_0, vectors_char
    )
    pieces, grad, send_1, send_f0 = together((pieces, grad, send_1, send_f0))
    pieces = [add(a[k : k + 4], b[k : k + 4]) for a, b in (pieces[:2], pieces[2:]) for k in (0, 4)]
    pieces, send_1, send_f0 = together((pieces, send_1, send_f0))
    got_1 = over_core(send_1)
    got_f0 = over_core(send_f0)
    pieces[1], pieces[3] = one(pieces[1], f0), one(pieces[3], f1)
    grad, got_1, got_f0, keep_1 = together((grad, got_1, got_f0, keep_1))
    own_1, *away_1 = fold_cores(keep_1, got_1)
    own_1, away_1, grad = together((own_1, away_1, grad))
    away_1 = [over_x(away_1[0]), over_y(away_1[1]), over_xy(away_1[2])]
    keep_0, send_0, _ = char_mix(
        True,
        True,
        me,
        word_lengths,
        grad,
        saved_0[:3],
        mats_0,
        vectors_char,
        (vec_0, ids, word_vec_0, word_vec_1, char_vec_1),
    )
    pieces, send_0 = together((pieces, send_0))
    got_0 = over_core(send_0)
    ours, away = (
        jnp.concatenate([add(a[k : k + 2], b[k : k + 2]) for a, b in (pieces[:2], pieces[2:])], axis=1) for k in (0, 2)
    )
    got_0, away = together((got_0, away))
    away = swap(away, "wide", 4)
    own_0, *away_0 = fold_one(keep_f0, got_f0, keep_0, got_0, send_0)
    away_0, away_1 = together((away_0, away_1))
    sent = away_0[0]
    moved = (over_x(away_0[0]), over_y(away_0[1]), over_xy(away_0[2]))
    own_0, *away_0 = fold_two(own_0, sent, *moved, own_1, *away_1)
    away_0, away = together((away_0, away))
    ours, away = (add(ours[k : k + 1], away[k : k + 1]) for k in (0, 1))
    away = over_pair(away)
    first = [own_0, away_0[0]] + [swap(away_0[k - 1], "wide", 2 * k) for k in (1, 2, 3)]
    out = unpack(me, [*first, ours, away, out_own, out_other], weights, embedding, vectors)
    return (char_out, out[-1], word_grad, out[9], *out[:9], *out[10:15])


def plain_program(
    word_states, character_ids, word_lengths, doc_lengths, embedding, weights, vectors, char_cot, word_cot
):
    char_gains, char_shifts, pool_query, word_gains, word_shifts = vectors
    width = char_cot.shape[3]
    both = ("wide", "narrow")
    firsts = (True, True)
    at = [jnp.array([0, 0, layer], jnp.int32) for layer in range(2)]
    table = lax.all_gather(embedding, both, axis=0, tiled=True)
    full = [lax.all_gather(lax.all_gather(m, "narrow", axis=1, tiled=True), "wide", axis=2, tiled=True) for m in weights]
    chars, words = [], []
    for layer in range(2):
        char, word = cut([m[layer] for m in full], table if layer == 0 else None)
        chars.append([char[8 * k : 8 * k + 8] for k in range(4)])
        words.append([word[k : k + 2] for c in (0, 16) for z in (0, 2) for k in range(c + z, c + z + 16, 4)])
    ids = character_ids.reshape(-1, LANES)
    vectors_char = (char_gains, char_shifts, pool_query)
    vectors_word = (word_gains, word_shifts)
    saved_0, delta_0, mats_0 = char_forward(True, True, at[0], word_lengths, ids, chars[0], *vectors_char)
    states = saved_0[4]
    saved_1, delta_1, mats_1, char_out = char_forward(False, True, at[0], word_lengths, states, chars[1], *vectors_char)
    docs = doc_lengths.shape[1]
    pair = [three(word_states, word_cot, doc_lengths)]
    *word_saved, w3, upper, down = word_first(at[0], docs, pair, [delta_0], words[0], *vectors_word)
    word_out, _, grad_1, word_vec_1, mixed_1, *held = word_last(
        at[1], docs, w3, [delta_1], pair, word_fetch(at[1], words[1]), *vectors_word
    )
    word_mats = (upper, down)
    w1, qkv, mixed_0, w2, hidden = word_saved
    grad_0, _, word_vec_0, *factors = word_back(
        at[0], docs, pair, grad_1, (w1, qkv, w2, hidden), word_mats, *vectors_word, held
    )
    words = [word_weights(firsts, at[0], mixed, mixed, made) for mixed, made in ((mixed_0, factors), (mixed_1, held))]
    cot = char_cot[0].reshape(-1, width)
    grad, keep_f, send_f, vec_1 = char_feed(
        False, True, at[1], word_lengths, cot, (grad_1, grad_1), (0, 0), saved_1[3:], mats_1, vectors_char
    )
    grad, keep_1, send_1, char_vec_1 = char_mix(
        False, True, at[1], word_lengths, grad, saved_1[:3], mats_1, vectors_char, (vec_1, keep_f, send_f)
    )
    word_grad, grad, keep_f, send_f, vec_0 = char_feed(
        True, True, at[0], word_lengths, grad, (grad_0, grad_0), (0, 0), saved_0[3:], mats_0, vectors_char
    )
    keep_0, send_0, _ = char_mix(
        True,
        True,
        at[0],
        word_lengths,
        grad,
        saved_0[:3],
        mats_0,
        vectors_char,
        (vec_0, ids, word_vec_0, word_vec_1, char_vec_1),
    )
    summed = lax.psum(whole_vector(send_0[16, :64]), both)
    keep_0, send_0 = (
        jnp.concatenate([a[:16, :64], f, a[:16, 64:]], axis=1) for a, f in ((keep_0, keep_f), (send_0, send_f))
    )
    blocks = ((keep_0, send_0), (keep_1, send_1), *words)
    full = [uncut(jnp.concatenate(g), k < 2, k == 0) for k, g in enumerate(blocks)]
    matrix_grads = [
        lax.psum_scatter(
            lax.psum_scatter(jnp.stack([a, b]), "wide", scatter_dimension=2, tiled=True),
            "narrow",
            scatter_dimension=1,
            tiled=True,
        ).astype(F32)
        for a, b in zip(full[0][0] + full[2][0], full[1][0] + full[3][0])
    ]
    embedding_grad = lax.psum_scatter(full[0][1].astype(F32), both, scatter_dimension=0, tiled=True)
    word_vectors = summed[:32].reshape(4, 2, 4, LANES).transpose(1, 2, 0, 3).reshape(2, 4, 512)
    char_vectors = summed[32:].reshape(2, 2, 8, LANES).transpose(1, 2, 0, 3).reshape(2, 8, 256)
    return (
        char_out,
        word_out,
        word_grad,
        embedding_grad,
        *matrix_grads,
        char_vectors[:, 0:2],
        char_vectors[:, 2:4],
        char_vectors[:, 4],
        word_vectors[:, 0:2],
        word_vectors[:, 2:4],
    )


def on_device(direct, *arguments):
    char_cot, word_cot = arguments[19:]
    program = direct_program if direct else plain_program
    char_out, word_out, word_grad, *rest = program(
        *arguments[:5], arguments[5:14], arguments[14:19], char_cot, word_cot
    )
    return (char_out.reshape(char_cot.shape), word_out[None], word_grad[None], *rest)


def solution(mesh):
    rows = ("wide", "narrow")
    matrix = P(None, "narrow", "wide")
    by_rows = P(rows)
    return jax.shard_map(
        partial(on_device, mesh.shape["wide"] == 8 and mesh.shape["narrow"] == 4),
        mesh=mesh,
        in_specs=(by_rows,) * 5 + (matrix,) * 9 + (P(),) * 5 + (by_rows,) * 2,
        out_specs=(by_rows,) * 4 + (matrix,) * 9 + (P(),) * 5,
        check_vma=False,
    )
```

```python
from functools import partial

import jax
import jax.numpy as jnp
from jax import lax
from jax.experimental import pallas as pl
from jax.experimental.pallas import tpu as pltpu
from jax.sharding import PartitionSpec as P

F32 = jnp.float32
BF = jnp.bfloat16
SLOTS = 16
masked_score = -1e30
ROOT = 0.7978845608028654
CUBE = 0.044715
LANES = 128
C_QKV, C_OUT, C_UP, C_PROJ, C_DOWN, C_EMB = (0, 48), (48, 16), (64, 64), (128, 32), (160, 32), (224, 16)
C_PAIRED = (C_QKV, C_OUT, C_UP, C_PROJ)
C_ROWS = 224
HELD_0 = C_ROWS + 16
W_QKV, W_OUT, W_UP, W_DOWN = (0, 192), (192, 64), (256, 256), (512, 64)
W_ROWS = 768
CHUNK = 512
VMEM, SMALL, LARGE = 18 << 20, 6 << 20, 60 << 20
COST_FORWARD, COST_FEED, COST_MIX = 2e9, 2e9, 2e9
A_SPAN, F_SPAN = (0, 64), (64, 160)
E_ROWS = 16


def dot(left, right, l, r):
    return lax.dot_general(left, right, (((l,), (r,)), ((), ())), preferred_element_type=F32)


def nn(left, right):
    return dot(left, right, 1, 0)


def nt(left, right):
    return dot(left, right, 1, 1)


def tn(left, right):
    return dot(left, right, 0, 0)


def iota(shape, dim):
    return lax.broadcasted_iota(jnp.int32, shape, dim)


def norm_parts(states):
    centre = states - jnp.mean(states, axis=-1, keepdims=True)
    spread = jnp.mean(centre * centre, axis=-1, keepdims=True)
    root = lax.rsqrt(spread + 1e-05)
    return centre * root, root


def norm_back(grad, hat, root, gain):
    scaled = grad * gain
    inner = scaled - jnp.mean(scaled, axis=-1, keepdims=True)
    back = root * (inner - hat * jnp.mean(scaled * hat, axis=-1, keepdims=True))
    return back, jnp.sum(grad * hat, axis=0, keepdims=True), jnp.sum(grad, axis=0, keepdims=True)


def gelu_value(h):
    return 0.5 * h * (1.0 + jnp.tanh(ROOT * (h + CUBE * h * h * h)))


def gelu_both(h):
    square = h * h
    t = jnp.tanh(ROOT * (h + CUBE * square * h))
    half = 0.5 * (1.0 + t)
    slope = half + 0.5 * h * (1.0 - t * t) * (ROOT * (1.0 + 3.0 * CUBE * square))
    return h * half, slope


def softmax_rows(scores):
    shifted = jnp.exp(scores - jnp.max(scores, axis=-1, keepdims=True))
    return shifted / jnp.sum(shifted, axis=-1, keepdims=True)


def low_half(shape):
    return iota(shape, len(shape) - 1) % LANES < 64


def two_heads(x):
    low = low_half(x.shape)
    zero = jnp.zeros_like(x)
    return jnp.concatenate([jnp.where(low, x, zero), jnp.where(low, zero, x)], axis=0)


def join_heads(x):
    k = x.shape[0] // 2
    return jnp.where(low_half((k, LANES)), x[:k], x[k:])


def place(rw, ry, x_first):
    rx, rz = rw & 1, rw >> 1
    return ry * 8 + rx * 4 + rz if x_first else rx * 8 + ry * 4 + rz


def begin(copies):
    copies = [pltpu.make_async_copy(*c) for c in copies]
    for copy in copies:
        copy.start()
    return copies


def finish(copies):
    for copy in copies:
        copy.wait()


def pack_kernel(*refs):
    c0, mine, theirs = refs[10:13]
    cq, co, cu, cd, cp, wq, wo, wu, wd, emb = refs[13:23]
    finish(begin([(a, b, refs[23].at[k]) for k, (a, b) in enumerate(zip(refs[:10], refs[13:23]))]))

    def turned(x):
        return x.astype(F32).T

    for layer, (c, base) in enumerate(((c0, 0), (mine, W_ROWS))):
        for t, (row, rows) in zip((turned(cq[layer]), co[layer], turned(cu[layer]), turned(cp[layer])), C_PAIRED):
            t = t.astype(F32)
            c[base + row : base + row + rows, :] = jnp.concatenate([t[:rows], t[rows:]], axis=1).astype(BF)
        for k in range(2):
            row = base + C_DOWN[0] + 32 * k
            c[row : row + 32, :] = cd[layer, :, k * LANES : (k + 1) * LANES]
    e = emb[...].astype(F32)
    theirs[W_ROWS:, :] = mine[W_ROWS:, :]
    c0[C_EMB[0] : C_EMB[0] + 16, :] = jnp.concatenate([e[:, :LANES], e[:, LANES:]], axis=0).astype(BF)
    own = (lax.axis_index("wide") >> 1) & 1
    for layer, w in ((own, mine), (1 - own, theirs)):
        w[W_QKV[0] : W_QKV[0] + 192, :] = wq[layer]
        w[W_OUT[0] : W_OUT[0] + 64, :] = wo[layer]
        w[W_UP[0] : W_UP[0] + 256, :] = turned(wu[layer]).astype(BF)
        for k in range(4):
            row = W_DOWN[0] + 64 * k
            w[row : row + 64, :] = wd[layer, :, k * LANES : (k + 1) * LANES]


def whole(shape, dtype):
    return jax.ShapeDtypeStruct(shape, dtype)


def cost(flops, moved):
    return pl.CostEstimate(flops=int(flops), bytes_accessed=int(moved), transcendentals=0)


smem = pl.BlockSpec(memory_space=pltpu.SMEM)
vmem = pl.BlockSpec(memory_space=pltpu.VMEM)
anywhere = pl.BlockSpec(memory_space=pl.ANY)
TURNED = (1, 3, 5, 6, 8)


def pack(weights, embedding):
    weights = [m.swapaxes(1, 2) if k in TURNED else m for k, m in enumerate(weights)]
    return pl.pallas_call(
        pack_kernel,
        in_specs=[anywhere] * 10,
        out_shape=(
            whole((HELD_0, LANES), BF),
            whole((W_ROWS + C_ROWS, LANES), BF),
            whole((W_ROWS + C_ROWS, LANES), BF),
        ),
        scratch_shapes=[pltpu.VMEM(m.shape, BF) for m in (*weights, embedding)] + [pltpu.SemaphoreType.DMA((10,))],
        compiler_params=pltpu.CompilerParams(vmem_limit_bytes=LARGE),
        cost_estimate=cost(0, 4e6),
    )(*weights, embedding)


def low_vector(x):
    return x.astype(BF)


def whole_vector(x):
    return x.astype(F32)


def unpack_kernel(me, *refs):
    first, (own_word, other_word, own_out, other_out) = refs[:5], refs[5:9]
    cq, co, cu, cd, cp, wq, wo, wu, wd, emb, cg, cs, pq, wg, ws, word_out = refs[9:]
    layer_now = me[2]
    word_out[...] = jnp.where(layer_now == 1, own_out[...], other_out[...])
    both = [first[k][0 : HELD_0 + C_ROWS, :].astype(F32) for k in (0, 2, 3, 4)]
    both = (both[0] + both[1]) + (both[2] + both[3])
    c0, c1 = both[:HELD_0], both[HELD_0:]
    v = [whole_vector(ref[HELD_0 + C_ROWS :, :]) for ref in first[1:5]]
    v = (v[0] + v[1]) + (v[2] + v[3])
    for layer, c in enumerate((c0, c1)):
        for k, ref, (row, rows) in zip((0, 1, 2, 4), (cq, co, cu, cp), C_PAIRED):
            t = c[row : row + rows, :]
            t = jnp.concatenate([t[:, :64], t[:, 64:]], axis=0)
            ref[layer] = t if k in TURNED else t.T
        for k in range(2):
            row = C_DOWN[0] + 32 * k
            cd[layer, :, k * LANES : (k + 1) * LANES] = c[row : row + 32, :]
        for t in range(4):
            row = 8 * t + 4 * layer
            wg[layer, :, t * LANES : (t + 1) * LANES] = v[row : row + 2]
            ws[layer, :, t * LANES : (t + 1) * LANES] = v[row + 2 : row + 4]
        for t in range(2):
            row = 32 + 16 * t + 8 * layer
            cg[layer, :, t * LANES : (t + 1) * LANES] = v[row : row + 2]
            cs[layer, :, t * LANES : (t + 1) * LANES] = v[row + 2 : row + 4]
            pq[layer : layer + 1, t * LANES : (t + 1) * LANES] = v[row + 4 : row + 5]
    e = c0[C_EMB[0] : C_EMB[0] + 16, :]
    emb[...] = jnp.concatenate([e[:8], e[8:]], axis=1)
    for layer, w in ((layer_now, own_word), (1 - layer_now, other_word)):
        wq[layer] = w[0, W_QKV[0] : W_QKV[0] + 192, :].astype(F32)
        wo[layer] = w[0, W_OUT[0] : W_OUT[0] + 64, :].astype(F32)
        wu[layer] = w[0, W_UP[0] : W_UP[0] + 256, :].astype(F32).T
        for k in range(4):
            row = W_DOWN[0] + 64 * k
            wd[layer, :, k * LANES : (k + 1) * LANES] = w[0, row : row + 64, :].astype(F32)


def unpack(me, blocks, weights, embedding, vectors):
    shapes = [m.shape for m in weights]
    shapes = [(a, c, b) if k in TURNED else (a, b, c) for k, (a, b, c) in enumerate(shapes)]
    shapes += [embedding.shape] + [v.shape for v in vectors]
    out = pl.pallas_call(
        unpack_kernel,
        in_specs=[smem] + [vmem] * len(blocks),
        out_shape=tuple(whole(x, F32) for x in shapes) + (whole(blocks[-1].shape, BF),),
        cost_estimate=cost(0, 8e6),
    )(me, *blocks)
    return [x.swapaxes(1, 2) if k in TURNED else x for k, x in enumerate(out)]


def fold_one_kernel(keep_f, got_f, keep_a, got_a, sent_a, ours, *away):
    vector = [ref[16, 0:64, :] for ref in (sent_a, got_a)]
    vector = low_vector(whole_vector(vector[0]) + whole_vector(vector[1]))
    for part, ref in enumerate((ours, *away)):
        for k in range(4):
            at, row = 4 * part + k, k * HELD_0
            ref[row : row + 64, :] = (keep_a[at, 0:64, :].astype(F32) + got_a[at, 0:64, :].astype(F32)).astype(BF)
            ref[row + 64 : row + 224, :] = (keep_f[at].astype(F32) + got_f[at].astype(F32)).astype(BF)
            ref[row + 224 : row + 240, :] = (
                keep_a[at, 64:80, :].astype(F32) + got_a[at, 64:80, :].astype(F32)
            ).astype(BF)
        if part > 0:
            ref[4 * HELD_0 :, :] = vector


def fold_one(*operands):
    return pl.pallas_call(
        fold_one_kernel,
        out_shape=[whole((4 * HELD_0, LANES), BF)] + [whole((4 * HELD_0 + 64, LANES), BF)] * 3,
        compiler_params=pltpu.CompilerParams(vmem_limit_bytes=SMALL),
        cost_estimate=cost(0, 4e6),
    )(*operands)


def fold_two_kernel(ours, sent, over_x, over_y, over_xy, ours_1, x_1, y_1, xy_1, own, *away):
    vector = [whole_vector(ref[4 * HELD_0 :, :]) for ref in (sent, over_x, over_y, over_xy)]
    vector = ((vector[0] + vector[1]) + (vector[2] + vector[3])).astype(BF)
    for k, ref in enumerate((own, *away)):
        row = k * HELD_0
        near = [r[row : row + HELD_0, :].astype(F32) for r in (ours, over_x, over_y, over_xy)]
        ref[0:HELD_0, :] = ((near[0] + near[1]) + (near[2] + near[3])).astype(BF)
        near = [r[k].astype(F32) for r in (ours_1, x_1, y_1, xy_1)]
        ref[HELD_0 : HELD_0 + C_ROWS, :] = ((near[0] + near[1]) + (near[2] + near[3])).astype(BF)
        if k > 0:
            ref[HELD_0 + C_ROWS :, :] = vector


def fold_two(*operands):
    rows = HELD_0 + C_ROWS
    return pl.pallas_call(
        fold_two_kernel,
        out_shape=[whole((rows, LANES), BF)] + [whole((rows + 64, LANES), BF)] * 3,
        compiler_params=pltpu.CompilerParams(vmem_limit_bytes=SMALL),
        cost_estimate=cost(0, 4e6),
    )(*operands)


def fold_cores_kernel(keep, got, *out):
    for part, ref in enumerate(out):
        for k in range(4):
            ref[k] = (keep[4 * part + k].astype(F32) + got[4 * part + k].astype(F32)).astype(BF)


def fold_cores(keep, got):
    return pl.pallas_call(
        fold_cores_kernel,
        out_shape=[whole((4, *keep.shape[1:]), BF)] * 4,
        compiler_params=pltpu.CompilerParams(vmem_limit_bytes=SMALL),
        cost_estimate=cost(0, 4e6),
    )(keep, got)


def assemble(x_first, me, span, raw, mats):
    mw, my, mc = me[0], me[1] >> 1, me[1] & 1
    for w in range(8):
        for y in range(2):
            at = place(w ^ mw, y ^ my, x_first)
            cores = (mc * 16 + at, (1 - mc) * 16 + at)
            for ref, (row, rows) in zip(mats[:4], C_PAIRED):
                if ref is None:
                    continue
                row = row - span
                zero, one = (raw[k, row : row + rows, :] for k in cores)
                first = w * 2 * rows
                columns = slice(y * LANES, (y + 1) * LANES)
                ref[first : first + rows, columns] = jnp.concatenate([zero[:, :64], one[:, :64]], axis=1)
                ref[first + rows : first + 2 * rows, columns] = jnp.concatenate(
                    [zero[:, 64:], one[:, 64:]], axis=1
                )
            if mats[4] is None:
                continue
            for c, k in enumerate(cores):
                for t in range(2):
                    column = (2 * y + c) * 256 + t * LANES
                    row = C_DOWN[0] + 32 * t - span
                    mats[4][w * 32 : w * 32 + 32, column : column + LANES] = raw[k, row : row + 32, :]

def put_char(x_first, me, keep, send, span, mats):
    mw, my, mc = me[0], me[1] >> 1, me[1] & 1

    def put(at, row, rows, zero, one):
        row = row - span
        keep[at, row : row + rows, :] = jnp.where(mc == 0, zero, one)
        send[at, row : row + rows, :] = jnp.where(mc == 0, one, zero)

    for w in range(8):
        for y in range(2):
            at = place(w ^ mw, y ^ my, x_first)
            for ref, (row, rows) in zip(mats[:4], C_PAIRED):
                if ref is None:
                    continue
                columns = slice(y * LANES, (y + 1) * LANES)
                top = ref[w * 2 * rows : w * 2 * rows + rows, columns]
                bottom = ref[w * 2 * rows + rows : w * 2 * rows + 2 * rows, columns]
                put(
                    at,
                    row,
                    rows,
                    jnp.concatenate([top[:, :64], bottom[:, :64]], axis=1),
                    jnp.concatenate([top[:, 64:], bottom[:, 64:]], axis=1),
                )
            if mats[4] is None:
                continue
            for t in range(2):
                zero, one = (
                    mats[4][w * 32 : w * 32 + 32, (2 * y + c) * 256 + t * LANES : (2 * y + c) * 256 + (t + 1) * LANES]
                    for c in range(2)
                )
                put(at, C_DOWN[0] + 32 * t, 32, zero, one)


def char_positions(ids, me, x_first):
    device = ids >> 3
    rw = (device >> 2) ^ me[0]
    rn = (device & 3) ^ me[1]
    return ((rn & 1) * 16 + place(rw, rn >> 1, x_first)) * 16 + (ids & 7)


def valid_keys(lens, first):
    lane = iota((1, LANES), 1)
    length = jnp.zeros((1, LANES), jnp.int32)
    for k in range(8):
        length = jnp.where(lane // SLOTS == k, lens[0, first + k], length)
    return lane % SLOTS < length


def to_column(row):
    square = (LANES, LANES)
    return jnp.sum(jnp.where(iota(square, 0) == iota(square, 1), row, 0.0), axis=-1, keepdims=True)


def char_masks(lens, first):
    same = iota((LANES, LANES), 0) // SLOTS == iota((LANES, LANES), 1) // SLOTS
    valid = valid_keys(lens, first)
    return to_column(jnp.where(valid, 1.0, 0.0)), same & valid, same


def pool_weights(states, query, valid):
    scores = jnp.sum(states * query, axis=-1, keepdims=True)
    scores = jnp.where(valid > 0.5, scores, masked_score).reshape(-1, SLOTS, 1)
    shifted = jnp.exp(scores - jnp.max(scores, axis=1, keepdims=True))
    return shifted / jnp.sum(shifted, axis=1, keepdims=True)


def of_layer(first, gain, shift, query):
    layer = 0 if first else 1
    return gain[layer], shift[layer], query[layer : layer + 1, :]


def part_copies(parts, raw, row, rows, at, sems):
    each = 32 // len(parts)
    return [
        (part.at[:, pl.ds(row, rows)], raw.at[pl.ds(each * k, each), pl.ds(at, rows)], sems.at[k])
        for k, part in enumerate(parts)
    ]


def char_forward_kernel(first, x_first, count, *refs):
    me, lens, source = refs[:3]
    parts, refs = refs[3 : 3 + count], refs[3 + count :]
    gain, shift, query = of_layer(first, *refs[:3])
    qkv_out, mixed_out, after_out, next_out, extra_out, pooled_out, delta_out = refs[3:10]
    mats, refs = refs[10:15], refs[15:]
    hidden_here, raw, table, sems_a, sems_f, sems_e = refs
    m_qkv, m_out, m_up, m_proj, m_down = mats
    rows_all = qkv_out.shape[0]
    near = begin(part_copies(parts, raw, 0, 64, 0, sems_a))
    if first:
        near += begin(part_copies(parts, raw, C_EMB[0], 16, C_EMB[0], sems_e))
    far = begin(part_copies(parts, raw, 64, 160, 64, sems_f))
    finish(near)
    assemble(x_first, me, 0, raw, (m_qkv, m_out, None, None, None))
    if first:
        for k in range(32):
            table[k * 16 : k * 16 + 16, :] = raw[k, C_EMB[0] : C_EMB[0] + 16, :]
    for chunk in range(rows_all // CHUNK):
        span = slice(chunk * CHUNK, (chunk + 1) * CHUNK)
        halves = CHUNK // LANES
        masks = [char_masks(lens, chunk * (CHUNK // SLOTS) + 8 * h) for h in range(halves)]
        if first:
            sides = []
            for h in range(halves):
                ids = source[pl.ds(chunk * halves + h, 1), :]
                column = to_column(char_positions(ids, me, x_first).astype(F32)).astype(jnp.int32)
                lane = iota((LANES, 512), 1)
                left = jnp.where(lane == column, 1.0, 0.0).astype(BF)
                right = jnp.where(lane == column + 8, 1.0, 0.0).astype(BF)
                sides.append(jnp.concatenate([nn(left, table[...]), nn(right, table[...])], axis=1))
            x = jnp.concatenate(sides, axis=0)
            extra_out[span] = x
        else:
            x = source[span]
        hat, _ = norm_parts(x)
        normed = (hat * gain[0:1] + shift[0:1]).astype(BF)
        qkv_out[span] = nt(normed, m_qkv[...]).astype(BF)
        blocks = char_blocks(qkv_out, chunk)
        allowed = stacked([jnp.concatenate([m[1]] * 2, axis=1) for m in masks for _ in range(2)])
        scores = jnp.where(allowed, stacked([nt(q, k) for q, k, _ in blocks]) * 0.125, masked_score)
        attend = [softmax_rows(scores[:, :LANES]).astype(BF), softmax_rows(scores[:, LANES:]).astype(BF)]
        attend = jnp.concatenate(attend, axis=1)
        mixed = [nn(attend[n * LANES : (n + 1) * LANES], v) for n, (_, _, v) in enumerate(blocks)]
        mixed = in_rows(mixed, halves).astype(BF)
        mixed_out[span] = mixed
        after = x + nt(mixed, m_out[...])
        after_out[span] = after
        hat, _ = norm_parts(after)
        normed = (hat * gain[1:2] + shift[1:2]).astype(BF)
        if chunk == 0:
            finish(far)
            assemble(x_first, me, 0, raw, (None, None, m_up, m_proj, m_down))
        hidden_here[span] = nt(normed, m_up[...])
        states = after_out[span] + nt(gelu_value(hidden_here[span]).astype(BF), m_down[...])
        next_out[span] = states
        if not first:
            extra_out[span] = states.astype(BF)
        weights = pool_weights(states, query, jnp.concatenate([m[0] for m in masks], axis=0))
        pooled = jnp.sum(weights * states.reshape(-1, SLOTS, 256), axis=1).astype(BF)
        words = slice(chunk * (CHUNK // SLOTS), (chunk + 1) * (CHUNK // SLOTS))
        pooled_out[words] = pooled
        delta_out[words] = nt(pooled, m_proj[...])


def char_blocks(qkv, chunk):
    blocks = []
    for h in range(CHUNK // LANES):
        for pair in range(2):
            q, k, v = char_heads(qkv, chunk * CHUNK + h * LANES, pair)
            blocks.append((q, two_heads(k), two_heads(v)))
    return blocks


def char_heads(qkv, base, pair):
    return (
        qkv[base : base + LANES, t * 256 + pair * LANES : t * 256 + (pair + 1) * LANES] for t in range(3)
    )


def char_forward(first, x_first, me, lens, source, parts, gain, shift, query):
    words = lens.shape[1]
    rows = words * SLOTS
    big = [(768, BF), (256, BF), (256, F32), (256, F32), (256, F32) if first else (256, BF)]
    held = C_ROWS + (16 if first else 0)
    shapes = [whole((rows, 1024), F32)] if not first else []
    out = pl.pallas_call(
        partial(char_forward_kernel, first, x_first, len(parts)),
        in_specs=[smem, smem, vmem] + [anywhere] * len(parts) + [vmem] * 3,
        out_specs=[vmem] * (12 + len(shapes)),
        out_shape=[whole((rows, c), t) for c, t in big]
        + [whole((words, 256), BF), whole((words, 512), F32)]
        + [whole(s, BF) for s in MATS]
        + shapes,
        scratch_shapes=([pltpu.VMEM((rows, 1024), F32)] if first else [])
        + [pltpu.VMEM((32, held, LANES), BF), pltpu.VMEM((512, LANES) if first else (16, LANES), BF)]
        + [pltpu.SemaphoreType.DMA((8,))] * 3,
        compiler_params=pltpu.CompilerParams(vmem_limit_bytes=VMEM),
        cost_estimate=cost(COST_FORWARD, 12e6),
    )(me, lens, source, *parts, gain, shift, query)
    qkv, mixed, after, states, extra, pooled, delta = out[:7]
    mats, hidden = out[7:12], out[12:]
    if first:
        return (extra, qkv, mixed, after, states, pooled, *hidden), delta, mats
    return (source, qkv, mixed, after, states, pooled, *hidden), delta, mats, extra


MATS = ((768, 256), (256, 256), (1024, 256), (512, 256), (256, 1024))


def pool_back(states, query, valid, grad):
    weights = pool_weights(states, query, valid)
    cube = states.reshape(-1, SLOTS, 256)
    wide = grad.reshape(-1, 1, 256)
    by_weight = jnp.sum(cube * wide, axis=-1, keepdims=True)
    by_score = weights * (by_weight - jnp.sum(weights * by_weight, axis=1, keepdims=True))
    added = weights * wide + by_score * query.reshape(1, 1, 256)
    by_query = jnp.sum((by_score * cube).reshape(states.shape), axis=0, keepdims=True)
    return added.reshape(states.shape), by_query


def accumulate(ref, value, chunk):
    if chunk == 0:
        ref[...] = value
    else:
        ref[...] += value


def char_feed_kernel(first, x_first, at, me, lens, word_own, word_other, *refs):
    pooled_in, grad_in, next_in, after_in, m_up, m_proj, m_down = refs[:7]
    gain, shift, query = of_layer(first, *refs[7:10])
    refs = refs[10:]
    if first:
        word_out, refs = refs[0], refs[1:]
    else:
        hidden_in, refs = refs[0], refs[1:]
    grad_out, keep, send, vectors, t_up, t_proj, t_down, a_up, a_proj, a_down = refs
    rows_all = grad_out.shape[0]
    words_all = rows_all // SLOTS
    word_grad = jnp.where(
        me[2] == (0 if first else 1),
        word_own[at[0] * words_all : (at[0] + 1) * words_all],
        word_other[at[1] * words_all : (at[1] + 1) * words_all],
    )
    if first:
        word_out[...] = word_grad
    vectors[...] = jnp.zeros(vectors.shape, F32)
    low_word = word_grad.astype(BF)
    a_proj[...] = tn(low_word, pooled_in[...])
    grad_pooled = nn(low_word, m_proj[...])
    for chunk in range(rows_all // CHUNK):
        span = slice(chunk * CHUNK, (chunk + 1) * CHUNK)
        words = CHUNK // SLOTS
        valid = [valid_keys(lens, chunk * words + 8 * h) for h in range(CHUNK // LANES)]
        valid = jnp.concatenate([to_column(jnp.where(v, 1.0, 0.0)) for v in valid], axis=0)
        added, by_query = pool_back(next_in[span], query, valid, grad_pooled[chunk * words : (chunk + 1) * words])
        grad = grad_in[span].astype(F32) + added
        vectors[4:5, :] += by_query
        low = grad.astype(BF)
        hat, root = norm_parts(after_in[span])
        normed = (hat * gain[1:2] + shift[1:2]).astype(BF)
        act, slope = gelu_both(nt(normed, m_up[...]) if first else hidden_in[span])
        accumulate(a_down, tn(low, act.astype(BF)), chunk)
        by_hidden = (slope * nn(low, m_down[...])).astype(BF)
        accumulate(a_up, tn(normed, by_hidden), chunk)
        back, by_gain, by_shift = norm_back(nn(by_hidden, m_up[...]), hat, root, gain[1:2])
        grad_out[span] = grad + back
        vectors[1:2, :] += by_gain
        vectors[3:4, :] += by_shift
    t_up[...] = a_up[...].T.astype(BF)
    t_proj[...] = a_proj[...].astype(BF)
    t_down[...] = a_down[...].astype(BF)
    put_char(x_first, me, keep, send, F_SPAN[0], (None, None, t_up, t_proj, t_down))


def char_feed(first, x_first, me, lens, grad, words, at, saved, mats, vectors):
    after, states, pooled, *hidden = saved
    rows = after.shape[0]
    outs = [whole((rows, 256), F32)]
    if first:
        outs = [whole((rows // SLOTS, 512), F32)] + outs
    held = F_SPAN[1]
    return pl.pallas_call(
        partial(char_feed_kernel, first, x_first, at),
        in_specs=[smem, smem] + [vmem] * (12 + len(hidden)),
        out_specs=[vmem] * (len(outs) + 3),
        out_shape=outs + [whole((16, held, LANES), BF)] * 2 + [whole((8, 256), F32)],
        scratch_shapes=[pltpu.VMEM(MATS[k], BF) for k in (2, 3, 4)]
        + [pltpu.VMEM(x, F32) for x in ((256, 1024), (512, 256), (256, 1024))],
        compiler_params=pltpu.CompilerParams(vmem_limit_bytes=VMEM),
        cost_estimate=cost(COST_FEED, 12e6),
    )(me, lens, *words, pooled, grad, states, after, *mats[2:], *vectors, *hidden)


def char_mix_kernel(first, x_first, me, lens, grad_in, mixed_in, qkv_in, x_in, m_qkv, m_out, *refs):
    gain, shift, _ = of_layer(first, *refs[:3])
    vec_feed, refs = refs[3], refs[4:]
    if first:
        ids, word_0, word_1, char_1, keep, send, vectors = refs[:7]
        refs = refs[7:]
    else:
        keep_feed, send_feed, grad_out, keep, send, vectors = refs[:6]
        refs = refs[6:]
    t_qkv, t_out, a_qkv, a_out, a_table = refs
    rows_all = grad_in.shape[0]
    vectors[...] = vec_feed[...]
    for chunk in range(rows_all // CHUNK):
        span = slice(chunk * CHUNK, (chunk + 1) * CHUNK)
        grad = grad_in[span]
        low = grad.astype(BF)
        accumulate(a_out, tn(low, mixed_in[span]), chunk)
        by_mixed = nn(low, m_out[...]).astype(BF)
        blocks = char_blocks(qkv_in, chunk)
        masks = [char_masks(lens, chunk * (CHUNK // SLOTS) + 8 * h) for h in range(CHUNK // LANES)]
        allowed = jnp.concatenate([same & (valid > 0.5) for valid, _, same in masks for _ in range(2)], axis=1)
        grads = [
            by_mixed[h * LANES : (h + 1) * LANES, pair * LANES : (pair + 1) * LANES]
            for h in range(CHUNK // LANES)
            for pair in range(2)
        ]
        spans = [slice(n * LANES, (n + 1) * LANES) for n in range(len(blocks))]
        scores = jnp.concatenate([nt(k, q) for q, k, _ in blocks], axis=1)
        by_attend = jnp.concatenate([nt(v, g) for g, (_, _, v) in zip(grads, blocks)], axis=1)
        attend, by_scores = [], []
        for h in range(2):
            part = jnp.where(allowed, scores[h * LANES : (h + 1) * LANES] * 0.125, masked_score)
            shifted = jnp.exp(part - jnp.max(part, axis=0, keepdims=True))
            part = shifted / jnp.sum(shifted, axis=0, keepdims=True)
            product = part * by_attend[h * LANES : (h + 1) * LANES]
            by_scores.append((product - part * jnp.sum(product, axis=0, keepdims=True)).astype(BF))
            attend.append(part.astype(BF))
        attend, by_scores = stacked(attend), stacked(by_scores)
        by_q = [tn(by_scores[:, n], k) * 0.125 for n, (_, k, _) in zip(spans, blocks)]
        by_k = [join_heads(nn(by_scores[:, n], q)) * 0.125 for n, (q, _, _) in zip(spans, blocks)]
        by_v = [join_heads(nn(attend[:, n], g)) for n, g in zip(spans, grads)]
        by_qkv = jnp.concatenate([in_rows(x, CHUNK // LANES) for x in (by_q, by_k, by_v)], axis=1).astype(BF)
        hat, root = norm_parts(x_in[span])
        normed = (hat * gain[0:1] + shift[0:1]).astype(BF)
        accumulate(a_qkv, tn(normed, by_qkv), chunk)
        back, by_gain, by_shift = norm_back(nn(by_qkv, m_qkv[...]), hat, root, gain[0:1])
        grad = grad + back
        vectors[0:1, :] += by_gain
        vectors[2:3, :] += by_shift
        if first:
            for h in range(CHUNK // LANES):
                at = char_positions(ids[pl.ds(chunk * (CHUNK // LANES) + h, 1), :], me, x_first)
                row = iota((512, LANES), 0)
                part = grad[h * LANES : (h + 1) * LANES]
                high = part.astype(BF)
                rest = (part - high.astype(F32)).astype(BF)
                both = jnp.concatenate([high, rest], axis=0)
                for side in range(2):
                    hot = jnp.where(row == at + 8 * side, 1.0, 0.0).astype(BF)
                    hot = jnp.concatenate([hot, hot], axis=1)
                    accumulate(a_table, nn(hot, both[:, side * LANES : (side + 1) * LANES]), chunk + h + side)
        else:
            grad_out[span] = grad
    t_qkv[...] = a_qkv[...].T.astype(BF)
    t_out[...] = a_out[...].astype(BF)
    put_char(x_first, me, keep, send, A_SPAN[0], (t_qkv, t_out, None, None, None))
    if first:
        row = A_SPAN[1]
        for k in range(16):
            keep[k, row : row + E_ROWS, :] = a_table[k * 16 : k * 16 + 16, :].astype(BF)
            send[k, row : row + E_ROWS, :] = a_table[256 + k * 16 : 272 + k * 16, :].astype(BF)
        word = jnp.concatenate([word_0[0:4], word_1[0:4]], axis=0)
        char = jnp.concatenate([vectors[...], char_1[...]], axis=0)
        tiles = [x[:, t * LANES : (t + 1) * LANES] for x in (word, char) for t in range(x.shape[1] // LANES)]
        vector = low_vector(jnp.concatenate(tiles, axis=0))
        held = send.shape[1]
        send[16, 0:64, :] = vector
        send[16, 64:, :] = jnp.zeros((held - 64, LANES), BF)
    else:
        keep[:, F_SPAN[0] :, :] = keep_feed[...]
        send[:, F_SPAN[0] :, :] = send_feed[...]


def char_mix(first, x_first, me, lens, grad, saved, mats, vectors, others):
    x, qkv, mixed = saved
    rows = x.shape[0]
    if first:
        outs, held, sends = [], A_SPAN[1] + E_ROWS, 17
    else:
        outs, held, sends = [whole((rows, 256), F32)], C_ROWS, 16
    return pl.pallas_call(
        partial(char_mix_kernel, first, x_first),
        in_specs=[smem, smem] + [vmem] * (9 + len(others)),
        out_specs=[vmem] * (len(outs) + 3),
        out_shape=outs
        + [whole((16, held, LANES), BF), whole((sends, held, LANES), BF), whole((8, 256), F32)],
        scratch_shapes=[pltpu.VMEM(MATS[k], BF) for k in (0, 1)]
        + [pltpu.VMEM(x, F32) for x in ((256, 768), (256, 256), (512 if first else 8, LANES))],
        compiler_params=pltpu.CompilerParams(vmem_limit_bytes=VMEM),
        cost_estimate=cost(COST_MIX, 12e6),
    )(me, lens, grad, mixed, qkv, x, *mats[:2], *vectors, *others)


def char_middle_kernel(me, lens, *refs):
    feed_1, refs = refs[:13], refs[13:]
    mix_1, refs = refs[:8], refs[8:]
    feed_0, refs = refs[:11], refs[11:]
    mix_out, feed_out, refs = refs[:3], refs[3:8], refs[8:]
    grad_feed, grad_mix, keep, send, vectors = refs[:5]
    mix_scratch, feed_scratch = refs[5:10], refs[10:]
    char_feed_kernel(
        False, True, (0, 1), me, lens, *feed_1, grad_feed, keep, send, vectors, *feed_scratch
    )
    mixed, qkv, x, m_qkv, m_out, *gains = mix_1
    char_mix_kernel(
        *(False, True, me, lens, grad_feed, mixed, qkv, x, m_qkv, m_out, *gains, vectors, keep, send),
        *(grad_mix, *mix_out, *mix_scratch),
    )
    char_feed_kernel(True, True, (0, 0), me, lens, *feed_0[:3], grad_mix, *feed_0[3:], *feed_out, *feed_scratch)


def char_middle(me, lens, grad, words_1, saved_1, mats_1, words_0, saved_0, mats_0, vectors):
    x, qkv, mixed, after_1, states_1, pooled_1, hidden_1 = saved_1
    after, states, pooled = saved_0
    rows = x.shape[0]
    feed = [whole((16, F_SPAN[1], LANES), BF)] * 2 + [whole((8, 256), F32)]
    return pl.pallas_call(
        char_middle_kernel,
        in_specs=[smem, smem] + [vmem] * 32,
        out_specs=[vmem] * 8,
        out_shape=[whole((16, C_ROWS, LANES), BF)] * 2
        + [whole((8, 256), F32), whole((rows // SLOTS, 512), F32), whole((rows, 256), F32)]
        + feed,
        scratch_shapes=[pltpu.VMEM((rows, 256), F32)] * 2
        + [pltpu.VMEM(x.shape, x.dtype) for x in feed]
        + [pltpu.VMEM(MATS[k], BF) for k in (0, 1)]
        + [pltpu.VMEM(x, F32) for x in ((256, 768), (256, 256), (8, LANES))]
        + [pltpu.VMEM(MATS[k], BF) for k in (2, 3, 4)]
        + [pltpu.VMEM(x, F32) for x in ((256, 1024), (512, 256), (256, 1024))],
        compiler_params=pltpu.CompilerParams(vmem_limit_bytes=VMEM),
        cost_estimate=cost(COST_MIX + 2 * COST_FEED, 36e6),
    )(
        *(me, lens, *words_1, pooled_1, grad, states_1, after_1, *mats_1[2:], *vectors, hidden_1),
        *(mixed, qkv, x, *mats_1[:2], *vectors),
        *(*words_0, pooled, states, after, *mats_0[2:], *vectors),
    )


def fetch_word(me, parts, upper, down, sems):
    for k, part in enumerate(parts):
        rc, far, ry, rx = k >> 3, (k >> 2) & 1, (k >> 1) & 1, k & 1

        def one(s, _, part=part, rc=rc, far=far, ry=ry, rx=rx):
            w, n = ((far * 2 + s) * 2 + rx) ^ me[0], (ry * 2 + rc) ^ me[1]
            block = part.at[s]
            column = pl.ds(pl.multiple_of(n * LANES, LANES), LANES)
            for which, base, (row, rows) in ((0, 0, W_QKV), (1, 1536, W_OUT), (2, 2048, W_UP)):
                to = pl.ds(pl.multiple_of(base + w * rows, 64), rows)
                pltpu.make_async_copy(block.at[pl.ds(row, rows)], upper.at[to, column], sems.at[which]).start()
            for t in range(4):
                column = pl.ds(pl.multiple_of(n * 512 + t * LANES, LANES), LANES)
                to = pl.ds(pl.multiple_of(w * 64, 64), 64)
                pltpu.make_async_copy(
                    block.at[pl.ds(W_DOWN[0] + 64 * t, 64)], down.at[to, column], sems.at[3]
                ).start()
            return 0

        lax.fori_loop(0, 2, one, 0)
    return [
        pltpu.make_async_copy(ref, ref, sems.at[k])
        for k, ref in enumerate((upper.at[pl.ds(0, 1536)], upper.at[pl.ds(1536, 512)], upper.at[pl.ds(2048, 2048)], down))
    ]


def word_allowed(docs, words):
    shape = (words, 2 * words)
    i, j = iota(shape, 0).astype(F32), (iota(shape, 1) % words).astype(F32)
    end = jnp.zeros((1, 1), F32)
    of_i, of_j = jnp.zeros(shape, jnp.int32), jnp.zeros(shape, jnp.int32)
    for k in range(docs.shape[1]):
        end = end + docs[:, k : k + 1]
        of_i = of_i + (i >= end).astype(jnp.int32)
        of_j = of_j + (j >= end).astype(jnp.int32)
    return (of_i == of_j) & (j <= i)


def docs_of(states, documents):
    return [x[2, 0:1, 0:documents].astype(F32) for x in states]


def by_half(x, reduce, fill):
    low = low_half(x.shape)
    left = reduce(jnp.where(low, x, fill), axis=-1, keepdims=True)
    right = reduce(jnp.where(low, fill, x), axis=-1, keepdims=True)
    return jnp.where(low, left, right)


def word_blocks(qkv, allowed):
    rows = qkv.shape[0] // len(allowed)
    blocks = []
    for r in range(len(allowed)):
        for pair in range(4):
            q, k, v = word_heads(qkv, r * rows, rows, pair)
            blocks.append((q, two_heads(k), two_heads(v)))
    return blocks, jnp.concatenate([pairs for pairs in allowed for _ in range(4)], axis=0)


def stacked(parts):
    return jnp.concatenate(parts, axis=0)


def in_rows(parts, count):
    each = len(parts) // count
    return stacked([jnp.concatenate(parts[r * each : (r + 1) * each], axis=1) for r in range(count)])


def word_attend(blocks, allowed):
    scores = jnp.where(allowed, stacked([nt(q, k) for q, k, _ in blocks]) * 0.125, masked_score)
    shifted = jnp.exp(scores - by_half(scores, jnp.max, 2 * masked_score))
    return shifted / by_half(shifted, jnp.sum, 0.0)


def word_forward_body(w1, coming, upper, down, gain, shift, allowed):
    hat, root = norm_parts(w1)
    normed = (hat * gain[0:1] + shift[0:1]).astype(BF)
    await_one(coming, 0)
    qkv = nt(normed, upper[0:1536, :]).astype(BF)
    rows = w1.shape[0] // len(allowed)
    blocks, pairs = word_blocks(qkv, allowed)
    attend = word_attend(blocks, pairs).astype(BF)
    mixed = [nn(attend[n * rows : (n + 1) * rows], v) for n, (_, _, v) in enumerate(blocks)]
    mixed = in_rows(mixed, len(allowed)).astype(BF)
    await_one(coming, 1)
    w2 = w1 + nt(mixed, upper[1536:2048, :])
    hat, root = norm_parts(w2)
    normed = (hat * gain[1:2] + shift[1:2]).astype(BF)
    await_one(coming, 2)
    hidden = nt(normed, upper[2048:4096, :])
    await_one(coming, 3)
    w3 = w2 + nt(gelu_value(hidden).astype(BF), down[...])
    return qkv, mixed, w2, hidden, w3


def word_heads(qkv, row, rows, pair):
    return (qkv[row : row + rows, t * 512 + pair * LANES : t * 512 + (pair + 1) * LANES] for t in range(3))


def await_one(coming, k):
    if coming is not None:
        coming[k].wait()


def word_backward_body(grad, w1, qkv, w2, hidden, upper, down, gain, shift, allowed, vectors):
    low_2 = grad.astype(BF)
    act, slope = gelu_both(hidden)
    by_hidden = (slope * nn(low_2, down[...])).astype(BF)
    hat, root = norm_parts(w2)
    normed_2 = (hat * gain[1:2] + shift[1:2]).astype(BF)
    back, by_gain, by_shift = norm_back(nn(by_hidden, upper[2048:4096, :]), hat, root, gain[1:2])
    grad = grad + back
    vectors[1:2, :] = by_gain
    vectors[3:4, :] = by_shift
    low_1 = grad.astype(BF)
    by_mixed = nn(low_1, upper[1536:2048, :]).astype(BF)
    rows = w1.shape[0] // len(allowed)
    blocks, pairs = word_blocks(qkv, allowed)
    spans = [slice(n * rows, (n + 1) * rows) for n in range(len(blocks))]
    grads = [
        by_mixed[r * rows : (r + 1) * rows, pair * LANES : (pair + 1) * LANES]
        for r in range(len(allowed))
        for pair in range(4)
    ]
    attend = word_attend(blocks, pairs)
    product = attend * stacked([nt(g, v) for g, (_, _, v) in zip(grads, blocks)])
    by_scores = (product - attend * by_half(product, jnp.sum, 0.0)).astype(BF)
    attend = attend.astype(BF)
    by_q = [nn(by_scores[n], k) * 0.125 for n, (_, k, _) in zip(spans, blocks)]
    by_k = [join_heads(tn(by_scores[n], q)) * 0.125 for n, (q, _, _) in zip(spans, blocks)]
    by_v = [join_heads(tn(attend[n], g)) for n, g in zip(spans, grads)]
    by_qkv = jnp.concatenate([in_rows(x, len(allowed)) for x in (by_q, by_k, by_v)], axis=1).astype(BF)
    hat, root = norm_parts(w1)
    normed_1 = (hat * gain[0:1] + shift[0:1]).astype(BF)
    back, by_gain, by_shift = norm_back(nn(by_qkv, upper[0:1536, :]), hat, root, gain[0:1])
    vectors[0:1, :] = by_gain
    vectors[2:3, :] = by_shift
    return grad + back, (normed_1, by_qkv, low_1, normed_2, by_hidden, act.astype(BF), low_2)


FACTORS = (512, 1536, 512, 512, 2048, 2048, 512)


def word_weights_kernel(firsts, me, mixed_0, mixed_1, *refs):
    normed_1, by_qkv, low_1, normed_2, by_hidden, act, low_2, keep_out, send_out, keep, send, sems = refs
    leaving = []

    def leave(row, rows):
        span = pl.ds(row, rows)
        k = len(leaving)
        leaving.extend(
            begin(
                [
                    (a.at[:, span], b.at[:, span], sems.at[k + n])
                    for n, (a, b) in enumerate(((send, send_out), (keep, keep_out)))
                ]
            )
        )

    mw, my, mc = me[0], me[1] >> 1, me[1] & 1
    mixed = jnp.where(me[2] == 0, mixed_0[...], mixed_1[...])

    def put(w, row, rows, blocks):
        for y in range(2):
            at = place(w ^ mw, y ^ my, firsts[row // 384])
            zero, one = blocks(2 * y), blocks(2 * y + 1)
            keep[at, row : row + rows, :] = jnp.where(mc == 0, zero, one)
            send[at, row : row + rows, :] = jnp.where(mc == 0, one, zero)

    for pair in range(4):
        columns = slice(pair * LANES, (pair + 1) * LANES)
        part = tn(low_2[:, columns], act[...]).astype(BF)
        for k in range(2):
            for t in range(4):
                put(
                    2 * pair + k,
                    W_DOWN[0] + 64 * t,
                    64,
                    lambda n: part[k * 64 : k * 64 + 64, n * 512 + t * LANES : n * 512 + (t + 1) * LANES],
                )
    leave(*(W_DOWN[0], 256))
    for w in range(8):
        part = tn(by_hidden[:, w * 256 : (w + 1) * 256], normed_2[...]).astype(BF)
        for k in range(2):
            put(
                w,
                W_UP[0] + 128 * k,
                128,
                lambda n: part[k * 128 : k * 128 + 128, n * LANES : (n + 1) * LANES],
            )
    leave(*W_UP)
    for pair in range(4):
        columns = slice(pair * LANES, (pair + 1) * LANES)
        part = tn(low_1[:, columns], mixed).astype(BF)
        for k in range(2):
            put(
                2 * pair + k,
                W_OUT[0],
                64,
                lambda n: part[k * 64 : k * 64 + 64, n * LANES : (n + 1) * LANES],
            )
    leave(*W_OUT)
    for pair in range(4):
        part = tn(by_qkv[:, pair * 384 : (pair + 1) * 384], normed_1[...]).astype(BF)
        for k in range(2):
            put(
                2 * pair + k,
                W_QKV[0],
                192,
                lambda n: part[k * 192 : (k + 1) * 192, n * LANES : (n + 1) * LANES],
            )
    leave(*W_QKV)
    finish(leaving)


def word_weights(firsts, me, mixed_0, mixed_1, factors):
    return pl.pallas_call(
        partial(word_weights_kernel, firsts),
        in_specs=[smem] + [vmem] * 9,
        out_specs=[anywhere] * 2,
        out_shape=[whole((16, W_ROWS, LANES), BF)] * 2,
        scratch_shapes=[pltpu.VMEM((16, W_ROWS, LANES), BF)] * 2 + [pltpu.SemaphoreType.DMA((8,))],
        compiler_params=pltpu.CompilerParams(vmem_limit_bytes=VMEM),
        cost_estimate=cost(2e9, 9e6),
    )(me, mixed_0, mixed_1, *factors)


def both_deltas(refs):
    own = refs[0][...]
    return stacked([own, nt(refs[1][...], refs[2][...])]) if len(refs) > 1 else own


def swapped(x, count):
    half = x.shape[0] // 2
    return jnp.concatenate([x[half:], x[:half]], axis=0) if count == 2 else x


UPPER, DOWN = (4096, 512), (512, 2048)
word_scratch = [pltpu.SemaphoreType.DMA((4,))]


def word_fetch_kernel(me, *refs):
    *parts, upper, down, sems = refs
    finish(fetch_word(me, parts, upper, down, sems))


def word_fetch(me, parts):
    return pl.pallas_call(
        word_fetch_kernel,
        in_specs=[smem] + [anywhere] * 16,
        out_specs=[vmem] * 2,
        out_shape=[whole(UPPER, BF), whole(DOWN, BF)],
        scratch_shapes=word_scratch,
        compiler_params=pltpu.CompilerParams(vmem_limit_bytes=VMEM),
    )(me, *parts)


def word_call(kernel, count, documents, tables, operands, outs, scratch, flops, alias=None):
    return pl.pallas_call(
        partial(kernel, count, documents),
        in_specs=[smem] * len(tables) + [anywhere if x.shape[1:] == (W_ROWS, LANES) else vmem for x in operands],
        out_specs=[vmem] * len(outs),
        out_shape=[whole(shape, dtype) for shape, dtype in outs],
        scratch_shapes=scratch,
        input_output_aliases=alias or {},
        compiler_params=pltpu.CompilerParams(vmem_limit_bytes=VMEM),
        cost_estimate=cost(flops, 16e6),
    )(*tables, *operands)


def word_first_kernel(count, documents, me, *refs):
    states, refs = refs[:count], refs[count:]
    deltas, parts = refs[: 2 * count - 1], refs[2 * count - 1 :]
    docs = docs_of(states, documents)
    gain, shift, w1_out, qkv_out, mixed_out, w2_out, hidden_out, w3_out, upper, down, sems = parts[16:]
    coming = fetch_word(me, parts[:16], upper, down, sems)

    @pl.when(me[2] == 0)
    def _():
        w1 = stacked([a[0].astype(F32) for a in states]) + both_deltas(deltas)
        w1_out[...] = w1
        allowed = [word_allowed(d, w1.shape[0] // count) for d in docs]
        qkv, mixed, w2, hidden, w3 = word_forward_body(w1, coming, upper, down, gain[0], shift[0], allowed)
        qkv_out[...] = qkv
        mixed_out[...] = mixed
        w2_out[...] = w2
        hidden_out[...] = hidden
        w3_out[...] = w3

    @pl.when(me[2] != 0)
    def _():
        finish(coming)
        w3_out[...] = jnp.zeros(w3_out.shape, F32)


def word_first(me, documents, states, deltas, parts, gain, shift):
    count = len(states)
    words = count * deltas[0].shape[0]
    shapes = [(512, F32), (1536, BF), (512, BF), (512, F32), (2048, F32), (512, F32)]
    return word_call(
        word_first_kernel,
        count,
        documents,
        [me],
        [*states, *deltas, *parts, gain, shift],
        [((words, c), t) for c, t in shapes] + [(UPPER, BF), (DOWN, BF)],
        word_scratch,
        1e9,
    )


def word_last_kernel(count, documents, me, *refs):
    w_in, deltas, refs = refs[0], refs[1 : 2 * count], refs[2 * count :]
    cots, parts = refs[:count], refs[count:]
    docs = docs_of(cots, documents)
    upper, down, gain, shift, out_own, out_other, grad_out, vectors, mixed_out = parts[:9]
    factors = parts[9:]
    vectors[...] = jnp.zeros(vectors.shape, F32)

    @pl.when(me[2] == 1)
    def _():
        w1 = swapped(w_in[...], count) + both_deltas(deltas)
        rows = w1.shape[0] // count
        allowed = [word_allowed(d, rows) for d in docs]
        gains, shifts = gain[1], shift[1]
        qkv, mixed, w2, hidden, w3 = word_forward_body(w1, None, upper, down, gains, shifts, allowed)
        out_own[...] = w3[:rows].astype(BF)
        out_other[...] = w3[(count - 1) * rows :].astype(BF)
        grad = jnp.concatenate([c[1].astype(F32) for c in cots], axis=0)
        mixed_out[...] = mixed
        grad, made = word_backward_body(grad, w1, qkv, w2, hidden, upper, down, gains, shifts, allowed, vectors)
        grad_out[...] = grad
        for ref, value in zip(factors, made):
            ref[...] = value

    @pl.when(me[2] != 1)
    def _():
        for ref in (out_own, out_other, grad_out):
            ref[...] = jnp.zeros(ref.shape, ref.dtype)


def word_last(me, documents, w_in, deltas, cots, mats, gain, shift):
    count = len(cots)
    words = w_in.shape[0]
    row = words // count
    return word_call(
        word_last_kernel,
        count,
        documents,
        [me],
        [w_in, *deltas, *cots, *mats, gain, shift],
        [((row, 512), BF)] * 2
        + [((words, 512), F32), ((8, 512), F32), ((words, 512), BF)]
        + [((words, c), BF) for c in FACTORS],
        [],
        2e9,
    )


def word_back_kernel(count, documents, me, *refs):
    states, (grad_in, w1, qkv, w2, hidden), parts = refs[:count], refs[count : count + 5], refs[count + 5 :]
    docs = docs_of(states, documents)
    upper, down, gain, shift = parts[:4]
    held, parts_out = parts[4:11], parts[11:]
    grad_own, grad_other, vectors = parts_out[:3]
    factors = parts_out[3:]
    vectors[...] = jnp.zeros(vectors.shape, F32)

    @pl.when(me[2] == 0)
    def _():
        rows = w1.shape[0] // count
        grad, made = word_backward_body(
            swapped(grad_in[...], count),
            w1[...],
            qkv[...],
            w2[...],
            hidden[...],
            upper,
            down,
            gain[0],
            shift[0],
            [word_allowed(d, rows) for d in docs],
            vectors,
        )
        grad_own[...] = grad[:rows]
        grad_other[...] = grad[(count - 1) * rows :]
        for ref, value in zip(factors, made):
            ref[...] = value

    @pl.when(me[2] != 0)
    def _():
        for ref in (grad_own, grad_other):
            ref[...] = jnp.zeros(ref.shape, F32)
        for ref, value in zip(factors, held):
            ref[...] = value[...]


def word_back(me, documents, states, grad, saved, mats, gain, shift, held):
    count = len(states)
    words = grad.shape[0]
    return word_call(
        word_back_kernel,
        count,
        documents,
        [me],
        [*states, grad, *saved, *mats, gain, shift, *held],
        [((words // count, 512), F32)] * 2 + [((8, 512), F32)] + [((words, c), BF) for c in FACTORS],
        [],
        2e9,
    )


def swap(x, axis, flip):
    return lax.ppermute(x, axis, [(k, k ^ flip) for k in range(lax.axis_size(axis))])


def over_x(x):
    return swap(x, "wide", 1)


def over_y(x):
    return swap(x, "narrow", 2)


def over_core(x):
    return swap(x, "narrow", 1)


def over_pair(x):
    return swap(x, "wide", 2)


def after(x, *others):
    return lax.optimization_barrier((x, *others))[0]


def add(*terms):
    total = terms[0].astype(F32)
    for term in terms[1:]:
        total = total + term.astype(F32)
    return total.astype(BF)


def gather_z(block):
    return jnp.stack([block] + [swap(block, "wide", 2 * k) for k in (1, 2, 3)])


def gather_core(parts):
    return (*parts, *[over_core(part) for part in parts])


def two(x, x_first):
    return (over_y if x_first else over_x)(x)


def one(x, x_first):
    return (over_x if x_first else over_y)(x)


def cut(matrices, table):
    qkv, out, up, down, proj, *words = matrices

    def split(m):
        r, c = m.shape
        return m.T.reshape(8, c // 8, 4, r // 4).transpose(0, 2, 1, 3)

    def paired(m):
        b = split(m)
        c = b.shape[2]
        return b.reshape(8, 4, 2, c // 2, 64).transpose(0, 1, 3, 2, 4).reshape(8, 4, c // 2, LANES)

    def tiled(m):
        b = split(m)
        c, r = b.shape[2:]
        return b.reshape(8, 4, c, r // LANES, LANES).transpose(0, 1, 3, 2, 4).reshape(8, 4, -1, LANES)

    char = [paired(qkv), paired(out), paired(up), paired(proj), tiled(down)]
    if table is not None:
        char.append(table.reshape(8, 4, 8, 2, LANES).transpose(0, 1, 3, 2, 4).reshape(8, 4, 16, LANES))
    word = [tiled(m) for m in words]
    return [ordered(jnp.concatenate(x, axis=2)) for x in (char, word)]


def ordered(blocks):
    b = blocks.reshape(4, 2, 2, 2, *blocks.shape[2:]).transpose(3, 2, 1, 0, 4, 5)
    return b.reshape(32, *blocks.shape[2:])


def uncut(blocks, is_char, with_table):
    b = blocks.reshape(2, 2, 2, 4, *blocks.shape[1:]).transpose(3, 2, 1, 0, 4, 5)
    b = b.reshape(8, 4, *blocks.shape[1:])

    def joined(x):
        c, r = x.shape[2:]
        return x.transpose(0, 2, 1, 3).reshape(8 * c, 4 * r).T

    def paired(x):
        c = x.shape[2]
        return joined(x.reshape(8, 4, c, 2, 64).transpose(0, 1, 3, 2, 4).reshape(8, 4, 2 * c, 64))

    def tiled(x, tiles):
        c = x.shape[2] // tiles
        return joined(x.reshape(8, 4, tiles, c, LANES).transpose(0, 1, 3, 2, 4).reshape(8, 4, c, tiles * LANES))

    def rows(span, count=None):
        return b[:, :, span[0] : span[0] + (count or span[1])]

    if not is_char:
        return [tiled(rows(W_QKV), 1), tiled(rows(W_OUT), 1), tiled(rows(W_UP), 1), tiled(rows(W_DOWN, 256), 4)], None
    table = None
    if with_table:
        table = rows(C_EMB).reshape(32, 2, 8, LANES).transpose(0, 2, 1, 3).reshape(256, 256)
    qkv, out, up, proj = (paired(rows(span)) for span in C_PAIRED)
    return [qkv, out, up, tiled(rows(C_DOWN, 64), 2), proj], table


def over_xy(x):
    flip = lax.axis_size("narrow") + 2
    return lax.ppermute(x, ("wide", "narrow"), [(k, k ^ flip) for k in range(lax.axis_size(("wide", "narrow")))])


together = lax.optimization_barrier


def whole_chip(z):
    return [z, over_x(z), over_y(z), over_xy(z)]


def three(word_states, word_cot, doc_lengths):
    words, width = word_states.shape[1:]
    docs = jnp.pad(doc_lengths.astype(BF), ((0, words - 1), (0, width - doc_lengths.shape[1])))
    return jnp.stack([word_states[0], word_cot[0], docs])


def direct_program(
    word_states, character_ids, word_lengths, doc_lengths, embedding, weights, vectors, char_cot, word_cot
):
    char_gains, char_shifts, pool_query, word_gains, word_shifts = vectors
    vectors_char = (char_gains, char_shifts, pool_query)
    vectors_word = (word_gains, word_shifts)
    width = char_cot.shape[3]
    wide = lax.axis_index("wide")
    me = jnp.stack([wide, lax.axis_index("narrow"), (wide >> 1) & 1]).astype(jnp.int32)
    firsts = (True, False)
    f0, f1 = firsts
    c0, mine, theirs = pack(weights, embedding)
    pair = three(word_states, word_cot, doc_lengths)
    ids = character_ids.reshape(-1, LANES)
    got = over_pair(theirs)
    z0 = gather_z(c0)
    word = jnp.stack([mine, got])
    z0, word, ids, pair = together((z0, word, ids, pair))
    near_0 = whole_chip(z0)
    far = swap(word, "wide", 4)
    word_near = whole_chip(word[:, :W_ROWS])
    other_pair = over_pair(pair)
    near_0, far, word_near, other_pair = together((near_0, far, word_near, other_pair))
    char_0 = gather_core(near_0)
    far_near = whole_chip(far[:, :W_ROWS])
    char_0, word_near = together((char_0, word_near))
    saved_0, delta_0, mats_0 = char_forward(True, True, me, word_lengths, ids, char_0, *vectors_char)
    delta_0, far_near, word, far, word_near, pooled = together((delta_0, far_near, word, far, word_near, saved_0[5]))
    other_delta_0 = over_pair(pooled)
    word_cores = [over_core(part) for part in word_near]
    far_cores = [over_core(part) for part in far_near]
    z1 = jnp.concatenate([word[:, W_ROWS:], far[:, W_ROWS:]], axis=0)
    word_cores, far_cores, other_delta_0, z1 = together((word_cores, far_cores, other_delta_0, z1))
    near_1 = whole_chip(z1)
    word_parts = [*word_near, *far_near, *word_cores, *far_cores]
    docs = doc_lengths.shape[1]
    pairs = [pair, other_pair]
    *word_saved, w3, upper, down = word_first(me, docs, pairs, [delta_0, other_delta_0, mats_0[3]], word_parts, *vectors_word)
    near_1, w3 = together((near_1, w3))
    char_1 = gather_core(near_1)
    char_1, states = together((char_1, saved_0[4]))
    saved_1, delta_1, mats_1, char_out = char_forward(False, True, me, word_lengths, states, char_1, *vectors_char)
    other_w3 = over_pair(w3)
    other_delta_1 = over_pair(saved_1[5])
    out_own, out_other, grad_1, word_vec_1, mixed_1, *held = word_last(
        me, docs, other_w3, [delta_1, other_delta_1, mats_1[3]], pairs, (upper, down), *vectors_word
    )
    w1, qkv, mixed_0, w2, hidden = word_saved
    got_1 = over_pair(grad_1)
    grad_own, grad_other, word_vec_0, *factors = word_back(
        me, docs, pairs, got_1, (w1, qkv, w2, hidden), (upper, down), *vectors_word, held
    )
    keep, send = word_weights(firsts, me, mixed_0, mixed_1, factors)
    got = over_core(send)
    got_0 = over_pair(grad_other)
    out_other = over_pair(out_other)
    cot = char_cot[0].reshape(-1, width)
    got, keep, got_0 = together((got, keep, got_0))
    pieces = []
    for h in range(2):
        span = slice(384 * h, 384 * h + 384)
        pieces += [add(keep[k : k + 8, span], got[k : k + 8, span]) for k in (0, 8)]
    pieces, cot = together((pieces, cot))
    pieces[1], pieces[3] = two(pieces[1], f0), two(pieces[3], f1)
    keep_1, send_1, char_vec_1, word_grad, grad, keep_f0, send_f0, vec_0 = char_middle(
        me, word_lengths, cot, (grad_1, got_1), saved_1, mats_1, (grad_own, got_0), saved_0[3:], mats_0, vectors_char
    )
    pieces, grad, send_1, send_f0 = together((pieces, grad, send_1, send_f0))
    pieces = [add(a[k : k + 4], b[k : k + 4]) for a, b in (pieces[:2], pieces[2:]) for k in (0, 4)]
    pieces, send_1, send_f0 = together((pieces, send_1, send_f0))
    got_1 = over_core(send_1)
    got_f0 = over_core(send_f0)
    pieces[1], pieces[3] = one(pieces[1], f0), one(pieces[3], f1)
    grad, got_1, got_f0, keep_1 = together((grad, got_1, got_f0, keep_1))
    own_1, *away_1 = fold_cores(keep_1, got_1)
    own_1, away_1, grad = together((own_1, away_1, grad))
    away_1 = [over_x(away_1[0]), over_y(away_1[1]), over_xy(away_1[2])]
    keep_0, send_0, _ = char_mix(
        True,
        True,
        me,
        word_lengths,
        grad,
        saved_0[:3],
        mats_0,
        vectors_char,
        (vec_0, ids, word_vec_0, word_vec_1, char_vec_1),
    )
    pieces, send_0 = together((pieces, send_0))
    got_0 = over_core(send_0)
    ours, away = (
        jnp.concatenate([add(a[k : k + 2], b[k : k + 2]) for a, b in (pieces[:2], pieces[2:])], axis=1) for k in (0, 2)
    )
    got_0, away = together((got_0, away))
    away = swap(away, "wide", 4)
    own_0, *away_0 = fold_one(keep_f0, got_f0, keep_0, got_0, send_0)
    away_0, away_1 = together((away_0, away_1))
    sent = away_0[0]
    moved = (over_x(away_0[0]), over_y(away_0[1]), over_xy(away_0[2]))
    own_0, *away_0 = fold_two(own_0, sent, *moved, own_1, *away_1)
    away_0, away = together((away_0, away))
    ours, away = (add(ours[k : k + 1], away[k : k + 1]) for k in (0, 1))
    away = over_pair(away)
    first = [own_0, away_0[0]] + [swap(away_0[k - 1], "wide", 2 * k) for k in (1, 2, 3)]
    out = unpack(me, [*first, ours, away, out_own, out_other], weights, embedding, vectors)
    return (char_out, out[-1], word_grad, out[9], *out[:9], *out[10:15])


def plain_program(
    word_states, character_ids, word_lengths, doc_lengths, embedding, weights, vectors, char_cot, word_cot
):
    char_gains, char_shifts, pool_query, word_gains, word_shifts = vectors
    width = char_cot.shape[3]
    both = ("wide", "narrow")
    firsts = (True, True)
    at = [jnp.array([0, 0, layer], jnp.int32) for layer in range(2)]
    table = lax.all_gather(embedding, both, axis=0, tiled=True)
    full = [lax.all_gather(lax.all_gather(m, "narrow", axis=1, tiled=True), "wide", axis=2, tiled=True) for m in weights]
    chars, words = [], []
    for layer in range(2):
        char, word = cut([m[layer] for m in full], table if layer == 0 else None)
        chars.append([char[8 * k : 8 * k + 8] for k in range(4)])
        words.append([word[k : k + 2] for c in (0, 16) for z in (0, 2) for k in range(c + z, c + z + 16, 4)])
    ids = character_ids.reshape(-1, LANES)
    vectors_char = (char_gains, char_shifts, pool_query)
    vectors_word = (word_gains, word_shifts)
    saved_0, delta_0, mats_0 = char_forward(True, True, at[0], word_lengths, ids, chars[0], *vectors_char)
    states = saved_0[4]
    saved_1, delta_1, mats_1, char_out = char_forward(False, True, at[0], word_lengths, states, chars[1], *vectors_char)
    docs = doc_lengths.shape[1]
    pair = [three(word_states, word_cot, doc_lengths)]
    *word_saved, w3, upper, down = word_first(at[0], docs, pair, [delta_0], words[0], *vectors_word)
    word_out, _, grad_1, word_vec_1, mixed_1, *held = word_last(
        at[1], docs, w3, [delta_1], pair, word_fetch(at[1], words[1]), *vectors_word
    )
    word_mats = (upper, down)
    w1, qkv, mixed_0, w2, hidden = word_saved
    grad_0, _, word_vec_0, *factors = word_back(
        at[0], docs, pair, grad_1, (w1, qkv, w2, hidden), word_mats, *vectors_word, held
    )
    words = [word_weights(firsts, at[0], mixed, mixed, made) for mixed, made in ((mixed_0, factors), (mixed_1, held))]
    cot = char_cot[0].reshape(-1, width)
    grad, keep_f, send_f, vec_1 = char_feed(
        False, True, at[1], word_lengths, cot, (grad_1, grad_1), (0, 0), saved_1[3:], mats_1, vectors_char
    )
    grad, keep_1, send_1, char_vec_1 = char_mix(
        False, True, at[1], word_lengths, grad, saved_1[:3], mats_1, vectors_char, (vec_1, keep_f, send_f)
    )
    word_grad, grad, keep_f, send_f, vec_0 = char_feed(
        True, True, at[0], word_lengths, grad, (grad_0, grad_0), (0, 0), saved_0[3:], mats_0, vectors_char
    )
    keep_0, send_0, _ = char_mix(
        True,
        True,
        at[0],
        word_lengths,
        grad,
        saved_0[:3],
        mats_0,
        vectors_char,
        (vec_0, ids, word_vec_0, word_vec_1, char_vec_1),
    )
    summed = lax.psum(whole_vector(send_0[16, :64]), both)
    keep_0, send_0 = (
        jnp.concatenate([a[:16, :64], f, a[:16, 64:]], axis=1) for a, f in ((keep_0, keep_f), (send_0, send_f))
    )
    blocks = ((keep_0, send_0), (keep_1, send_1), *words)
    full = [uncut(jnp.concatenate(g), k < 2, k == 0) for k, g in enumerate(blocks)]
    matrix_grads = [
        lax.psum_scatter(
            lax.psum_scatter(jnp.stack([a, b]), "wide", scatter_dimension=2, tiled=True),
            "narrow",
            scatter_dimension=1,
            tiled=True,
        ).astype(F32)
        for a, b in zip(full[0][0] + full[2][0], full[1][0] + full[3][0])
    ]
    embedding_grad = lax.psum_scatter(full[0][1].astype(F32), both, scatter_dimension=0, tiled=True)
    word_vectors = summed[:32].reshape(4, 2, 4, LANES).transpose(1, 2, 0, 3).reshape(2, 4, 512)
    char_vectors = summed[32:].reshape(2, 2, 8, LANES).transpose(1, 2, 0, 3).reshape(2, 8, 256)
    return (
        char_out,
        word_out,
        word_grad,
        embedding_grad,
        *matrix_grads,
        char_vectors[:, 0:2],
        char_vectors[:, 2:4],
        char_vectors[:, 4],
        word_vectors[:, 0:2],
        word_vectors[:, 2:4],
    )


def on_device(direct, *arguments):
    char_cot, word_cot = arguments[19:]
    program = direct_program if direct else plain_program
    char_out, word_out, word_grad, *rest = program(
        *arguments[:5], arguments[5:14], arguments[14:19], char_cot, word_cot
    )
    return (char_out.reshape(char_cot.shape), word_out[None], word_grad[None], *rest)


def solution(mesh):
    rows = ("wide", "narrow")
    matrix = P(None, "narrow", "wide")
    by_rows = P(rows)
    return jax.shard_map(
        partial(on_device, mesh.shape["wide"] == 8 and mesh.shape["narrow"] == 4),
        mesh=mesh,
        in_specs=(by_rows,) * 5 + (matrix,) * 9 + (P(),) * 5 + (by_rows,) * 2,
        out_specs=(by_rows,) * 4 + (matrix,) * 9 + (P(),) * 5,
        check_vma=False,
    )
```
